32 devices in a mesh: dp: 8 (over z, y), tensor: 4 (over x, core).
Axes of the slice: x: 2, y: 2, z: 4, core: 2. Of those that a mesh axis runs over, the one named last changes fastest.
Arguments:
- source_rows: bfloat16 [8, 1024, 1024], P(None, 'dp', 'tensor'), may hold values from -6 to 6
- cotangent: bfloat16 [8, 1024, 1024], P('dp', None, 'tensor'), may hold values from -6 to 6
- lengths: int32 [8], replicated, may hold values from 256 to 1024, as said below
- dealing: int32 [8], replicated, may hold values from 0 to 7, each once
- norm_gain: float32 [1024], replicated, may hold values from 0.5 to 1.5
- query_weight: bfloat16 [1024, 1024], P(None, 'tensor'), may hold values from -0.1875 to 0.1875
- key_weight: bfloat16 [1024, 1024], P(None, 'tensor'), may hold values from -0.1875 to 0.1875
- value_weight: bfloat16 [1024, 2048], P(None, 'tensor'), may hold values from -0.1875 to 0.1875
- query_conv: float32 [4, 1024], P(None, 'tensor'), may hold values from -3 to 3
- key_conv: float32 [4, 1024], P(None, 'tensor'), may hold values from -3 to 3
- value_conv: float32 [4, 2048], P(None, 'tensor'), may hold values from -3 to 3
- beta_weight: bfloat16 [1024, 8], P(None, 'tensor'), may hold values from -0.1875 to 0.1875
- decay_weight: bfloat16 [1024, 8], P(None, 'tensor'), may hold values from -0.375 to 0.375
- decay_log: float32 [8], P('tensor'), may hold values from -7 to -2
- decay_bias: float32 [8], P('tensor'), may hold values from -1 to 1
- gate_weight: bfloat16 [1024, 2048], P(None, 'tensor'), may hold values from -0.1875 to 0.1875
- head_gain: float32 [256], replicated, may hold values from 0.5 to 1.5
- out_weight: bfloat16 [1024, 2048], P(None, 'tensor'), may hold values from -0.25 to 0.25
- ffn_gain: float32 [1024], replicated, may hold values from 0.5 to 1.5
- ffn_gate: bfloat16 [1024, 2816], P(None, 'tensor'), may hold values from -0.1875 to 0.1875
- ffn_up: bfloat16 [1024, 2816], P(None, 'tensor'), may hold values from -0.1875 to 0.1875
- ffn_down: bfloat16 [1024, 2816], P(None, 'tensor'), may hold values from -0.21875 to 0.21875
Outputs:
- mixed: bfloat16 [8, 1024, 1024], P('dp', None, 'tensor')
- source_grad: bfloat16 [8, 1024, 1024], P(None, 'dp', 'tensor')
- norm_gain_grad: float32 [1024], P('dp')
- query_weight_grad: float32 [1024, 1024], P('dp', 'tensor')
- key_weight_grad: float32 [1024, 1024], P('dp', 'tensor')
- value_weight_grad: float32 [1024, 2048], P('dp', 'tensor')
- query_conv_grad: float32 [4, 1024], P(None, 'tensor')
- key_conv_grad: float32 [4, 1024], P(None, 'tensor')
- value_conv_grad: float32 [4, 2048], P(None, 'tensor')
- beta_weight_grad: float32 [1024, 8], P('dp', 'tensor')
- decay_weight_grad: float32 [1024, 8], P('dp', 'tensor')
- decay_log_grad: float32 [8], P('tensor')
- decay_bias_grad: float32 [8], P('tensor')
- gate_weight_grad: float32 [1024, 2048], P('dp', 'tensor')
- head_gain_grad: float32 [256], replicated
- out_weight_grad: float32 [1024, 2048], P('dp', 'tensor')
- ffn_gain_grad: float32 [1024], P('dp')
- ffn_gate_grad: float32 [1024, 2816], P('dp', 'tensor')
- ffn_up_grad: float32 [1024, 2816], P('dp', 'tensor')
- ffn_down_grad: float32 [1024, 2816], P('dp', 'tensor')
The draws below stay inside these ranges and needn't reach their ends.
Inputs may be any that keep to these rules, and one draw needn't show every extreme that they name: `lengths`: positions 0 to length - 1 of a sequence's slot are its tokens, the rest padding; in every draw some sequence has exactly 1024 tokens. `dealing`: a permutation of the sequences.
All inputs are finite; a program needn't handle non-finite values.
Results may differ from the reference program's by a relative error of at most 0.015.
Values may be sent and summed in bfloat16 or wider, within the bound.
No kernel may reach another device: no remote copies, remote signals or barrier semaphores. Data moves between devices by JAX's collectives and lax.ppermute only.
A program may use at most 256 MiB of HBM per device.

```python
import math
import jax
import jax.numpy as jnp
from jax import lax

D = 1024
H = 8
DV = 256
FF = 2816
CONV = 4
STRETCH = 64
SLOT = 1024
MINLEN = 256
SEQS = 8
KD = 1024
VD = 2048


def draw_lengths(key, part):
    key = jax.random.fold_in(key, 11)
    first_key, second_key = jax.random.split(key)
    drawn = jax.random.randint(first_key, (SEQS,), MINLEN, SLOT + 1)
    longest = jax.random.randint(second_key, (), 0, SEQS)
    return jnp.where(jnp.arange(SEQS) == longest, SLOT, drawn).astype(jnp.int32)


def spiked(entries, key, source, target, parts, factor):
    owner, partner = [(jnp.arange(entries.shape[dim]) // (entries.shape[dim] // parts)).reshape([-1 if axis == dim else 1 for axis in range(entries.ndim)]) for dim in (source, target)]
    chosen = jax.random.permutation(key, parts)[partner]
    strong = (owner == chosen) | (owner == (partner + parts // 2) % parts)
    return jnp.where(strong, factor * entries, entries)


def block_levels(stream_key, shape, shards, low, top_value):
    level, own = 1.0, jax.random.fold_in(stream_key, 6)
    for position, shards_of in shards:
        draws = jnp.exp(jax.random.uniform(jax.random.fold_in(own, position), (shards_of,), jnp.float32, low / len(shards), top_value / len(shards)))
        level = level * jnp.repeat(draws, shape[position] // shards_of).reshape([-1 if axis == position else 1 for axis in range(len(shape))])
    return level


def bell_draw(key, extent, width, most, shards=(), kind=jnp.bfloat16):
    array = jax.random.normal(key, extent, jnp.float32) * width
    if len(shards) > 0:
        array = block_levels(key, extent, shards, -0.22, 0.18) * array
    return jnp.clip(array, min=-most, max=most).astype(kind)


def heavy_noise(stream_key, shape, spread, reach, pieces, heavy, dtype=jnp.bfloat16):
    values = spread * jax.random.normal(stream_key, shape, jnp.float32)
    if pieces:
        values = values * block_levels(stream_key, shape, pieces, -0.22, 0.18)
    return jnp.clip(spiked(values, jax.random.fold_in(stream_key, 3), *heavy), -reach, reach).astype(dtype)


def setup_inputs(seed: int = 0) -> dict:
    key_list = jax.random.split(jax.random.key(seed), 23)
    source_rows = bell_draw(key_list[0], (SEQS, SLOT, D), 1.0, 6.0, ((1, 8), (2, 4)))
    cotangent = heavy_noise(key_list[1], (SEQS, SLOT, D), 1.0, 6.0, ((0, 8), (2, 4)), (0, 2, 8, 2.0))
    lengths = draw_lengths(jax.random.fold_in(key_list[22], 71), 0)
    dealing = jax.random.permutation(key_list[3], SEQS).astype(jnp.int32)
    norm_gain = jnp.clip(1.0 + 0.1 * jax.random.normal(key_list[4], (D,), jnp.float32), 0.5, 1.5)
    query_weight = bell_draw(key_list[5], (D, KD), D ** -0.5, 0.1875, ((1, 4),))
    key_weight = bell_draw(key_list[6], (D, KD), D ** -0.5, 0.1875, ((1, 4),))
    value_weight = bell_draw(key_list[7], (D, VD), D ** -0.5, 0.1875, ((1, 4),))
    query_conv = bell_draw(key_list[8], (CONV, KD), CONV ** -0.5, 3.0, ((1, 4),), jnp.float32)
    key_conv = bell_draw(key_list[9], (CONV, KD), CONV ** -0.5, 3.0, ((1, 4),), jnp.float32)
    value_conv = bell_draw(key_list[10], (CONV, VD), CONV ** -0.5, 3.0, ((1, 4),), jnp.float32)
    beta_weight = bell_draw(key_list[11], (D, H), D ** -0.5, 0.1875, ((1, 4),))
    decay_weight = bell_draw(key_list[12], (D, H), (D // 4) ** -0.5, 0.375, ((1, 4),))
    decay_log = jnp.clip(-7.0 + 5.0 * jax.random.uniform(key_list[13], (H,), jnp.float32) ** block_levels(key_list[13], (H,), ((0, 4),), -0.2, 0.2), -7.0, -2.0)
    decay_bias = jnp.clip(jax.random.uniform(key_list[14], (H,), jnp.float32, -1.0, 1.0) * block_levels(key_list[14], (H,), ((0, 4),), -0.4, 0.0), -1.0, 1.0)
    gate_weight = bell_draw(key_list[15], (D, VD), D ** -0.5, 0.1875, ((1, 4),))
    head_gain = jnp.clip(1.0 + 0.1 * jax.random.normal(key_list[16], (DV,), jnp.float32), 0.5, 1.5)
    out_weight = bell_draw(key_list[17], (D, VD), (VD // 4) ** -0.5, 0.25, ((1, 4),))
    ffn_gain = jnp.clip(1.0 + 0.1 * jax.random.normal(key_list[18], (D,), jnp.float32), 0.5, 1.5)
    ffn_gate = bell_draw(key_list[19], (D, FF), D ** -0.5, 0.1875, ((1, 4),))
    ffn_up = bell_draw(key_list[20], (D, FF), D ** -0.5, 0.1875, ((1, 4),))
    ffn_down = bell_draw(key_list[21], (D, FF), (FF // 4) ** -0.5, 0.21875, ((1, 4),))
    return {"source_rows": source_rows, "cotangent": cotangent, "lengths": lengths, "dealing": dealing, "norm_gain": norm_gain, "query_weight": query_weight, "key_weight": key_weight, "value_weight": value_weight, "query_conv": query_conv, "key_conv": key_conv, "value_conv": value_conv, "beta_weight": beta_weight, "decay_weight": decay_weight, "decay_log": decay_log, "decay_bias": decay_bias, "gate_weight": gate_weight, "head_gain": head_gain, "out_weight": out_weight, "ffn_gain": ffn_gain, "ffn_gate": ffn_gate, "ffn_up": ffn_up, "ffn_down": ffn_down}


@jax.custom_vjp
def low(v):
    return lax.optimization_barrier(v.astype(jnp.bfloat16)).astype(jnp.float32)

@jax.custom_vjp
def low_back(v):
    return v

def low_keep(v):
    return (low(v), None)

def low_pass(kept, grad):
    return (grad,)

def back_keep(v):
    return (v, None)

def back_low(kept, grad):
    return (low(grad),)
low.defvjp(low_keep, low_pass)
low_back.defvjp(back_keep, back_low)

def matmul(left, right):
    return jnp.dot(left, right, preferred_element_type=jnp.float32, precision=lax.Precision.HIGHEST)

def causal_mix(signal, weights):
    taps = weights.shape[0]
    length = signal.shape[1]
    padded = jnp.pad(signal, ((0, 0), (taps - 1, 0), (0, 0)))
    summed = jnp.zeros_like(signal)
    for offset in range(taps):
        summed = summed + weights[offset] * padded[:, offset:offset + length]
    return summed

def recurrence(queries, key_heads, values, strength, decay_rate, span_size):
    groups, length, head_count, key_dim = queries.shape
    value_dim = values.shape[-1]
    block_count = length // span_size

    def arrange(array_in):
        moved = jnp.moveaxis(array_in, 1, 0)
        return moved.reshape((block_count, span_size) + moved.shape[1:])

    def token_step(memory, items):
        query_vec, key_vec, value_vec, beta_now, decay_now = items
        memory = jnp.exp(decay_now)[..., None, None] * memory
        recall = jnp.einsum('ghde,ghd->ghe', memory, key_vec, precision=lax.Precision.HIGHEST)
        update = beta_now[..., None] * (value_vec - recall)
        memory = memory + key_vec[..., :, None] * update[..., None, :]
        output = jnp.einsum('ghde,ghd->ghe', memory, query_vec, precision=lax.Precision.HIGHEST)
        return (memory, output)

    @jax.checkpoint
    def block_step(memory, items):
        return lax.scan(token_step, memory, items)
    start_memory = jnp.zeros((groups, head_count, key_dim, value_dim), jnp.float32)
    final_memory, outputs = lax.scan(block_step, start_memory, (arrange(queries), arrange(key_heads), arrange(values), arrange(strength), arrange(decay_rate)))
    outputs = outputs.reshape((length, groups, head_count, value_dim))
    return jnp.moveaxis(outputs, 0, 1)

def mixer(query_proj, key_proj, value_proj, gate_proj, beta_proj, decay_proj, query_conv, key_conv, value_conv, decay_log, decay_bias, head_gain):
    groups, length = query_proj.shape[:2]
    head_count = decay_log.shape[0]
    value_dim = head_gain.shape[0]
    key_dim = query_proj.shape[-1] // head_count
    queries = jax.nn.silu(causal_mix(query_proj, query_conv)).reshape(groups, length, head_count, key_dim)
    key_heads = jax.nn.silu(causal_mix(key_proj, key_conv)).reshape(groups, length, head_count, key_dim)
    values = jax.nn.silu(causal_mix(value_proj, value_conv)).reshape(groups, length, head_count, value_dim)
    queries = queries * lax.rsqrt(lax.optimization_barrier(jnp.sum(queries * queries, -1, keepdims=True)) + 1e-06) * key_dim ** (-0.5)
    key_heads = key_heads * lax.rsqrt(lax.optimization_barrier(jnp.sum(key_heads * key_heads, -1, keepdims=True)) + 1e-06)
    strength = jax.nn.sigmoid(beta_proj)
    decay_rate = -jnp.exp(decay_log) * jax.nn.softplus(decay_proj + decay_bias)
    outputs = recurrence(queries, key_heads, values, strength, decay_rate, STRETCH)
    normed = outputs * lax.rsqrt(lax.optimization_barrier(jnp.mean(outputs * outputs, -1, keepdims=True)) + 1e-06) * head_gain
    return normed.reshape(groups, length, head_count * value_dim) * jax.nn.silu(gate_proj)

def layer(params, rows, valid_rows):
    norm_gain, query_weight, key_weight, value_weight, query_conv, key_conv, value_conv, beta_weight, decay_weight, decay_log, decay_bias, gate_weight, head_gain, out_weight, ffn_gain, ffn_gate, ffn_up, ffn_down = params
    groups, length, model_width = rows.shape
    flat = rows.reshape(groups * length, model_width)
    first_scale = lax.rsqrt(lax.optimization_barrier(jnp.mean(flat * flat, -1, keepdims=True)) + 1e-06)
    hidden_first = low(flat * first_scale * norm_gain)

    def project(weight):
        return low_back(matmul(hidden_first, weight)).reshape(groups, length, -1)
    mixed_out = mixer(project(query_weight), project(key_weight), project(value_weight), project(gate_weight), project(beta_weight), project(decay_weight), query_conv, key_conv, value_conv, decay_log, decay_bias, head_gain)
    mixed_low = low(mixed_out.reshape(groups * length, -1))
    branch = low_back(matmul(mixed_low, out_weight.T))
    residual = flat + valid_rows * branch
    second_scale = lax.rsqrt(lax.optimization_barrier(jnp.mean(residual * residual, -1, keepdims=True)) + 1e-06)
    hidden_second = low(residual * second_scale * ffn_gain)
    gate_act = low_back(matmul(hidden_second, ffn_gate))
    up_act = low_back(matmul(hidden_second, ffn_up))
    product = low(jax.nn.silu(gate_act) * up_act)
    output = residual + valid_rows * matmul(product, ffn_down.T)
    return output.reshape(groups, length, model_width)

def reference(source_rows, cotangent, lengths, dealing, norm_gain, query_weight, key_weight, value_weight, query_conv, key_conv, value_conv, beta_weight, decay_weight, decay_log, decay_bias, gate_weight, head_gain, out_weight, ffn_gain, ffn_gate, ffn_up, ffn_down):
    params = tuple((item.astype(jnp.float32) for item in (norm_gain, query_weight, key_weight, value_weight, query_conv, key_conv, value_conv, beta_weight, decay_weight, decay_log, decay_bias, gate_weight, head_gain, out_weight, ffn_gain, ffn_gate, ffn_up, ffn_down)))
    dealt_rows = jnp.take(source_rows.astype(jnp.float32), dealing, axis=0)
    dealt_lengths = jnp.take(lengths, dealing)
    group_size = math.gcd(SEQS, max(1, 4096 // SLOT))
    group_count = SEQS // group_size

    def one_group(summed, items):
        rows, cot_rows, group_lengths = items
        valid_rows = (jnp.arange(SLOT)[None, :] < group_lengths[:, None]).astype(jnp.float32).reshape(-1, 1)
        output, pull = jax.vjp(lambda weights, inputs: layer(weights, inputs, valid_rows), params, rows)
        grads, rows_grad = pull(cot_rows)
        summed = jax.tree.map(jnp.add, summed, grads)
        return (summed, (output.astype(jnp.bfloat16), rows_grad.astype(jnp.bfloat16)))
    zeros = tuple((jnp.zeros_like(item) for item in params))
    summed, (outputs, row_grads) = lax.scan(one_group, zeros, (dealt_rows.reshape(group_count, group_size, SLOT, D), cotangent.astype(jnp.float32).reshape(group_count, group_size, SLOT, D), dealt_lengths.reshape(group_count, group_size)))
    mixed = outputs.reshape(SEQS, SLOT, D)
    dealt_grad = row_grads.reshape(SEQS, SLOT, D)
    source_grad = jnp.zeros_like(dealt_grad).at[dealing].set(dealt_grad)
    return (mixed, source_grad, summed[0], summed[1], summed[2], summed[3], summed[4], summed[5], summed[6], summed[7], summed[8], summed[9], summed[10], summed[11], summed[12], summed[13], summed[14], summed[15], summed[16], summed[17])
```

```python
import functools
import jax
import jax.numpy as jnp
from jax import lax
from jax.sharding import PartitionSpec as P
from jax.experimental import pallas as pl
from jax.experimental.pallas import tpu as pltpu

F32 = jnp.float32
BF = jnp.bfloat16
NN = ((1,), (0,))
NT = ((1,), (1,))
TN = ((0,), (0,))
CH = 128
EPS = 1e-6
TAIL = 16
VMEM_LIMIT = 30 * 1024 * 1024


def mm(a, b, dims=NN):
    return lax.dot_general(a.astype(BF), b.astype(BF), (dims, ((), ())), preferred_element_type=F32)


def mm3(a, b, dims=NN):
    ah, bh = a.astype(BF), b.astype(BF)
    al, bl = a - ah.astype(F32), b - bh.astype(F32)
    rows = a.shape[0]
    both = mm(jnp.concatenate([ah, al.astype(BF)], 0), bh, dims)
    return both[0:rows] + (both[rows:] + mm(ah, bl, dims))


def mm_exact(a, b):
    return lax.dot_general(
        a, b, (NN, ((), ())), precision=lax.Precision.HIGHEST, preferred_element_type=F32
    )


def sigm(u):
    return 0.5 * jnp.tanh(0.5 * u) + 0.5


def grid_iotas():
    return (
        lax.broadcasted_iota(jnp.int32, (CH, CH), 0),
        lax.broadcasted_iota(jnp.int32, (CH, CH), 1),
    )


def conv_rows(buf, conv, start, cols):
    acc = None
    for i in range(4):
        term = conv[i : i + 1, cols] * buf[start - 3 + i : start - 3 + i + CH, cols]
        acc = term if acc is None else acc + term
    return acc


def soft_plus(u):
    return jnp.maximum(u, 0.0) + jnp.log1p(jnp.exp(-jnp.abs(u)))


def fwd_kernel(
    heads, dk, dv, width,
    idx, x0, x1, x2, x3, gain, wq, wk, wv, wg, wba, conv, dec, hgain, wo, s_in, halo_in,
    h_out, proj_out, ba_out, u_out, o_out, st_out, t_out, z_out, send_out, keep_out, s_fin, halo_fin, scale_out, a_out, p_out,
    cbuf, gbuf, qs, ks, vs, abuf, wbuf, vbuf, nbuf, fbuf, rowb, colb,
):
    rows = x0.shape[0]
    quarter = x0.shape[1]
    qd, vd = heads * dk, heads * dv
    chunks = rows // CH
    cbuf[0:8, :] = halo_in[...]
    xs = (x0, x1, x2, x3)
    tile = 128
    for r in range(rows // tile):
        rr = slice(r * tile, r * tile + tile)
        parts = [x[rr, :].astype(F32) for x in xs]
        total = jnp.sum(sum(p * p for p in parts), -1, keepdims=True)
        scale = lax.rsqrt(total * (1.0 / width) + EPS)
        scale_out[:, rr] = jnp.transpose(jnp.broadcast_to(scale, (tile, CH)))[0:8, :]
        for n in range(4):
            cols = pl.ds(pl.multiple_of(idx[n] * quarter, quarter), quarter)
            h_out[rr, cols] = (parts[n] * scale * gain[idx[n]]).astype(BF)
    for w, lo, n in ((wq, 0, qd), (wk, qd, qd), (wv, 2 * qd, vd)):
        part = mm(h_out[...], w[...])
        cbuf[8 : 8 + rows, lo : lo + n] = part
        proj_out[:, lo : lo + n] = part
    part = mm(h_out[...], wg[...])
    gbuf[...] = part
    proj_out[:, 2 * qd + vd :] = part
    ba_out[...] = mm(h_out[...], wba[...])
    halo_fin[...] = cbuf[rows : rows + 8, :]
    ii, jj = grid_iotas()
    lower = jnp.where(ii >= jj, 1.0, 0.0).astype(F32)
    lane = lax.broadcasted_iota(jnp.int32, (1, CH), 1)
    for c in range(chunks):
        rr = slice(c * CH, c * CH + CH)
        raw = ba_out[rr, :]
        beta = sigm(raw)
        rate = dec[0:1, :] * soft_plus(raw + dec[1:2, :])
        rate = jnp.where((lane >= heads) & (lane < 2 * heads), rate, 0.0)
        run = mm_exact(lower, rate)
        colb[c] = jnp.where(lane < heads, beta, run)
        rowb[c] = jnp.transpose(run)
        for h in range(heads):
            for which, dst, mul in ((0, qs, dk ** -0.5), (qd, ks, 1.0)):
                cols = slice(which + h * dk, which + h * dk + dk)
                u = conv_rows(cbuf, conv, 8 + c * CH, cols)
                u = u * sigm(u)
                norm = lax.rsqrt(jnp.sum(u * u, -1, keepdims=True) + EPS) * mul
                dst[rr, h * dk : h * dk + dk] = u * norm
            cols = slice(2 * qd + h * dv, 2 * qd + h * dv + dv)
            u = conv_rows(cbuf, conv, 8 + c * CH, cols)
            vs[rr, h * dv : h * dv + dv] = u * sigm(u)
    units = [(c, h) for c in range(chunks) for h in range(heads)]
    xr = ii ^ jj
    eye = jnp.where(ii == jj, 1.0, 0.0).astype(F32)
    for n, (c, h) in enumerate(units):
        rr = slice(c * CH, c * CH + CH)
        k = ks[rr, h * dk : h * dk + dk]
        bc = colb[c, :, heads + h : heads + h + 1]
        br = rowb[c, heads + h : heads + h + 1, :]
        bt = colb[c, :, h : h + 1]
        a = jnp.where(ii > jj, bt * mm(k, k, NT) * jnp.exp(bc - br), 0.0)
        abuf[n] = a.astype(BF)
        a_out[n] = a
        t_out[n] = (eye - jnp.where(xr == 1, a, 0.0)).astype(BF)
    step = 2
    while step < CH:
        for n in range(len(units)):
            t = t_out[n]
            part = jnp.where((xr >= step) & (xr < 2 * step), abuf[n].astype(F32), 0.0)
            t_out[n] = (t.astype(F32) - mm(mm(t, part), t)).astype(BF)
        step *= 2
    for n, (c, h) in enumerate(units):
        rr = slice(c * CH, c * CH + CH)
        k = ks[rr, h * dk : h * dk + dk]
        v = vs[rr, h * dv : h * dv + dv]
        bc = colb[c, :, heads + h : heads + h + 1]
        bt = colb[c, :, h : h + 1]
        last = colb[c, CH - 1 : CH, heads + h : heads + h + 1]
        t = jnp.where(ii > jj, t_out[n].astype(F32), 0.0).astype(BF)
        t_out[n] = t
        bk, bv = (bt * jnp.exp(bc)) * k, bt * v
        w = (bk + mm(t, bk)).astype(BF)
        vv = bv + mm(t, bv)
        wbuf[n] = w
        vbuf[n] = vv
        kt = (k * jnp.exp(last - bc)).astype(BF)
        nbuf[n] = mm(kt, w, TN).astype(BF)
        fbuf[n] = mm(kt, vv, TN)
    for h in range(heads):
        s_fin[h] = s_in[h]
    for c in range(chunks):
        rr = slice(c * CH, c * CH + CH)
        for h in range(heads):
            n = c * heads + h
            s = s_fin[h]
            sb = s.astype(BF)
            st_out[n] = sb
            last = colb[c, CH - 1 : CH, heads + h : heads + h + 1]
            s_fin[h] = jnp.exp(last) * s + fbuf[n] - mm(nbuf[n], sb)
        for h in range(heads):
            n = c * heads + h
            q = qs[rr, h * dk : h * dk + dk]
            k = ks[rr, h * dk : h * dk + dk]
            bc = colb[c, :, heads + h : heads + h + 1]
            br = rowb[c, heads + h : heads + h + 1, :]
            p = jnp.where(ii >= jj, mm3(q, k, NT) * jnp.exp(bc - br), 0.0)
            p_out[n] = p
            s = st_out[n]
            both = mm(jnp.concatenate([wbuf[n], (q * jnp.exp(bc)).astype(BF)], 0), s)
            u = vbuf[n] - both[0:CH]
            u_out[rr, h * dv : h * dv + dv] = u
            o = both[CH:] + mm3(p, u)
            o_out[rr, h * dv : h * dv + dv] = o
            scale = lax.rsqrt(jnp.mean(o * o, -1, keepdims=True) + EPS)
            g = gbuf[rr, h * dv : h * dv + dv]
            z = o * scale * hgain[...] * (g * sigm(g))
            z_out[rr, h * dv : h * dv + dv] = z.astype(BF)
    out_blocks(idx, z_out, wo, send_out, keep_out, rows, quarter)


def out_blocks(idx, src, wo, send_out, keep_out, rows, quarter):
    for dst, pos, which in ((send_out, 0, 3), (send_out, 1, 2), (keep_out, 0, 1), (keep_out, 1, 0)):
        blk = pl.ds(pl.multiple_of(idx[which] * quarter, quarter), quarter)
        dst[pos] = mm(src[...], wo[blk, :], NT).astype(BF)


def mixer_forward(idx, xs, gain, wq, wk, wv, wg, wba, conv, dec, hgain, wo, s_in, halo_in):
    rows, quarter = xs[0].shape
    width = wq.shape[0]
    heads, dk, dv = s_in.shape
    qd, vd = heads * dk, heads * dv
    units = rows // CH * heads
    chunks = rows // CH
    outs = [
        ((rows, width), BF), ((rows, 2 * qd + 2 * vd), F32), ((rows, CH), F32),
        ((rows, vd), F32), ((rows, vd), F32), ((units, dk, dv), BF), ((units, CH, CH), BF),
        ((rows, vd), BF), ((2, rows, quarter), BF), ((2, rows, quarter), BF),
        ((heads, dk, dv), F32), ((8, 2 * qd + vd), F32), ((8, rows), F32),
        ((units, CH, CH), F32), ((units, CH, CH), F32),
    ]
    smem = pl.BlockSpec(memory_space=pltpu.SMEM)
    vm = pl.BlockSpec(memory_space=pltpu.VMEM)
    return pl.pallas_call(
        functools.partial(fwd_kernel, heads, dk, dv, width),
        out_shape=[jax.ShapeDtypeStruct(s, d) for s, d in outs],
        in_specs=[smem] + [vm] * 16,
        out_specs=[vm] * len(outs),
        scratch_shapes=[
            pltpu.VMEM((rows + 8, 2 * qd + vd), F32), pltpu.VMEM((rows, vd), F32),
            pltpu.VMEM((rows, qd), F32), pltpu.VMEM((rows, qd), F32), pltpu.VMEM((rows, vd), F32),
            pltpu.VMEM((units, CH, CH), BF), pltpu.VMEM((units, CH, dk), BF),
            pltpu.VMEM((units, CH, dv), F32), pltpu.VMEM((units, dk, dk), BF),
            pltpu.VMEM((units, dk, dv), F32), pltpu.VMEM((chunks, CH, CH), F32),
            pltpu.VMEM((chunks, CH, CH), F32),
        ],
        compiler_params=pltpu.CompilerParams(vmem_limit_bytes=VMEM_LIMIT),
        cost_estimate=pl.CostEstimate(flops=rows * 32000000, bytes_accessed=12 * rows * 1024, transcendentals=rows * 4096),
        name="mix_fwd",
    )(idx, *xs, gain, wq, wk, wv, wg, wba, conv, dec, hgain, wo, s_in, halo_in)


def bwd_kernel(
    heads, dk, dv, width,
    idx, amine, acore, h_in, proj, ba, u_in, o_in, st_in, t_in, a_in, p_in, wq, wk, wv, wg, wba, conv, dec, hgain, wo,
    halo_in, ds_in, dhalo_in,
    dproj_out, dba_out, send_out, keep_out, small_out, ds_fin, dhalo_fin,
    da_out, dzb, pbuf, cbuf, sgbuf, dcbuf, dob, qs, ks, vs, r0b, ktb, d0b, mb, dsb, rowb, colb,
):
    rows, quarter = amine.shape[1:]
    qd, vd = heads * dk, heads * dv
    cw = 2 * qd + vd
    chunks = rows // CH
    units = [(c, h) for c in range(chunks) for h in range(heads)]
    ii, jj = grid_iotas()
    lower = jnp.where(ii >= jj, 1.0, 0.0).astype(F32)
    strict = jnp.where(ii > jj, 1.0, 0.0).astype(F32)
    upper = jnp.where(ii <= jj, 1.0, 0.0).astype(F32)
    lane = lax.broadcasted_iota(jnp.int32, (1, CH), 1)
    for n, a in enumerate((amine.at[0], amine.at[1], acore.at[0], acore.at[1])):
        cols = pl.ds(pl.multiple_of(idx[n] * quarter, quarter), quarter)
        da_out[:, cols] = a[...]
    dzb[...] = mm(da_out[...], wo[...])
    pbuf[0:8, :] = halo_in[...]
    pbuf[8 : 8 + rows, :] = proj[:, 0:cw].astype(F32)
    dcbuf[rows : rows + 8, :] = dhalo_in[...]
    hg = hgain[...]
    ghead = jnp.zeros((1, dv), F32)
    for c in range(chunks):
        rr = slice(c * CH, c * CH + CH)
        raw = ba[rr, :]
        rate = dec[0:1, :] * soft_plus(raw + dec[1:2, :])
        rate = jnp.where((lane >= heads) & (lane < 2 * heads), rate, 0.0)
        run = mm_exact(lower, rate)
        act = jnp.where(lane < heads, sigm(raw), run)
        colb[c] = act
        rowb[c] = jnp.transpose(act)
        for h in range(heads):
            for which, dst, mul in ((0, qs, dk ** -0.5), (qd, ks, 1.0)):
                cols = slice(which + h * dk, which + h * dk + dk)
                u = conv_rows(pbuf, conv, 8 + c * CH, cols)
                sg = sigm(u)
                cbuf[rr, cols] = u
                sgbuf[rr, cols] = sg
                u = u * sg
                norm = lax.rsqrt(jnp.sum(u * u, -1, keepdims=True) + EPS) * mul
                dst[rr, h * dk : h * dk + dk] = u * norm
            cols = slice(2 * qd + h * dv, 2 * qd + h * dv + dv)
            u = conv_rows(pbuf, conv, 8 + c * CH, cols)
            sg = sigm(u)
            cbuf[rr, cols] = u
            sgbuf[rr, cols] = sg
            vs[rr, h * dv : h * dv + dv] = u * sg
            hv = slice(h * dv, h * dv + dv)
            o = o_in[rr, hv].astype(F32)
            scale = lax.rsqrt(jnp.mean(o * o, -1, keepdims=True) + EPS)
            on = o * scale
            g = proj[rr, cw + h * dv : cw + h * dv + dv].astype(F32)
            sg = sigm(g)
            dzh = dzb[rr, hv]
            dproj_out[rr, cw + h * dv : cw + h * dv + dv] = (
                dzh * on * hg * (sg * (1.0 + g * (1.0 - sg)))
            ).astype(BF)
            dn = dzh * (g * sg)
            ghead = ghead + jnp.sum(dn * on, 0, keepdims=True)
            e = dn * hg
            dob[rr, hv] = scale * (e - on * jnp.mean(e * on, -1, keepdims=True))
    small_out[...] = jnp.zeros_like(small_out)
    small_out[4:5, 0:dv] = ghead
    for n, (c, h) in enumerate(units):
        rr = slice(c * CH, c * CH + CH)
        q = qs[rr, h * dk : h * dk + dk]
        k = ks[rr, h * dk : h * dk + dk]
        do = dob[rr, h * dv : h * dv + dv]
        bc = colb[c, :, heads + h : heads + h + 1]
        br = rowb[c, heads + h : heads + h + 1, :]
        bt = colb[c, :, h : h + 1]
        last = colb[c, CH - 1 : CH, heads + h : heads + h + 1]
        grow = jnp.exp(bc)
        t = t_in[n]
        pd = mm3(jnp.transpose(p_in[n]), do)
        r0 = pd + mm(t, pd, TN)
        kt = k * jnp.exp(last - bc)
        kt = (kt + mm(t, kt, TN)).astype(BF)
        bgk = (bt * grow * k).astype(BF)
        r0b[n] = r0
        ktb[n] = kt
        d0b[n] = mm(grow * q, do, TN) - mm(bgk, r0, TN)
        mb[n] = mm(bgk, kt, TN).astype(BF)
    for h in range(heads):
        ds_fin[h] = ds_in[h]
    for c in reversed(range(chunks)):
        for h in range(heads):
            n = c * heads + h
            s = ds_fin[h]
            sb = s.astype(BF)
            dsb[n] = s
            last = colb[c, CH - 1 : CH, heads + h : heads + h + 1]
            ds_fin[h] = jnp.exp(last) * s + d0b[n] - mm(mb[n], sb)
    for c in range(chunks):
        rr = slice(c * CH, c * CH + CH)
        first = jnp.zeros((CH, CH), F32)
        second = jnp.zeros((CH, CH), F32)
        gextra = jnp.zeros((CH, CH), F32)
        for h in range(heads):
            n = c * heads + h
            q = qs[rr, h * dk : h * dk + dk]
            k = ks[rr, h * dk : h * dk + dk]
            v = vs[rr, h * dv : h * dv + dv]
            do = dob[rr, h * dv : h * dv + dv]
            u = u_in[rr, h * dv : h * dv + dv]
            s0 = st_in[n]
            ds = dsb[n]
            dsl = ds.astype(BF)
            qf, kf = q, k
            bc = colb[c, :, heads + h : heads + h + 1]
            br = rowb[c, heads + h : heads + h + 1, :]
            bt = colb[c, :, h : h + 1]
            btr = rowb[c, h : h + 1, :]
            last = colb[c, CH - 1 : CH, heads + h : heads + h + 1]
            grow = jnp.exp(bc)
            tail = jnp.exp(last - bc)
            r = r0b[n] + mm(ktb[n], dsl)
            dec_d = jnp.exp(bc - br)
            uh = u.astype(BF)
            ul = (u - uh.astype(F32)).astype(BF)
            pairh = jnp.concatenate([r, do], 0)
            pairl = pairh - pairh.astype(BF).astype(F32)
            raw4 = mm(jnp.concatenate([pairh, pairl], 0), uh, NT)
            raw = raw4[0 : 2 * CH] + (raw4[2 * CH :] + mm(pairh, ul, NT))
            da = jnp.where(ii > jj, -raw[0:CH] * dec_d, 0.0)
            dp = jnp.where(ii >= jj, raw[CH:] * dec_d, 0.0)
            inter = raw[CH:] * p_in[n] - raw[0:CH] * a_in[n]
            ih = inter.astype(BF)
            cums = mm(upper, jnp.concatenate([ih, (inter - ih.astype(F32)).astype(BF)], 1))
            cum = cums[:, 0:CH] + cums[:, CH:]
            states = mm(pairh, s0, NT)
            rs = grow * states[0:CH]
            dq1 = grow * states[CH:]
            local = mm(jnp.concatenate([dp, da], 0), k)
            dq = dq1 + local[0:CH]
            x = local[CH:] - rs
            us = tail * mm(uh, dsl, NT)
            dkw = mm(jnp.concatenate([dp, bt * da], 0), jnp.concatenate([q, k], 0), TN) + us
            dk_all = bt * x + dkw
            dbeta = jnp.sum(kf * x, -1, keepdims=True) + jnp.sum(r * v, -1, keepdims=True)
            ci = jnp.sum(qf * dq1 - bt * (kf * rs), -1, keepdims=True)
            wj = jnp.sum(kf * us, -1, keepdims=True)
            base = jnp.sum(jnp.where(jj < ii, cum, 0.0), -1, keepdims=True)
            whole = jnp.exp(last) * jnp.sum(
                jnp.sum(s0.astype(F32) * ds, -1, keepdims=True), 0, keepdims=True
            )
            first = first + jnp.where(lane == heads + h, ci, 0.0)
            second = second + jnp.where(lane == heads + h, wj, 0.0)
            gextra = gextra + jnp.where(lane == heads + h, base + whole, 0.0)
            gextra = gextra + jnp.where(lane == h, dbeta, 0.0)
            for dst, grad, mul in ((0, dq, dk ** -0.5), (qd, dk_all, 1.0)):
                cols = slice(dst + h * dk, dst + h * dk + dk)
                cv = cbuf[rr, cols]
                sg = sgbuf[rr, cols]
                y = cv * sg
                norm = lax.rsqrt(jnp.sum(y * y, -1, keepdims=True) + EPS)
                yn = y * norm
                dy = (norm * mul) * (grad - yn * jnp.sum(grad * yn, -1, keepdims=True))
                dcbuf[rr, cols] = dy * (sg * (1.0 + cv * (1.0 - sg)))
            cols = slice(2 * qd + h * dv, 2 * qd + h * dv + dv)
            cv = cbuf[rr, cols]
            sg = sgbuf[rr, cols]
            dcbuf[rr, cols] = bt * r * (sg * (1.0 + cv * (1.0 - sg)))
        dg = mm_exact(upper, first) + mm_exact(strict, second) + gextra
        raw = ba[rr, :]
        act = raw + dec[1:2, :]
        sp = soft_plus(act)
        sb = sigm(raw)
        dfac = dec[0:1, :]
        isb = lane < heads
        isd = (lane >= heads) & (lane < 2 * heads)
        draw = jnp.where(isb, dg * sb * (1.0 - sb), jnp.where(isd, dg * dfac * sigm(act), 0.0))
        dba_out[rr, :] = draw.astype(BF)
        small_out[5:6, 0:CH] += jnp.sum(jnp.where(isd, dg * dfac * sp, 0.0), 0, keepdims=True)
        small_out[6:7, 0:CH] += jnp.sum(jnp.where(isd, draw, 0.0), 0, keepdims=True)
    dhalo_fin[...] = dcbuf[0:8, :]
    for c in range(chunks):
        rr = slice(c * CH, c * CH + CH)
        for lo in range(0, cw, 256):
            cols = slice(lo, lo + 256)
            acc = None
            dc = dcbuf[rr, cols]
            for i in range(4):
                sh = slice(c * CH + 3 - i, c * CH + 3 - i + CH)
                term = conv[i : i + 1, cols] * dcbuf[sh, cols]
                acc = term if acc is None else acc + term
                src = pbuf[c * CH + 5 + i : c * CH + 5 + i + CH, cols]
                small_out[i : i + 1, cols] += jnp.sum(dc * src, 0, keepdims=True)
            dproj_out[rr, cols] = acc.astype(BF)
    rowsum = jnp.zeros((8, rows), F32)
    ones = jnp.ones((8, quarter), BF)
    for dst, pos, which in ((send_out, 0, 3), (send_out, 1, 2), (keep_out, 0, 1), (keep_out, 1, 0)):
        blk = pl.ds(pl.multiple_of(idx[which] * quarter, quarter), quarter)
        out = (
            mm(dproj_out[:, 0:qd], wq[blk, :], NT)
            + mm(dproj_out[:, qd : 2 * qd], wk[blk, :], NT)
            + mm(dproj_out[:, 2 * qd : cw], wv[blk, :], NT)
            + mm(dproj_out[:, cw:], wg[blk, :], NT)
            + mm(dba_out[...], wba[blk, :], NT)
        )
        dst[pos, 0:rows, :] = out.astype(BF)
        prod = out * h_in[:, blk].astype(F32)
        small_out[7:8, blk] = jnp.sum(prod, 0, keepdims=True)
        rowsum = rowsum + mm(ones, prod, NT)
    put_stats(send_out, keep_out, rowsum, rows, quarter)


def put_stats(send_out, keep_out, rowsum, rows, quarter):
    for dst in (send_out, keep_out):
        dst[:, rows : rows + TAIL, :] = jnp.zeros((2, TAIL, quarter), BF)
        for n in range(rows // quarter):
            dst[0, rows + n : rows + n + 1, :] = rowsum[0:1, n * quarter : n * quarter + quarter].astype(BF)


def mixer_backward(idx, das, h, proj, ba, u, o, st, t, a, p, wq, wk, wv, wg, wba, conv, dec, hgain, wo, halo, ds, dhalo):
    rows, quarter = das[0].shape[1:]
    width = wq.shape[0]
    heads, dk, dv = ds.shape
    qd, vd = heads * dk, heads * dv
    cw = 2 * qd + vd
    chunks = rows // CH
    units = chunks * heads
    outs = [
        ((rows, cw + vd), BF), ((rows, CH), BF), ((2, rows + TAIL, quarter), BF), ((2, rows + TAIL, quarter), BF),
        ((8, width), F32), ((heads, dk, dv), F32), ((8, cw), F32),
    ]
    smem = pl.BlockSpec(memory_space=pltpu.SMEM)
    vm = pl.BlockSpec(memory_space=pltpu.VMEM)
    return pl.pallas_call(
        functools.partial(bwd_kernel, heads, dk, dv, width),
        out_shape=[jax.ShapeDtypeStruct(s, d) for s, d in outs],
        in_specs=[smem] + [vm] * 23,
        out_specs=[vm] * len(outs),
        scratch_shapes=[
            pltpu.VMEM((rows, width), BF), pltpu.VMEM((rows, vd), F32),
            pltpu.VMEM((rows + 8, cw), F32), pltpu.VMEM((rows, cw), F32), pltpu.VMEM((rows, cw), F32), pltpu.VMEM((rows + 8, cw), F32),
            pltpu.VMEM((rows, vd), F32),
            pltpu.VMEM((rows, qd), F32), pltpu.VMEM((rows, qd), F32), pltpu.VMEM((rows, vd), F32),
            pltpu.VMEM((units, CH, dv), F32), pltpu.VMEM((units, CH, CH), BF),
            pltpu.VMEM((units, dk, dv), F32), pltpu.VMEM((units, dk, dk), BF),
            pltpu.VMEM((units, dk, dv), F32), pltpu.VMEM((chunks, CH, CH), F32),
            pltpu.VMEM((chunks, CH, CH), F32),
        ],
        compiler_params=pltpu.CompilerParams(vmem_limit_bytes=VMEM_LIMIT),
        cost_estimate=pl.CostEstimate(flops=rows * 58000000, bytes_accessed=24 * rows * 1024, transcendentals=rows * 8192),
        name="mix_bwd",
    )(idx, *das, h, proj, ba, u, o, st, t, a, p, wq, wk, wv, wg, wba, conv, dec, hgain, wo, halo, ds, dhalo)


def ffn_kernel(
    width, base, folded,
    idx, mine, core, c0, c1, c2, c3, gain, wg, wu, wd, *refs,
):
    (
        h_out, df_out, hid_out, dfg_out, dfu_out, send_out, keep_out, fsend_out, fkeep_out, gsum_out, scale_out,
        fgb, fub, dhb,
    ) = refs[2 * folded :]
    rows, quarter = mine.shape[1:]
    tile = CH
    rs, cs = (mine.at[0], mine.at[1], core.at[0], core.at[1]), (c0, c1, c2, c3)
    for r in range(rows // tile):
        rr = slice(r * tile, r * tile + tile)
        total = None
        for n in range(4):
            part = jnp.square(rs[n][rr, :].astype(F32) / gain[idx[n]])
            part = jnp.sum(part, -1, keepdims=True)
            total = part if total is None else total + part
        scale = lax.rsqrt(total * (1.0 / width) + EPS)
        scale_out[:, rr] = jnp.transpose(jnp.broadcast_to(scale, (tile, CH)))[0:8, :]
        place = base + r * tile + lax.broadcasted_iota(jnp.int32, (tile, 1), 0)
        valid = jnp.where(place < idx[4], 1.0, 0.0).astype(F32)
        for n in range(4):
            cols = pl.ds(pl.multiple_of(idx[n] * quarter, quarter), quarter)
            h_out[rr, cols] = rs[n][rr, :]
            df_out[rr, cols] = (cs[n][base + r * tile : base + r * tile + tile, :].astype(F32) * valid).astype(BF)
    fgb[...] = mm(h_out[...], wg[...], NT)
    fub[...] = mm(h_out[...], wu[...], NT)
    dhb[...] = mm(df_out[...], wd[...], NT)
    for r in range(rows // tile):
        rr = slice(r * tile, r * tile + tile)
        scale = jnp.transpose(jnp.broadcast_to(scale_out[0:1, rr], (CH, tile)))[:, 0:1]
        fg = scale * fgb[rr, :]
        fu = scale * fub[rr, :]
        ds = scale * dhb[rr, :]
        sg = sigm(fg)
        act = fg * sg
        hid_out[rr, :] = (act * fu).astype(BF)
        dfg_out[rr, :] = (ds * fu * sg * (1.0 + fg * (1.0 - sg))).astype(BF)
        dfu_out[rr, :] = (ds * act).astype(BF)
    rowsum = jnp.zeros((8, rows), F32)
    ones = jnp.ones((8, quarter), BF)
    order = ((0, 0, 3), (0, 1, 2), (1, 0, 1), (1, 1, 0))
    for kept, pos, which in order:
        blk = pl.ds(pl.multiple_of(idx[which] * quarter, quarter), quarter)
        out = mm(dfg_out[...], wg[:, blk]) + mm(dfu_out[...], wu[:, blk])
        (keep_out if kept else send_out)[pos, 0:rows, :] = out.astype(BF)
        prod = out * h_out[:, blk].astype(F32)
        gsum_out[0:1, blk] = jnp.sum(prod, 0, keepdims=True)
        rowsum = rowsum + mm(ones, prod, NT)
    put_stats(send_out, keep_out, rowsum, rows, quarter)
    for kept, pos, which in order:
        blk = pl.ds(pl.multiple_of(idx[which] * quarter, quarter), quarter)
        (fkeep_out if kept else fsend_out)[pos] = mm(hid_out[...], wd[:, blk]).astype(BF)


def ffn_both(base, idx, mine, core, cs, gain, wg, wu, wd, fold=None):
    rows, quarter = mine.shape[1:]
    units, width = wg.shape
    length = cs[0].shape[0]
    tall = ((2, rows + TAIL, quarter), BF)
    whole = ((2, length, quarter), BF)
    outs = [
        ((rows, width), BF), ((rows, width), BF), ((rows, units), BF), ((rows, units), BF), ((rows, units), BF),
        tall, tall, whole, whole, ((1, width), F32), ((8, rows), F32),
    ]
    smem = pl.BlockSpec(memory_space=pltpu.SMEM)
    vm = pl.BlockSpec(memory_space=pltpu.VMEM)
    part = base // rows
    slab = pl.BlockSpec((2, rows, quarter), lambda i: (0, part, 0), pipeline_mode=pl.Buffered(1))
    args = (idx, mine, core, *cs, gain, wg, wu, wd)
    specs = [smem] + [vm] * 10
    alias = {}
    if fold is not None:
        args += tuple(fold)
        specs += [pl.BlockSpec(memory_space=pl.ANY)] * 2
        alias = {len(args) - 2: 7, len(args) - 1: 8}
    return pl.pallas_call(
        functools.partial(ffn_kernel, width, base, fold is not None),
        grid=(1,),
        out_shape=[jax.ShapeDtypeStruct(s, d) for s, d in outs],
        in_specs=specs,
        out_specs=[vm] * 7 + [slab, slab, vm, vm],
        scratch_shapes=[pltpu.VMEM((rows, units), F32)] * 3,
        input_output_aliases=alias,
        compiler_params=pltpu.CompilerParams(vmem_limit_bytes=VMEM_LIMIT),
        cost_estimate=pl.CostEstimate(flops=rows * 27000000, bytes_accessed=10 * rows * width, transcendentals=rows * units),
        name="ffn_both",
    )(*args)


def valid_rows(idx, start, count):
    place = start + lax.broadcasted_iota(jnp.int32, (count, 1), 0)
    return jnp.where(place < idx[4], 1.0, 0.0).astype(F32)


def columns(row):
    block = jnp.transpose(jnp.broadcast_to(row, (CH, CH)))
    return jnp.concatenate([block, block], 1)


def resid_kernel(base, idx, t, u, x0, x1, gain, r_out, low_out):
    m = valid_rows(idx, base, t.shape[1])
    for n, x in ((0, x0), (1, x1)):
        r = x[...].astype(F32) + m * (t[1 - n].astype(F32) + u[n].astype(F32))
        r_out[n] = r
        low_out[n] = (r * gain[idx[n]]).astype(BF)


def part_specs(base, rows, quarter):
    once = pl.Buffered(1)
    return (
        pl.BlockSpec((2, rows, quarter), lambda i: (0, 0, 0), pipeline_mode=once),
        pl.BlockSpec((rows, quarter), lambda i: (0, 0), pipeline_mode=once),
        pl.BlockSpec((rows, quarter), lambda i: (base // rows, 0), pipeline_mode=once),
        pl.BlockSpec(memory_space=pltpu.SMEM),
        pl.BlockSpec(memory_space=pltpu.VMEM),
    )


def resid_step(base, idx, t, u, x0, x1, gain):
    rows, quarter = t.shape[1:]
    pair, tile, whole, smem, vm = part_specs(base, rows, quarter)
    return pl.pallas_call(
        functools.partial(resid_kernel, base),
        grid=(1,),
        out_shape=[jax.ShapeDtypeStruct(t.shape, F32), jax.ShapeDtypeStruct(t.shape, BF)],
        in_specs=[smem, pair, pair, whole, tile, vm],
        out_specs=[pair, pair],
        name="resid",
    )(idx, t, u, x0, x1, gain)


def stat_row(tail, c, quarter):
    line, at = c * CH // quarter, c * CH % quarter
    return tail[0, line : line + 1, at : at + CH].astype(F32)


def dresid_kernel(base, width, idx, t, tt, u, ut, r, c0, c1, gain, scale, dr_out, da_out):
    rows, quarter = r.shape[1:]
    for c in range(rows // CH):
        rr = slice(c * CH, c * CH + CH)
        m = valid_rows(idx, base + c * CH, CH)
        dot = stat_row(tt, c, quarter) + stat_row(ut, c, quarter)
        s = scale[0:1, rr]
        fac = columns(s * s * dot * (1.0 / width))
        for n, cot in ((0, c0), (1, c1)):
            d = t[1 - n, rr, :].astype(F32) + u[n, rr, :].astype(F32)
            dr = cot[rr, :].astype(F32) + d * gain[idx[n]] - r[n, rr, :] * fac
            if n == 0:
                dr_out[rr, :] = dr
            da_out[n, rr, :] = (m * dr).astype(BF)


def dresid_step(base, width, idx, t, u, r, c0, c1, gain, scale):
    rows, quarter = r.shape[1:]
    pair, tile, whole, smem, vm = part_specs(base, rows, quarter)
    foot = pl.BlockSpec((1, TAIL, quarter), lambda i: (0, rows // TAIL, 0))
    line = vm
    return pl.pallas_call(
        functools.partial(dresid_kernel, base, width),
        grid=(1,),
        out_shape=[jax.ShapeDtypeStruct(r.shape[1:], F32), jax.ShapeDtypeStruct(r.shape, BF)],
        in_specs=[smem, pair, foot, pair, foot, pair, whole, whole, vm, line],
        out_specs=[tile, pair],
        name="dresid",
    )(idx, t, t, u, u, r, c0, c1, gain, scale)


def dinput_kernel(width, idx, keep, kt, got, gt, back, bt, dr, x0, gain, scale, *refs):
    rows, quarter = dr.shape
    g = gain[idx[0]]
    for c in range(rows // CH):
        rr = slice(c * CH, c * CH + CH)
        dot = stat_row(kt, c, quarter) + stat_row(gt, c, quarter) + stat_row(bt, c, quarter)
        s = scale[0:1, rr]
        d = keep[0, rr, :].astype(F32) + got[0, rr, :].astype(F32) + back[0, rr, :].astype(F32)
        fac = columns(s * s * dot * (1.0 / width))
        dx = dr[rr, :] + columns(s) * (d * g) - x0[rr, :].astype(F32) * fac
        refs[-1][rr, :] = dx.astype(BF)


def dinput_step(base, width, idx, keep, got, back, dr, x0, gain, scale, fold=None):
    rows, quarter = dr.shape
    pair, tile, whole, smem, vm = part_specs(base, rows, quarter)
    one = pl.BlockSpec((1, rows, quarter), lambda i: (1, 0, 0))
    zero = pl.BlockSpec((1, rows, quarter), lambda i: (0, 0, 0))
    foot = pl.BlockSpec((1, TAIL, quarter), lambda i: (0, rows // TAIL, 0))
    line = vm
    back = back[None]
    args = (idx, keep, keep, got, got, back, back, dr, x0, gain, scale)
    specs = [smem, one, foot, one, foot, zero, foot, tile, whole, vm, line]
    alias = {}
    if fold is not None:
        alias = {len(args): 0}
        args += (fold,)
        specs.append(pl.BlockSpec(memory_space=pl.ANY))
    return pl.pallas_call(
        functools.partial(dinput_kernel, width),
        grid=(1,),
        out_shape=jax.ShapeDtypeStruct(x0.shape, BF),
        in_specs=specs,
        out_specs=whole,
        input_output_aliases=alias,
        name="dinput",
    )(*args)


def share_order(first):
    b0, b1, b2 = first
    kept = [((k >> 1) & 1) << b1 | (k & 1) << b2 for k in range(4)]
    return kept, [k | 1 << b0 for k in kept]


def ffn_grad_kernel(parts, units, at, *refs):
    ins, outs, buf = refs[: 5 * parts], refs[5 * parts : 5 * parts + 4], refs[-1]
    half = units // 2
    whole, low, high = (0, units), (0, half), (half, units)
    for left, right, places in (
        (2, 0, ((0, 0, whole),)), (3, 1, ((0, units, low), (1, 0, high))), (4, 1, ((1, half, whole),))
    ):
        total = None
        for s in range(parts):
            part = mm(ins[5 * s + left][...], ins[5 * s + right][...], TN)
            total = part if total is None else total + part
        buf[...] = total
        for group, first, (lo, hi) in places:
            kept, sent = share_order(FIRST if group == 0 else SECOND)
            for n in range(4):
                for dst, pos in ((outs[2 * group], sent), (outs[2 * group + 1], kept)):
                    blk = pl.ds(pl.multiple_of((at[5] ^ pos[n]) * 128, 128), 128)
                    dst[n, first : first + hi - lo, :] = buf[lo:hi, blk].astype(BF)


FIRST, SECOND = (0, 1, 2), (1, 0, 2)


def ffn_grads(at, ffn):
    rows, width = ffn[0][0].shape
    units = ffn[0][2].shape[1]
    args = [a for f in ffn for a in (f[1], f[0], f[2], f[3], f[4])]
    smem = pl.BlockSpec(memory_space=pltpu.SMEM)
    vm = pl.BlockSpec(memory_space=pltpu.VMEM)
    shapes = [(4, units + units // 2, 128)] * 4
    return pl.pallas_call(
        functools.partial(ffn_grad_kernel, len(ffn), units),
        out_shape=[jax.ShapeDtypeStruct(s, BF) for s in shapes],
        in_specs=[smem] + [vm] * len(args),
        out_specs=[vm] * 4,
        scratch_shapes=[pltpu.VMEM((units, width), F32)],
        compiler_params=pltpu.CompilerParams(vmem_limit_bytes=VMEM_LIMIT),
        cost_estimate=pl.CostEstimate(flops=9 * 10 ** 9, bytes_accessed=10 ** 7, transcendentals=0),
        name="ffn_grads",
    )(at, *args)


def row_grad_kernel(parts, plan, at, *refs):
    count = len(refs) - 2 * len(plan) - len(plan)
    ins = refs[:count]
    outs = refs[count : count + 2 * len(plan)]
    bufs = refs[count + 2 * len(plan) :]
    each = count // parts
    for group, (order, pieces) in enumerate(plan):
        buf = bufs[group]
        col = 0
        for left, right, lo, n in pieces:
            total = None
            for s in range(parts):
                part = mm(ins[each * s + left][...], ins[each * s + right][:, lo : lo + n], TN)
                total = part if total is None else total + part
            buf[:, col : col + n] = total
            col += n
        kept, sent = share_order(order)
        for n in range(4):
            for dst, pos in ((outs[2 * group], sent), (outs[2 * group + 1], kept)):
                blk = pl.ds(pl.multiple_of((at[5] ^ pos[n]) * 128, 128), 128)
                dst[n] = buf[blk, :].astype(BF)


def out_grad_kernel(parts, at, *refs):
    ins, (send, keep, full, buf) = refs[: 3 * parts], refs[3 * parts :]
    quarter = ins[0].shape[2]
    total = None
    for s in range(parts):
        mine, core, z = ins[3 * s : 3 * s + 3]
        for n, a in enumerate((mine.at[0], mine.at[1], core.at[0], core.at[1])):
            full[:, pl.ds(pl.multiple_of(at[n] * quarter, quarter), quarter)] = a[...]
        part = mm(full[...], z[...], TN)
        total = part if total is None else total + part
    buf[...] = total
    kept, sent = share_order(SECOND)
    for n in range(4):
        for dst, pos in ((send, sent), (keep, kept)):
            blk = pl.ds(pl.multiple_of((at[5] ^ pos[n]) * 128, 128), 128)
            dst[n] = buf[blk, :].astype(BF)


def out_grads(at, parts, args):
    rows, n = args[2].shape
    width = 4 * args[0].shape[2]
    smem = pl.BlockSpec(memory_space=pltpu.SMEM)
    vm = pl.BlockSpec(memory_space=pltpu.VMEM)
    return pl.pallas_call(
        functools.partial(out_grad_kernel, parts),
        out_shape=[jax.ShapeDtypeStruct((4, 128, n), BF)] * 2,
        in_specs=[smem] + [vm] * len(args),
        out_specs=[vm] * 2,
        scratch_shapes=[pltpu.VMEM((rows, width), BF), pltpu.VMEM((width, n), F32)],
        compiler_params=pltpu.CompilerParams(vmem_limit_bytes=VMEM_LIMIT),
        cost_estimate=pl.CostEstimate(flops=4 * 10 ** 9, bytes_accessed=10 ** 7, transcendentals=0),
        name="out_grads",
    )(at, *args)


def row_grads(at, parts, plan, args):
    width = args[0].shape[1]
    smem = pl.BlockSpec(memory_space=pltpu.SMEM)
    vm = pl.BlockSpec(memory_space=pltpu.VMEM)
    wides = [sum(p[3] for p in pieces) for _, pieces in plan]
    return pl.pallas_call(
        functools.partial(row_grad_kernel, parts, plan),
        out_shape=[jax.ShapeDtypeStruct((4, 128, w), BF) for w in wides for _ in range(2)],
        in_specs=[smem] + [vm] * len(args),
        out_specs=[vm] * (2 * len(plan)),
        scratch_shapes=[pltpu.VMEM((width, w), F32) for w in wides],
        compiler_params=pltpu.CompilerParams(vmem_limit_bytes=VMEM_LIMIT),
        cost_estimate=pl.CostEstimate(flops=6 * 10 ** 9, bytes_accessed=10 ** 7, transcendentals=0),
        name="row_grads",
    )(at, *args)


def swap(array, axis, size, bit):
    return lax.ppermute(array, axis, [(i, i ^ bit) for i in range(size)])


def beside(array):
    return swap(array, "tensor", 4, 1)


def across(array):
    return swap(array, "tensor", 4, 2)


def after(array, *others):
    return lax.optimization_barrier((array,) + others)[0]


def plus(left, right):
    return (left.astype(F32) + right.astype(F32)).astype(BF)


def total_tensor(array):
    array = array + beside(array)
    return array + across(array)


class Share:
    def __init__(self, send, keep, size, order):
        low = size.bit_length() - 1 - 3
        self.size, self.low = size, low
        self.bits = [1 << (low + b) for b in order]
        self.send, self.terms = send, [keep]

    def start(self, *deps):
        send = after(self.send, *deps) if deps else self.send
        self.terms.append(swap(send, "dp", self.size, self.bits[len(self.terms) - 1]))

    def middle(self, *deps):
        half = 2 if len(self.terms) == 2 else 1
        got = after(self.terms[-1], *deps) if deps else self.terms[-1]
        self.terms[-1] = got
        total = sum(t[half : 2 * half].astype(F32) for t in self.terms)
        self.send = total.astype(BF)

    def finish(self, axis, *deps):
        got = after(self.terms[-1], *deps) if deps else self.terms[-1]
        total = sum(t[0].astype(F32) for t in self.terms[:-1]) + got[0].astype(F32)
        me = lax.axis_index("dp")
        for bit in range(self.low - 1, -1, -1):
            half = total.shape[axis] // 2
            mine = (me >> bit) & 1
            send = lax.dynamic_slice_in_dim(total, (1 - mine) * half, half, axis).astype(BF)
            keep = lax.dynamic_slice_in_dim(total, mine * half, half, axis)
            total = keep + swap(send, "dp", self.size, 1 << bit).astype(F32)
        return total


NSEG = 2


def per_device(
    source_rows, cotangent, lengths, dealing, norm_gain, query_weight, key_weight, value_weight,
    query_conv, key_conv, value_conv, beta_weight, decay_weight, decay_log, decay_bias, gate_weight,
    head_gain, out_weight, ffn_gain, ffn_gate, ffn_up, ffn_down,
):
    dp = lax.axis_size("dp")
    me = lax.axis_index("tensor").astype(jnp.int32)
    block = lax.axis_index("dp").astype(jnp.int32) // (dp // 8)
    length, quarter = cotangent.shape[1:]
    width = norm_gain.shape[0]
    heads, dv = decay_log.shape[0], head_gain.shape[0]
    dk = query_weight.shape[1] // heads
    qd, vd = heads * dk, heads * dv
    cw = 2 * qd + vd
    units = ffn_gate.shape[1]
    rows = length // NSEG
    pieces = [slice(s * rows, s * rows + rows) for s in range(NSEG)]
    own = lax.dynamic_slice_in_dim

    cot = cotangent[0]
    cot1 = across(cot)
    cot2 = beside(cot)
    ordered = jnp.take(source_rows, dealing, axis=0)
    arrived = lax.all_to_all(ordered, "dp", split_axis=0, concat_axis=1, tiled=True)[0]
    own_length = jnp.take(lengths, dealing)[lax.axis_index("dp")]
    idx = jnp.stack([me, me ^ 2, me ^ 1, me ^ 3, own_length, block, block, block])

    wba = jnp.pad(jnp.concatenate([beta_weight, decay_weight], 1), ((0, 0), (0, CH - 2 * heads)))
    conv = jnp.concatenate([query_conv, key_conv, value_conv], 1)
    dec = jnp.stack([-jnp.exp(decay_log), decay_bias])
    dec = jnp.pad(dec, ((0, 6), (heads, CH - 2 * heads)))
    gain1 = norm_gain.reshape(4, 1, quarter)
    gain2 = ffn_gain.reshape(4, 1, quarter)
    hgain = head_gain[None]
    mixw = (query_weight, key_weight, value_weight, gate_weight, wba, conv, dec, hgain, out_weight)

    xs = []
    for s, p in enumerate(pieces):
        x = after(arrived[p], cot1 if s == 0 else xs[s - 1][1])
        x1 = across(x)
        xs.append((arrived[p], x1, beside(x), beside(x1)))
    cot3 = beside(cot1)
    cots = (cot, cot1, cot2, cot3)

    state = jnp.zeros((heads, dk, dv), F32)
    halo = jnp.zeros((8, cw), F32)
    halos, front, t, u = [], [], [], []
    for s in range(NSEG):
        if s > 0:
            state = after(state, t[s - 1])
        halos.append(halo)
        out = mixer_forward(idx, xs[s], gain1, *mixw, state, halo)
        state, halo = out[10], out[11]
        front.append(out)
        send = after(out[8], xs[s + 1][1]) if s + 1 < NSEG else out[8]
        t.append(plus(out[9], beside(send)))
        u.append(across(t[s]))
    resid, low, ffn, t2, u2 = [], [], [], [], []
    for s in range(NSEG):
        last = front[NSEG - 1][10] if s < NSEG - 1 else ffn[s - 1][10]
        r, lo = resid_step(s * rows, idx, t[s], after(u[s], last), arrived, xs[s][1], gain2)
        resid.append(r)
        low.append(lo)
        core = beside(lo)
        if s < NSEG - 1:
            lo = after(lo, t[s + 1])
        else:
            lo = after(lo, t2[s - 1])
        fold = None if s == 0 else ffn[s - 1][7:9]
        f = ffn_both(s * rows, idx, lo, core, cots, gain2, ffn_gate.T, ffn_up.T, ffn_down.T, fold)
        ffn.append(f)
        got = beside(f[5] if s == 0 else after(f[5], u2[s - 1]))
        t2.append(plus(f[6], got))
        u2.append(across(t2[s]))
    hold = t2[NSEG - 1]
    grads = ffn_grads(after(idx, hold), ffn)
    shares = [Share(grads[0], grads[1], dp, FIRST), Share(grads[2], grads[3], dp, SECOND)]
    dr, da = [], []
    for s in range(NSEG):
        wait = (hold,) if s == 0 else (grads[0], da[s - 1][0])
        d, a = dresid_step(
            s * rows, width, idx, t2[s], after(u2[s], *wait), resid[s], cot, cot1, gain2, ffn[s][10]
        )
        dr.append(d)
        da.append((a, beside(a)))
        if s == 0:
            for sh in shares:
                sh.start()

    back = [None] * NSEG
    ds = jnp.zeros((heads, dk, dv), F32)
    dhalo = jnp.zeros((8, cw), F32)
    got1, away1, bk1 = [None] * NSEG, [None] * NSEG, [None] * NSEG
    fsend, fkeep = ffn[NSEG - 1][7:9]
    fgot = beside(after(fsend, da[NSEG - 1][1]))
    for s in reversed(range(NSEG)):
        o = front[s]
        mine = da[s][0]
        if s < NSEG - 1:
            mine = after(mine, away1[s + 1], outg[0], *[sh.send for sh in shares])
        b = mixer_backward(
            idx, (mine, da[s][1]), o[0], o[1], o[2], o[3], o[4], o[5], o[6], o[13], o[14], *mixw, halos[s], ds, dhalo
        )
        ds, dhalo = b[5], b[6]
        back[s] = b
        if s == NSEG - 1:
            got1[s] = beside(b[2])
            away1[s] = plus(b[3][0], got1[s][0])
        else:
            got1[s] = beside(after(b[2], bk1[s + 1], *[sh.terms[-1] for sh in shares]))
            dx = dinput_step(
                (s + 1) * rows, width, idx, back[s + 1][3], got1[s + 1], after(bk1[s + 1], ds), dr[s + 1],
                arrived, gain1, front[s + 1][12],
            )
            away1[s] = plus(b[3][0], after(got1[s], dx)[0])
        bk1[s] = across(away1[s])
        if s == NSEG - 1:
            for sh in shares:
                sh.middle(ds)
                sh.start()
            outg = out_grads(
                after(idx, away1[s]), NSEG, [v for q in range(NSEG) for v in (*da[q], front[q][7])]
            )
            outs = Share(outg[0], outg[1], dp, SECOND)
            outs.start()
    faway = plus(fkeep[0], fgot[0])
    fback = across(after(faway, bk1[NSEG - 1]))
    small = after(sum(b[4] for b in back), away1[0])
    gsum = sum(f[9] for f in ffn)
    ends = total_tensor(jnp.concatenate([small[4:5], small[7:8], gsum], 0))
    small = jnp.concatenate([small[0:7], ends, jnp.zeros((6, width), F32)], 0)

    lead = []
    for s in range(NSEG):
        o, b = front[s], back[s]
        lead += [o[0], after(b[0], away1[0]), b[1]]
    quart = vd // 2
    plan = (
        (FIRST, ((0, 1, 0, 2 * qd), (0, 1, cw, quart), (0, 2, 0, CH))),
        (SECOND, ((0, 1, 2 * qd, vd), (0, 1, cw + quart, quart))),
    )
    wide = row_grads(idx, NSEG, plan, lead)
    tails = [Share(wide[0], wide[1], dp, FIRST), Share(wide[2], wide[3], dp, SECOND)]
    for sh in tails:
        sh.start()
    small = small + swap(after(small, wide[0]), "dp", dp, 1)
    for sh in shares + [outs]:
        sh.middle(wide[0])
        sh.start()
    keep = after(back[0][3], wide[0])
    dx = dinput_step(0, width, idx, keep, got1[0], bk1[0], dr[0], arrived, gain1, front[0][12], dx)
    returned = lax.all_to_all(
        dx.reshape(dp, length // dp, quarter), "dp", split_axis=0, concat_axis=0, tiled=True
    )
    for sh in tails:
        sh.middle(dx)
        sh.start()
    small = small + swap(after(small, tails[0].send), "dp", dp, 2)
    outs.middle(dx)
    outs.start()
    lower, upper = [sh.finish(1, tails[0].send) for sh in shares]
    mask = (jnp.arange(length) < own_length).astype(F32)[:, None]
    rest = fkeep[1].astype(F32) + after(fgot, dx)[1].astype(F32) + fback.astype(F32)
    mixed = (jnp.concatenate([r[0] for r in resid], 0) + mask * rest).astype(BF)
    for sh in tails:
        sh.middle()
        sh.start()
    small = small + swap(after(small, tails[0].send), "dp", dp, 4)
    bit = 8
    while bit < dp:
        small = small + swap(small, "dp", dp, bit)
        bit *= 2
    source_grad = jnp.zeros_like(returned).at[dealing].set(after(returned, tails[0].send))
    outw = outs.finish(0, tails[0].send)
    wide1, wide2 = [sh.finish(0) for sh in tails]
    shared, summed = small[0:7], small[7:10]
    part = width // dp
    start = lax.axis_index("dp") * part
    norm_gain_grad = own(summed[1] / norm_gain, start, part)
    ffn_gain_grad = own(summed[2] / ffn_gain, start, part)
    return (
        mixed[None],
        source_grad,
        norm_gain_grad,
        wide1[:, 0:qd],
        wide1[:, qd : 2 * qd],
        wide2[:, 0:vd],
        shared[0:4, 0:qd],
        shared[0:4, qd : 2 * qd],
        shared[0:4, 2 * qd : cw],
        wide1[:, 2 * qd + quart : 2 * qd + quart + heads],
        wide1[:, 2 * qd + quart + heads : 2 * qd + quart + 2 * heads],
        shared[5, heads : 2 * heads],
        shared[6, heads : 2 * heads],
        jnp.concatenate([wide1[:, 2 * qd : 2 * qd + quart], wide2[:, vd:]], 1),
        summed[0, 0:dv],
        outw,
        ffn_gain_grad,
        jnp.concatenate([lower[units:], upper[: units // 2]], 0).T,
        upper[units // 2 :].T,
        lower[:units].T,
    )


def solution(mesh):
    in_specs = (
        P(None, "dp", "tensor"),
        P("dp", None, "tensor"),
        P(),
        P(),
        P(),
        P(None, "tensor"),
        P(None, "tensor"),
        P(None, "tensor"),
        P(None, "tensor"),
        P(None, "tensor"),
        P(None, "tensor"),
        P(None, "tensor"),
        P(None, "tensor"),
        P("tensor"),
        P("tensor"),
        P(None, "tensor"),
        P(),
        P(None, "tensor"),
        P(),
        P(None, "tensor"),
        P(None, "tensor"),
        P(None, "tensor"),
    )
    out_specs = (
        P("dp", None, "tensor"),
        P(None, "dp", "tensor"),
        P("dp"),
        P("dp", "tensor"),
        P("dp", "tensor"),
        P("dp", "tensor"),
        P(None, "tensor"),
        P(None, "tensor"),
        P(None, "tensor"),
        P("dp", "tensor"),
        P("dp", "tensor"),
        P("tensor"),
        P("tensor"),
        P("dp", "tensor"),
        P(),
        P("dp", "tensor"),
        P("dp"),
        P("dp", "tensor"),
        P("dp", "tensor"),
        P("dp", "tensor"),
    )
    return jax.shard_map(
        per_device, mesh=mesh, in_specs=in_specs, out_specs=out_specs, check_vma=False
    )
```

```python
import functools
import jax
import jax.numpy as jnp
from jax import lax
from jax.sharding import PartitionSpec as P
from jax.experimental import pallas as pl
from jax.experimental.pallas import tpu as pltpu

F32 = jnp.float32
BF = jnp.bfloat16
NN = ((1,), (0,))
NT = ((1,), (1,))
TN = ((0,), (0,))
CH = 128
EPS = 1e-6
TAIL = 16
VMEM_LIMIT = 56 * 1024 * 1024


def mm(a, b, dims=NN):
    return lax.dot_general(a.astype(BF), b.astype(BF), (dims, ((), ())), preferred_element_type=F32)


def mm3(a, b, dims=NN):
    ah, bh = a.astype(BF), b.astype(BF)
    al, bl = a - ah.astype(F32), b - bh.astype(F32)
    rows = a.shape[0]
    both = mm(jnp.concatenate([ah, al.astype(BF)], 0), bh, dims)
    return both[0:rows] + (both[rows:] + mm(ah, bl, dims))


def mm_exact(a, b):
    return lax.dot_general(
        a, b, (NN, ((), ())), precision=lax.Precision.HIGHEST, preferred_element_type=F32
    )


def sigm(u):
    return 0.5 * jnp.tanh(0.5 * u) + 0.5


def grid_iotas():
    return (
        lax.broadcasted_iota(jnp.int32, (CH, CH), 0),
        lax.broadcasted_iota(jnp.int32, (CH, CH), 1),
    )


def conv_rows(buf, conv, start, cols):
    acc = None
    for i in range(4):
        term = conv[i : i + 1, cols] * buf[start - 3 + i : start - 3 + i + CH, cols]
        acc = term if acc is None else acc + term
    return acc


def soft_plus(u):
    return jnp.maximum(u, 0.0) + jnp.log1p(jnp.exp(-jnp.abs(u)))


def fwd_kernel(
    heads, dk, dv, width,
    idx, x0, x1, x2, x3, gain, wq, wk, wv, wg, wba, conv, dec, hgain, wo, s_in, halo_in,
    h_out, proj_out, ba_out, u_out, o_out, st_out, t_out, z_out, send_out, keep_out, s_fin, halo_fin, scale_out, a_out, p_out,
    cbuf, gbuf, qs, ks, vs, abuf, wbuf, vbuf, nbuf, fbuf, rowb, colb,
):
    rows = x0.shape[0]
    quarter = x0.shape[1]
    qd, vd = heads * dk, heads * dv
    chunks = rows // CH
    cbuf[0:8, :] = halo_in[...]
    xs = (x0, x1, x2, x3)
    tile = 128
    for r in range(rows // tile):
        rr = slice(r * tile, r * tile + tile)
        parts = [x[rr, :].astype(F32) for x in xs]
        total = jnp.sum(sum(p * p for p in parts), -1, keepdims=True)
        scale = lax.rsqrt(total * (1.0 / width) + EPS)
        scale_out[:, rr] = jnp.transpose(jnp.broadcast_to(scale, (tile, CH)))[0:8, :]
        for n in range(4):
            cols = pl.ds(pl.multiple_of(idx[n] * quarter, quarter), quarter)
            h_out[rr, cols] = (parts[n] * scale * gain[idx[n]]).astype(BF)
    for w, lo, n in ((wq, 0, qd), (wk, qd, qd), (wv, 2 * qd, vd)):
        part = mm(h_out[...], w[...])
        cbuf[8 : 8 + rows, lo : lo + n] = part
        proj_out[:, lo : lo + n] = part
    part = mm(h_out[...], wg[...])
    gbuf[...] = part
    proj_out[:, 2 * qd + vd :] = part
    ba_out[...] = mm(h_out[...], wba[...])
    halo_fin[...] = cbuf[rows : rows + 8, :]
    ii, jj = grid_iotas()
    lower = jnp.where(ii >= jj, 1.0, 0.0).astype(F32)
    lane = lax.broadcasted_iota(jnp.int32, (1, CH), 1)
    for c in range(chunks):
        rr = slice(c * CH, c * CH + CH)
        raw = ba_out[rr, :]
        beta = sigm(raw)
        rate = dec[0:1, :] * soft_plus(raw + dec[1:2, :])
        rate = jnp.where((lane >= heads) & (lane < 2 * heads), rate, 0.0)
        run = mm_exact(lower, rate)
        colb[c] = jnp.where(lane < heads, beta, run)
        rowb[c] = jnp.transpose(run)
        for h in range(heads):
            for which, dst, mul in ((0, qs, dk ** -0.5), (qd, ks, 1.0)):
                cols = slice(which + h * dk, which + h * dk + dk)
                u = conv_rows(cbuf, conv, 8 + c * CH, cols)
                u = u * sigm(u)
                norm = lax.rsqrt(jnp.sum(u * u, -1, keepdims=True) + EPS) * mul
                dst[rr, h * dk : h * dk + dk] = u * norm
            cols = slice(2 * qd + h * dv, 2 * qd + h * dv + dv)
            u = conv_rows(cbuf, conv, 8 + c * CH, cols)
            vs[rr, h * dv : h * dv + dv] = u * sigm(u)
    units = [(c, h) for c in range(chunks) for h in range(heads)]
    xr = ii ^ jj
    eye = jnp.where(ii == jj, 1.0, 0.0).astype(F32)
    for n, (c, h) in enumerate(units):
        rr = slice(c * CH, c * CH + CH)
        k = ks[rr, h * dk : h * dk + dk]
        bc = colb[c, :, heads + h : heads + h + 1]
        br = rowb[c, heads + h : heads + h + 1, :]
        bt = colb[c, :, h : h + 1]
        a = jnp.where(ii > jj, bt * mm(k, k, NT) * jnp.exp(bc - br), 0.0)
        abuf[n] = a.astype(BF)
        a_out[n] = a
        t_out[n] = (eye - jnp.where(xr == 1, a, 0.0)).astype(BF)
    step = 2
    while step < CH:
        for n in range(len(units)):
            t = t_out[n]
            part = jnp.where((xr >= step) & (xr < 2 * step), abuf[n].astype(F32), 0.0)
            t_out[n] = (t.astype(F32) - mm(mm(t, part), t)).astype(BF)
        step *= 2
    for n, (c, h) in enumerate(units):
        rr = slice(c * CH, c * CH + CH)
        k = ks[rr, h * dk : h * dk + dk]
        v = vs[rr, h * dv : h * dv + dv]
        bc = colb[c, :, heads + h : heads + h + 1]
        bt = colb[c, :, h : h + 1]
        last = colb[c, CH - 1 : CH, heads + h : heads + h + 1]
        t = jnp.where(ii > jj, t_out[n].astype(F32), 0.0).astype(BF)
        t_out[n] = t
        bk, bv = (bt * jnp.exp(bc)) * k, bt * v
        w = (bk + mm(t, bk)).astype(BF)
        vv = bv + mm(t, bv)
        wbuf[n] = w
        vbuf[n] = vv
        kt = (k * jnp.exp(last - bc)).astype(BF)
        nbuf[n] = mm(kt, w, TN).astype(BF)
        fbuf[n] = mm(kt, vv, TN)
    for h in range(heads):
        s_fin[h] = s_in[h]
    for c in range(chunks):
        rr = slice(c * CH, c * CH + CH)
        for h in range(heads):
            n = c * heads + h
            s = s_fin[h]
            sb = s.astype(BF)
            st_out[n] = sb
            last = colb[c, CH - 1 : CH, heads + h : heads + h + 1]
            s_fin[h] = jnp.exp(last) * s + fbuf[n] - mm(nbuf[n], sb)
        for h in range(heads):
            n = c * heads + h
            q = qs[rr, h * dk : h * dk + dk]
            k = ks[rr, h * dk : h * dk + dk]
            bc = colb[c, :, heads + h : heads + h + 1]
            br = rowb[c, heads + h : heads + h + 1, :]
            p = jnp.where(ii >= jj, mm3(q, k, NT) * jnp.exp(bc - br), 0.0)
            p_out[n] = p
            s = st_out[n]
            both = mm(jnp.concatenate([wbuf[n], (q * jnp.exp(bc)).astype(BF)], 0), s)
            u = vbuf[n] - both[0:CH]
            u_out[rr, h * dv : h * dv + dv] = u
            o = both[CH:] + mm3(p, u)
            o_out[rr, h * dv : h * dv + dv] = o
            scale = lax.rsqrt(jnp.mean(o * o, -1, keepdims=True) + EPS)
            g = gbuf[rr, h * dv : h * dv + dv]
            z = o * scale * hgain[...] * (g * sigm(g))
            z_out[rr, h * dv : h * dv + dv] = z.astype(BF)
    out_blocks(idx, z_out, wo, send_out, keep_out, rows, quarter)


def out_blocks(idx, src, wo, send_out, keep_out, rows, quarter):
    for dst, pos, which in ((send_out, 0, 3), (send_out, 1, 2), (keep_out, 0, 1), (keep_out, 1, 0)):
        blk = pl.ds(pl.multiple_of(idx[which] * quarter, quarter), quarter)
        dst[pos] = mm(src[...], wo[blk, :], NT).astype(BF)


def mixer_forward(idx, xs, gain, wq, wk, wv, wg, wba, conv, dec, hgain, wo, s_in, halo_in):
    rows, quarter = xs[0].shape
    width = wq.shape[0]
    heads, dk, dv = s_in.shape
    qd, vd = heads * dk, heads * dv
    units = rows // CH * heads
    chunks = rows // CH
    outs = [
        ((rows, width), BF), ((rows, 2 * qd + 2 * vd), F32), ((rows, CH), F32),
        ((rows, vd), F32), ((rows, vd), F32), ((units, dk, dv), BF), ((units, CH, CH), BF),
        ((rows, vd), BF), ((2, rows, quarter), BF), ((2, rows, quarter), BF),
        ((heads, dk, dv), F32), ((8, 2 * qd + vd), F32), ((8, rows), F32),
        ((units, CH, CH), F32), ((units, CH, CH), F32),
    ]
    smem = pl.BlockSpec(memory_space=pltpu.SMEM)
    vm = pl.BlockSpec(memory_space=pltpu.VMEM)
    return pl.pallas_call(
        functools.partial(fwd_kernel, heads, dk, dv, width),
        out_shape=[jax.ShapeDtypeStruct(s, d) for s, d in outs],
        in_specs=[smem] + [vm] * 16,
        out_specs=[vm] * len(outs),
        scratch_shapes=[
            pltpu.VMEM((rows + 8, 2 * qd + vd), F32), pltpu.VMEM((rows, vd), F32),
            pltpu.VMEM((rows, qd), F32), pltpu.VMEM((rows, qd), F32), pltpu.VMEM((rows, vd), F32),
            pltpu.VMEM((units, CH, CH), BF), pltpu.VMEM((units, CH, dk), BF),
            pltpu.VMEM((units, CH, dv), F32), pltpu.VMEM((units, dk, dk), BF),
            pltpu.VMEM((units, dk, dv), F32), pltpu.VMEM((chunks, CH, CH), F32),
            pltpu.VMEM((chunks, CH, CH), F32),
        ],
        compiler_params=pltpu.CompilerParams(vmem_limit_bytes=VMEM_LIMIT),
        cost_estimate=pl.CostEstimate(flops=rows * 32000000, bytes_accessed=12 * rows * 1024, transcendentals=rows * 4096),
        name="mix_fwd",
    )(idx, *xs, gain, wq, wk, wv, wg, wba, conv, dec, hgain, wo, s_in, halo_in)


def bwd_kernel(
    heads, dk, dv, width,
    idx, amine, acore, h_in, proj, ba, u_in, o_in, st_in, t_in, a_in, p_in, wq, wk, wv, wg, wba, conv, dec, hgain, wo,
    halo_in, ds_in, dhalo_in,
    dproj_out, dba_out, send_out, keep_out, small_out, ds_fin, dhalo_fin,
    da_out, dzb, pbuf, cbuf, sgbuf, dcbuf, dob, qs, ks, vs, r0b, ktb, d0b, mb, dsb, rowb, colb,
):
    rows, quarter = amine.shape[1:]
    qd, vd = heads * dk, heads * dv
    cw = 2 * qd + vd
    chunks = rows // CH
    units = [(c, h) for c in range(chunks) for h in range(heads)]
    ii, jj = grid_iotas()
    lower = jnp.where(ii >= jj, 1.0, 0.0).astype(F32)
    strict = jnp.where(ii > jj, 1.0, 0.0).astype(F32)
    upper = jnp.where(ii <= jj, 1.0, 0.0).astype(F32)
    lane = lax.broadcasted_iota(jnp.int32, (1, CH), 1)
    for n, a in enumerate((amine.at[0], amine.at[1], acore.at[0], acore.at[1])):
        cols = pl.ds(pl.multiple_of(idx[n] * quarter, quarter), quarter)
        da_out[:, cols] = a[...]
    dzb[...] = mm(da_out[...], wo[...])
    pbuf[0:8, :] = halo_in[...]
    pbuf[8 : 8 + rows, :] = proj[:, 0:cw].astype(F32)
    dcbuf[rows : rows + 8, :] = dhalo_in[...]
    hg = hgain[...]
    ghead = jnp.zeros((1, dv), F32)
    for c in range(chunks):
        rr = slice(c * CH, c * CH + CH)
        raw = ba[rr, :]
        rate = dec[0:1, :] * soft_plus(raw + dec[1:2, :])
        rate = jnp.where((lane >= heads) & (lane < 2 * heads), rate, 0.0)
        run = mm_exact(lower, rate)
        act = jnp.where(lane < heads, sigm(raw), run)
        colb[c] = act
        rowb[c] = jnp.transpose(act)
        for h in range(heads):
            for which, dst, mul in ((0, qs, dk ** -0.5), (qd, ks, 1.0)):
                cols = slice(which + h * dk, which + h * dk + dk)
                u = conv_rows(pbuf, conv, 8 + c * CH, cols)
                sg = sigm(u)
                cbuf[rr, cols] = u
                sgbuf[rr, cols] = sg
                u = u * sg
                norm = lax.rsqrt(jnp.sum(u * u, -1, keepdims=True) + EPS) * mul
                dst[rr, h * dk : h * dk + dk] = u * norm
            cols = slice(2 * qd + h * dv, 2 * qd + h * dv + dv)
            u = conv_rows(pbuf, conv, 8 + c * CH, cols)
            sg = sigm(u)
            cbuf[rr, cols] = u
            sgbuf[rr, cols] = sg
            vs[rr, h * dv : h * dv + dv] = u * sg
            hv = slice(h * dv, h * dv + dv)
            o = o_in[rr, hv].astype(F32)
            scale = lax.rsqrt(jnp.mean(o * o, -1, keepdims=True) + EPS)
            on = o * scale
            g = proj[rr, cw + h * dv : cw + h * dv + dv].astype(F32)
            sg = sigm(g)
            dzh = dzb[rr, hv]
            dproj_out[rr, cw + h * dv : cw + h * dv + dv] = (
                dzh * on * hg * (sg * (1.0 + g * (1.0 - sg)))
            ).astype(BF)
            dn = dzh * (g * sg)
            ghead = ghead + jnp.sum(dn * on, 0, keepdims=True)
            e = dn * hg
            dob[rr, hv] = scale * (e - on * jnp.mean(e * on, -1, keepdims=True))
    small_out[...] = jnp.zeros_like(small_out)
    small_out[4:5, 0:dv] = ghead
    for n, (c, h) in enumerate(units):
        rr = slice(c * CH, c * CH + CH)
        q = qs[rr, h * dk : h * dk + dk]
        k = ks[rr, h * dk : h * dk + dk]
        do = dob[rr, h * dv : h * dv + dv]
        bc = colb[c, :, heads + h : heads + h + 1]
        br = rowb[c, heads + h : heads + h + 1, :]
        bt = colb[c, :, h : h + 1]
        last = colb[c, CH - 1 : CH, heads + h : heads + h + 1]
        grow = jnp.exp(bc)
        t = t_in[n]
        pd = mm3(jnp.transpose(p_in[n]), do)
        r0 = pd + mm(t, pd, TN)
        kt = k * jnp.exp(last - bc)
        kt = (kt + mm(t, kt, TN)).astype(BF)
        bgk = (bt * grow * k).astype(BF)
        r0b[n] = r0
        ktb[n] = kt
        d0b[n] = mm(grow * q, do, TN) - mm(bgk, r0, TN)
        mb[n] = mm(bgk, kt, TN).astype(BF)
    for h in range(heads):
        ds_fin[h] = ds_in[h]
    for c in reversed(range(chunks)):
        for h in range(heads):
            n = c * heads + h
            s = ds_fin[h]
            sb = s.astype(BF)
            dsb[n] = s
            last = colb[c, CH - 1 : CH, heads + h : heads + h + 1]
            ds_fin[h] = jnp.exp(last) * s + d0b[n] - mm(mb[n], sb)
    for c in range(chunks):
        rr = slice(c * CH, c * CH + CH)
        first = jnp.zeros((CH, CH), F32)
        second = jnp.zeros((CH, CH), F32)
        gextra = jnp.zeros((CH, CH), F32)
        for h in range(heads):
            n = c * heads + h
            q = qs[rr, h * dk : h * dk + dk]
            k = ks[rr, h * dk : h * dk + dk]
            v = vs[rr, h * dv : h * dv + dv]
            do = dob[rr, h * dv : h * dv + dv]
            u = u_in[rr, h * dv : h * dv + dv]
            s0 = st_in[n]
            ds = dsb[n]
            dsl = ds.astype(BF)
            qf, kf = q, k
            bc = colb[c, :, heads + h : heads + h + 1]
            br = rowb[c, heads + h : heads + h + 1, :]
            bt = colb[c, :, h : h + 1]
            btr = rowb[c, h : h + 1, :]
            last = colb[c, CH - 1 : CH, heads + h : heads + h + 1]
            grow = jnp.exp(bc)
            tail = jnp.exp(last - bc)
            r = r0b[n] + mm(ktb[n], dsl)
            dec_d = jnp.exp(bc - br)
            uh = u.astype(BF)
            ul = (u - uh.astype(F32)).astype(BF)
            pairh = jnp.concatenate([r, do], 0)
            pairl = pairh - pairh.astype(BF).astype(F32)
            raw4 = mm(jnp.concatenate([pairh, pairl], 0), uh, NT)
            raw = raw4[0 : 2 * CH] + (raw4[2 * CH :] + mm(pairh, ul, NT))
            da = jnp.where(ii > jj, -raw[0:CH] * dec_d, 0.0)
            dp = jnp.where(ii >= jj, raw[CH:] * dec_d, 0.0)
            inter = raw[CH:] * p_in[n] - raw[0:CH] * a_in[n]
            ih = inter.astype(BF)
            cums = mm(upper, jnp.concatenate([ih, (inter - ih.astype(F32)).astype(BF)], 1))
            cum = cums[:, 0:CH] + cums[:, CH:]
            states = mm(pairh, s0, NT)
            rs = grow * states[0:CH]
            dq1 = grow * states[CH:]
            local = mm(jnp.concatenate([dp, da], 0), k)
            dq = dq1 + local[0:CH]
            x = local[CH:] - rs
            us = tail * mm(uh, dsl, NT)
            dkw = mm(jnp.concatenate([dp, bt * da], 0), jnp.concatenate([q, k], 0), TN) + us
            dk_all = bt * x + dkw
            dbeta = jnp.sum(kf * x, -1, keepdims=True) + jnp.sum(r * v, -1, keepdims=True)
            ci = jnp.sum(qf * dq1 - bt * (kf * rs), -1, keepdims=True)
            wj = jnp.sum(kf * us, -1, keepdims=True)
            base = jnp.sum(jnp.where(jj < ii, cum, 0.0), -1, keepdims=True)
            whole = jnp.exp(last) * jnp.sum(
                jnp.sum(s0.astype(F32) * ds, -1, keepdims=True), 0, keepdims=True
            )
            first = first + jnp.where(lane == heads + h, ci, 0.0)
            second = second + jnp.where(lane == heads + h, wj, 0.0)
            gextra = gextra + jnp.where(lane == heads + h, base + whole, 0.0)
            gextra = gextra + jnp.where(lane == h, dbeta, 0.0)
            for dst, grad, mul in ((0, dq, dk ** -0.5), (qd, dk_all, 1.0)):
                cols = slice(dst + h * dk, dst + h * dk + dk)
                cv = cbuf[rr, cols]
                sg = sgbuf[rr, cols]
                y = cv * sg
                norm = lax.rsqrt(jnp.sum(y * y, -1, keepdims=True) + EPS)
                yn = y * norm
                dy = (norm * mul) * (grad - yn * jnp.sum(grad * yn, -1, keepdims=True))
                dcbuf[rr, cols] = dy * (sg * (1.0 + cv * (1.0 - sg)))
            cols = slice(2 * qd + h * dv, 2 * qd + h * dv + dv)
            cv = cbuf[rr, cols]
            sg = sgbuf[rr, cols]
            dcbuf[rr, cols] = bt * r * (sg * (1.0 + cv * (1.0 - sg)))
        dg = mm_exact(upper, first) + mm_exact(strict, second) + gextra
        raw = ba[rr, :]
        act = raw + dec[1:2, :]
        sp = soft_plus(act)
        sb = sigm(raw)
        dfac = dec[0:1, :]
        isb = lane < heads
        isd = (lane >= heads) & (lane < 2 * heads)
        draw = jnp.where(isb, dg * sb * (1.0 - sb), jnp.where(isd, dg * dfac * sigm(act), 0.0))
        dba_out[rr, :] = draw.astype(BF)
        small_out[5:6, 0:CH] += jnp.sum(jnp.where(isd, dg * dfac * sp, 0.0), 0, keepdims=True)
        small_out[6:7, 0:CH] += jnp.sum(jnp.where(isd, draw, 0.0), 0, keepdims=True)
    dhalo_fin[...] = dcbuf[0:8, :]
    for c in range(chunks):
        rr = slice(c * CH, c * CH + CH)
        for lo in range(0, cw, 256):
            cols = slice(lo, lo + 256)
            acc = None
            dc = dcbuf[rr, cols]
            for i in range(4):
                sh = slice(c * CH + 3 - i, c * CH + 3 - i + CH)
                term = conv[i : i + 1, cols] * dcbuf[sh, cols]
                acc = term if acc is None else acc + term
                src = pbuf[c * CH + 5 + i : c * CH + 5 + i + CH, cols]
                small_out[i : i + 1, cols] += jnp.sum(dc * src, 0, keepdims=True)
            dproj_out[rr, cols] = acc.astype(BF)
    rowsum = jnp.zeros((8, rows), F32)
    ones = jnp.ones((8, quarter), BF)
    for dst, pos, which in ((send_out, 0, 3), (send_out, 1, 2), (keep_out, 0, 1), (keep_out, 1, 0)):
        blk = pl.ds(pl.multiple_of(idx[which] * quarter, quarter), quarter)
        out = (
            mm(dproj_out[:, 0:qd], wq[blk, :], NT)
            + mm(dproj_out[:, qd : 2 * qd], wk[blk, :], NT)
            + mm(dproj_out[:, 2 * qd : cw], wv[blk, :], NT)
            + mm(dproj_out[:, cw:], wg[blk, :], NT)
            + mm(dba_out[...], wba[blk, :], NT)
        )
        dst[pos, 0:rows, :] = out.astype(BF)
        prod = out * h_in[:, blk].astype(F32)
        small_out[7:8, blk] = jnp.sum(prod, 0, keepdims=True)
        rowsum = rowsum + mm(ones, prod, NT)
    put_stats(send_out, keep_out, rowsum, rows, quarter)


def put_stats(send_out, keep_out, rowsum, rows, quarter):
    for dst in (send_out, keep_out):
        dst[:, rows : rows + TAIL, :] = jnp.zeros((2, TAIL, quarter), BF)
        for n in range(rows // quarter):
            dst[0, rows + n : rows + n + 1, :] = rowsum[0:1, n * quarter : n * quarter + quarter].astype(BF)


def mixer_backward(idx, das, h, proj, ba, u, o, st, t, a, p, wq, wk, wv, wg, wba, conv, dec, hgain, wo, halo, ds, dhalo):
    rows, quarter = das[0].shape[1:]
    width = wq.shape[0]
    heads, dk, dv = ds.shape
    qd, vd = heads * dk, heads * dv
    cw = 2 * qd + vd
    chunks = rows // CH
    units = chunks * heads
    outs = [
        ((rows, cw + vd), BF), ((rows, CH), BF), ((2, rows + TAIL, quarter), BF), ((2, rows + TAIL, quarter), BF),
        ((8, width), F32), ((heads, dk, dv), F32), ((8, cw), F32),
    ]
    smem = pl.BlockSpec(memory_space=pltpu.SMEM)
    vm = pl.BlockSpec(memory_space=pltpu.VMEM)
    return pl.pallas_call(
        functools.partial(bwd_kernel, heads, dk, dv, width),
        out_shape=[jax.ShapeDtypeStruct(s, d) for s, d in outs],
        in_specs=[smem] + [vm] * 23,
        out_specs=[vm] * len(outs),
        scratch_shapes=[
            pltpu.VMEM((rows, width), BF), pltpu.VMEM((rows, vd), F32),
            pltpu.VMEM((rows + 8, cw), F32), pltpu.VMEM((rows, cw), F32), pltpu.VMEM((rows, cw), F32), pltpu.VMEM((rows + 8, cw), F32),
            pltpu.VMEM((rows, vd), F32),
            pltpu.VMEM((rows, qd), F32), pltpu.VMEM((rows, qd), F32), pltpu.VMEM((rows, vd), F32),
            pltpu.VMEM((units, CH, dv), F32), pltpu.VMEM((units, CH, CH), BF),
            pltpu.VMEM((units, dk, dv), F32), pltpu.VMEM((units, dk, dk), BF),
            pltpu.VMEM((units, dk, dv), F32), pltpu.VMEM((chunks, CH, CH), F32),
            pltpu.VMEM((chunks, CH, CH), F32),
        ],
        compiler_params=pltpu.CompilerParams(vmem_limit_bytes=VMEM_LIMIT),
        cost_estimate=pl.CostEstimate(flops=rows * 58000000, bytes_accessed=24 * rows * 1024, transcendentals=rows * 8192),
        name="mix_bwd",
    )(idx, *das, h, proj, ba, u, o, st, t, a, p, wq, wk, wv, wg, wba, conv, dec, hgain, wo, halo, ds, dhalo)


def ffn_kernel(
    width, base, folded,
    idx, mine, core, c0, c1, c2, c3, gain, wg, wu, wd, *refs,
):
    (
        h_out, df_out, hid_out, dfg_out, dfu_out, send_out, keep_out, fsend_out, fkeep_out, gsum_out, scale_out,
        fgb, fub, dhb,
    ) = refs[2 * folded :]
    rows, quarter = mine.shape[1:]
    tile = CH
    rs, cs = (mine.at[0], mine.at[1], core.at[0], core.at[1]), (c0, c1, c2, c3)
    for r in range(rows // tile):
        rr = slice(r * tile, r * tile + tile)
        total = None
        for n in range(4):
            part = jnp.square(rs[n][rr, :].astype(F32) / gain[idx[n]])
            part = jnp.sum(part, -1, keepdims=True)
            total = part if total is None else total + part
        scale = lax.rsqrt(total * (1.0 / width) + EPS)
        scale_out[:, rr] = jnp.transpose(jnp.broadcast_to(scale, (tile, CH)))[0:8, :]
        place = base + r * tile + lax.broadcasted_iota(jnp.int32, (tile, 1), 0)
        valid = jnp.where(place < idx[4], 1.0, 0.0).astype(F32)
        for n in range(4):
            cols = pl.ds(pl.multiple_of(idx[n] * quarter, quarter), quarter)
            h_out[rr, cols] = rs[n][rr, :]
            df_out[rr, cols] = (cs[n][base + r * tile : base + r * tile + tile, :].astype(F32) * valid).astype(BF)
    fgb[...] = mm(h_out[...], wg[...], NT)
    fub[...] = mm(h_out[...], wu[...], NT)
    dhb[...] = mm(df_out[...], wd[...], NT)
    for r in range(rows // tile):
        rr = slice(r * tile, r * tile + tile)
        scale = jnp.transpose(jnp.broadcast_to(scale_out[0:1, rr], (CH, tile)))[:, 0:1]
        fg = scale * fgb[rr, :]
        fu = scale * fub[rr, :]
        ds = scale * dhb[rr, :]
        sg = sigm(fg)
        act = fg * sg
        hid_out[rr, :] = (act * fu).astype(BF)
        dfg_out[rr, :] = (ds * fu * sg * (1.0 + fg * (1.0 - sg))).astype(BF)
        dfu_out[rr, :] = (ds * act).astype(BF)
    rowsum = jnp.zeros((8, rows), F32)
    ones = jnp.ones((8, quarter), BF)
    order = ((0, 0, 3), (0, 1, 2), (1, 0, 1), (1, 1, 0))
    for kept, pos, which in order:
        blk = pl.ds(pl.multiple_of(idx[which] * quarter, quarter), quarter)
        out = mm(dfg_out[...], wg[:, blk]) + mm(dfu_out[...], wu[:, blk])
        (keep_out if kept else send_out)[pos, 0:rows, :] = out.astype(BF)
        prod = out * h_out[:, blk].astype(F32)
        gsum_out[0:1, blk] = jnp.sum(prod, 0, keepdims=True)
        rowsum = rowsum + mm(ones, prod, NT)
    put_stats(send_out, keep_out, rowsum, rows, quarter)
    for kept, pos, which in order:
        blk = pl.ds(pl.multiple_of(idx[which] * quarter, quarter), quarter)
        (fkeep_out if kept else fsend_out)[pos] = mm(hid_out[...], wd[:, blk]).astype(BF)


def ffn_both(base, idx, mine, core, cs, gain, wg, wu, wd, fold=None):
    rows, quarter = mine.shape[1:]
    units, width = wg.shape
    length = cs[0].shape[0]
    tall = ((2, rows + TAIL, quarter), BF)
    whole = ((2, length, quarter), BF)
    outs = [
        ((rows, width), BF), ((rows, width), BF), ((rows, units), BF), ((rows, units), BF), ((rows, units), BF),
        tall, tall, whole, whole, ((1, width), F32), ((8, rows), F32),
    ]
    smem = pl.BlockSpec(memory_space=pltpu.SMEM)
    vm = pl.BlockSpec(memory_space=pltpu.VMEM)
    part = base // rows
    slab = pl.BlockSpec((2, rows, quarter), lambda i: (0, part, 0), pipeline_mode=pl.Buffered(1))
    args = (idx, mine, core, *cs, gain, wg, wu, wd)
    specs = [smem] + [vm] * 10
    alias = {}
    if fold is not None:
        args += tuple(fold)
        specs += [pl.BlockSpec(memory_space=pl.ANY)] * 2
        alias = {len(args) - 2: 7, len(args) - 1: 8}
    return pl.pallas_call(
        functools.partial(ffn_kernel, width, base, fold is not None),
        grid=(1,),
        out_shape=[jax.ShapeDtypeStruct(s, d) for s, d in outs],
        in_specs=specs,
        out_specs=[vm] * 7 + [slab, slab, vm, vm],
        scratch_shapes=[pltpu.VMEM((rows, units), F32)] * 3,
        input_output_aliases=alias,
        compiler_params=pltpu.CompilerParams(vmem_limit_bytes=24 * 1024 * 1024),
        cost_estimate=pl.CostEstimate(flops=rows * 27000000, bytes_accessed=10 * rows * width, transcendentals=rows * units),
        name="ffn_both",
    )(*args)


def valid_rows(idx, start, count):
    place = start + lax.broadcasted_iota(jnp.int32, (count, 1), 0)
    return jnp.where(place < idx[4], 1.0, 0.0).astype(F32)


def columns(row):
    block = jnp.transpose(jnp.broadcast_to(row, (CH, CH)))
    return jnp.concatenate([block, block], 1)


def resid_kernel(base, idx, t, u, x0, x1, gain, r_out, low_out):
    m = valid_rows(idx, base, t.shape[1])
    for n, x in ((0, x0), (1, x1)):
        r = x[...].astype(F32) + m * (t[1 - n].astype(F32) + u[n].astype(F32))
        r_out[n] = r
        low_out[n] = (r * gain[idx[n]]).astype(BF)


def part_specs(base, rows, quarter):
    once = pl.Buffered(1)
    return (
        pl.BlockSpec((2, rows, quarter), lambda i: (0, 0, 0), pipeline_mode=once),
        pl.BlockSpec((rows, quarter), lambda i: (0, 0), pipeline_mode=once),
        pl.BlockSpec((rows, quarter), lambda i: (base // rows, 0), pipeline_mode=once),
        pl.BlockSpec(memory_space=pltpu.SMEM),
        pl.BlockSpec(memory_space=pltpu.VMEM),
    )


def resid_step(base, idx, t, u, x0, x1, gain):
    rows, quarter = t.shape[1:]
    pair, tile, whole, smem, vm = part_specs(base, rows, quarter)
    return pl.pallas_call(
        functools.partial(resid_kernel, base),
        grid=(1,),
        out_shape=[jax.ShapeDtypeStruct(t.shape, F32), jax.ShapeDtypeStruct(t.shape, BF)],
        in_specs=[smem, pair, pair, whole, tile, vm],
        out_specs=[pair, pair],
        compiler_params=pltpu.CompilerParams(vmem_limit_bytes=10 * 1024 * 1024),
        name="resid",
    )(idx, t, u, x0, x1, gain)


def stat_row(tail, c, quarter):
    line, at = c * CH // quarter, c * CH % quarter
    return tail[0, line : line + 1, at : at + CH].astype(F32)


def dresid_kernel(base, width, idx, t, tt, u, ut, r, c0, c1, gain, scale, dr_out, da_out):
    rows, quarter = r.shape[1:]
    for c in range(rows // CH):
        rr = slice(c * CH, c * CH + CH)
        m = valid_rows(idx, base + c * CH, CH)
        dot = stat_row(tt, c, quarter) + stat_row(ut, c, quarter)
        s = scale[0:1, rr]
        fac = columns(s * s * dot * (1.0 / width))
        for n, cot in ((0, c0), (1, c1)):
            d = t[1 - n, rr, :].astype(F32) + u[n, rr, :].astype(F32)
            dr = cot[rr, :].astype(F32) + d * gain[idx[n]] - r[n, rr, :] * fac
            if n == 0:
                dr_out[rr, :] = dr
            da_out[n, rr, :] = (m * dr).astype(BF)


def dresid_step(base, width, idx, t, u, r, c0, c1, gain, scale):
    rows, quarter = r.shape[1:]
    pair, tile, whole, smem, vm = part_specs(base, rows, quarter)
    foot = pl.BlockSpec((1, TAIL, quarter), lambda i: (0, rows // TAIL, 0))
    line = vm
    return pl.pallas_call(
        functools.partial(dresid_kernel, base, width),
        grid=(1,),
        out_shape=[jax.ShapeDtypeStruct(r.shape[1:], F32), jax.ShapeDtypeStruct(r.shape, BF)],
        in_specs=[smem, pair, foot, pair, foot, pair, whole, whole, vm, line],
        out_specs=[tile, pair],
        compiler_params=pltpu.CompilerParams(vmem_limit_bytes=10 * 1024 * 1024),
        name="dresid",
    )(idx, t, t, u, u, r, c0, c1, gain, scale)


def dinput_kernel(width, idx, keep, kt, got, gt, back, bt, dr, x0, gain, scale, *refs):
    rows, quarter = dr.shape
    g = gain[idx[0]]
    for c in range(rows // CH):
        rr = slice(c * CH, c * CH + CH)
        dot = stat_row(kt, c, quarter) + stat_row(gt, c, quarter) + stat_row(bt, c, quarter)
        s = scale[0:1, rr]
        d = keep[0, rr, :].astype(F32) + got[0, rr, :].astype(F32) + back[0, rr, :].astype(F32)
        fac = columns(s * s * dot * (1.0 / width))
        dx = dr[rr, :] + columns(s) * (d * g) - x0[rr, :].astype(F32) * fac
        refs[-1][rr, :] = dx.astype(BF)


def dinput_step(base, width, idx, keep, got, back, dr, x0, gain, scale, fold=None):
    rows, quarter = dr.shape
    pair, tile, whole, smem, vm = part_specs(base, rows, quarter)
    one = pl.BlockSpec((1, rows, quarter), lambda i: (1, 0, 0))
    zero = pl.BlockSpec((1, rows, quarter), lambda i: (0, 0, 0))
    foot = pl.BlockSpec((1, TAIL, quarter), lambda i: (0, rows // TAIL, 0))
    line = vm
    back = back[None]
    args = (idx, keep, keep, got, got, back, back, dr, x0, gain, scale)
    specs = [smem, one, foot, one, foot, zero, foot, tile, whole, vm, line]
    alias = {}
    if fold is not None:
        alias = {len(args): 0}
        args += (fold,)
        specs.append(pl.BlockSpec(memory_space=pl.ANY))
    return pl.pallas_call(
        functools.partial(dinput_kernel, width),
        grid=(1,),
        out_shape=jax.ShapeDtypeStruct(x0.shape, BF),
        in_specs=specs,
        out_specs=whole,
        input_output_aliases=alias,
        compiler_params=pltpu.CompilerParams(vmem_limit_bytes=8 * 1024 * 1024),
        name="dinput",
    )(*args)


def share_order(first):
    b0, b1, b2 = first
    kept = [((k >> 1) & 1) << b1 | (k & 1) << b2 for k in range(4)]
    return kept, [k | 1 << b0 for k in kept]


def ffn_grad_kernel(parts, units, at, *refs):
    ins, outs, buf = refs[: 5 * parts], refs[5 * parts : 5 * parts + 4], refs[-1]
    half = units // 2
    whole, low, high = (0, units), (0, half), (half, units)
    for left, right, places in (
        (2, 0, ((0, 0, whole),)), (3, 1, ((0, units, low), (1, 0, high))), (4, 1, ((1, half, whole),))
    ):
        total = None
        for s in range(parts):
            part = mm(ins[5 * s + left][...], ins[5 * s + right][...], TN)
            total = part if total is None else total + part
        buf[...] = total
        for group, first, (lo, hi) in places:
            kept, sent = share_order(FIRST if group == 0 else THIRD)
            for n in range(4):
                for dst, pos in ((outs[2 * group], sent), (outs[2 * group + 1], kept)):
                    blk = pl.ds(pl.multiple_of((at[5] ^ pos[n]) * 128, 128), 128)
                    dst[n, first : first + hi - lo, :] = buf[lo:hi, blk].astype(BF)


FIRST, SECOND, THIRD = (0, 1, 2), (1, 0, 2), (1, 2, 0)


def ffn_grads(at, ffn):
    rows, width = ffn[0][0].shape
    units = ffn[0][2].shape[1]
    args = [a for f in ffn for a in (f[1], f[0], f[2], f[3], f[4])]
    smem = pl.BlockSpec(memory_space=pltpu.SMEM)
    vm = pl.BlockSpec(memory_space=pltpu.VMEM)
    shapes = [(4, units + units // 2, 128)] * 4
    return pl.pallas_call(
        functools.partial(ffn_grad_kernel, len(ffn), units),
        out_shape=[jax.ShapeDtypeStruct(s, BF) for s in shapes],
        in_specs=[smem] + [vm] * len(args),
        out_specs=[vm] * 4,
        scratch_shapes=[pltpu.VMEM((units, width), F32)],
        compiler_params=pltpu.CompilerParams(vmem_limit_bytes=22 * 1024 * 1024),
        cost_estimate=pl.CostEstimate(flops=9 * 10 ** 9, bytes_accessed=10 ** 7, transcendentals=0),
        name="ffn_grads",
    )(at, *args)


def row_grad_kernel(parts, plan, at, *refs):
    count = len(refs) - 2 * len(plan) - len(plan)
    ins = refs[:count]
    outs = refs[count : count + 2 * len(plan)]
    bufs = refs[count + 2 * len(plan) :]
    each = count // parts
    for group, (order, pieces) in enumerate(plan):
        buf = bufs[group]
        col = 0
        for left, right, lo, n in pieces:
            total = None
            for s in range(parts):
                part = mm(ins[each * s + left][...], ins[each * s + right][:, lo : lo + n], TN)
                total = part if total is None else total + part
            buf[:, col : col + n] = total
            col += n
        kept, sent = share_order(order)
        for n in range(4):
            for dst, pos in ((outs[2 * group], sent), (outs[2 * group + 1], kept)):
                blk = pl.ds(pl.multiple_of((at[5] ^ pos[n]) * 128, 128), 128)
                dst[n] = buf[blk, :].astype(BF)


def out_grad_kernel(parts, heads, at, wo, hgain, *refs):
    ins, outs, (full, dzb, dgb, obuf, gbuf) = refs[: 6 * parts], refs[6 * parts : 6 * parts + 2], refs[6 * parts + 2 :]
    quarter = ins[0].shape[2]
    rows, vd = dzb.shape
    dv = vd // heads
    out_total, gate_total = None, None
    for s in range(parts):
        mine, core, z, h, g, o = ins[6 * s : 6 * s + 6]
        for n, a in enumerate((mine.at[0], mine.at[1], core.at[0], core.at[1])):
            full[:, pl.ds(pl.multiple_of(at[n] * quarter, quarter), quarter)] = a[...]
        dzb[...] = mm(full[...], wo[...])
        for r in range(rows // CH):
            for n in range(heads):
                at_r, at_c = slice(r * CH, r * CH + CH), slice(n * dv, n * dv + dv)
                ov = o[at_r, at_c]
                on = ov * lax.rsqrt(jnp.mean(ov * ov, -1, keepdims=True) + EPS)
                gv = g[at_r, at_c]
                sg = sigm(gv)
                grad = dzb[at_r, at_c] * on * hgain[...] * (sg * (1.0 + gv * (1.0 - sg)))
                dgb[at_r, at_c] = grad.astype(BF)
        part = mm(full[...], z[...], TN)
        out_total = part if out_total is None else out_total + part
        part = mm(h[...], dgb[...], TN)
        gate_total = part if gate_total is None else gate_total + part
    obuf[...] = out_total
    gbuf[...] = gate_total
    kept, sent = share_order(FIRST)
    for n in range(4):
        for dst, pos in ((outs[0], sent), (outs[1], kept)):
            blk = pl.ds(pl.multiple_of((at[5] ^ pos[n]) * 128, 128), 128)
            dst[n, :, 0:vd] = obuf[blk, :].astype(BF)
            dst[n, :, vd:] = gbuf[blk, :].astype(BF)


def out_grads(at, parts, heads, wo, hgain, args):
    rows, n = args[2].shape
    width = 4 * args[0].shape[2]
    smem = pl.BlockSpec(memory_space=pltpu.SMEM)
    vm = pl.BlockSpec(memory_space=pltpu.VMEM)
    last = args[4].shape[1] // n - 1
    gate = pl.BlockSpec((rows, n), lambda i: (0, last), pipeline_mode=pl.Buffered(1))
    return pl.pallas_call(
        functools.partial(out_grad_kernel, parts, heads),
        grid=(1,),
        out_shape=[jax.ShapeDtypeStruct((4, 128, 2 * n), BF)] * 2,
        in_specs=[smem, vm, vm] + [vm, vm, vm, vm, gate, vm] * parts,
        out_specs=[vm] * 2,
        scratch_shapes=[
            pltpu.VMEM((rows, width), BF), pltpu.VMEM((rows, n), F32), pltpu.VMEM((rows, n), BF),
            pltpu.VMEM((width, n), F32), pltpu.VMEM((width, n), F32),
        ],
        compiler_params=pltpu.CompilerParams(vmem_limit_bytes=56 * 1024 * 1024),
        cost_estimate=pl.CostEstimate(flops=8 * 10 ** 9, bytes_accessed=10 ** 7, transcendentals=0),
        name="out_grads",
    )(at, wo, hgain, *args)


def row_grads(at, parts, plan, args):
    width = args[0].shape[1]
    smem = pl.BlockSpec(memory_space=pltpu.SMEM)
    vm = pl.BlockSpec(memory_space=pltpu.VMEM)
    wides = [sum(p[3] for p in pieces) for _, pieces in plan]
    return pl.pallas_call(
        functools.partial(row_grad_kernel, parts, plan),
        out_shape=[jax.ShapeDtypeStruct((4, 128, w), BF) for w in wides for _ in range(2)],
        in_specs=[smem] + [vm] * len(args),
        out_specs=[vm] * (2 * len(plan)),
        scratch_shapes=[pltpu.VMEM((width, w), F32) for w in wides],
        compiler_params=pltpu.CompilerParams(vmem_limit_bytes=22 * 1024 * 1024),
        cost_estimate=pl.CostEstimate(flops=6 * 10 ** 9, bytes_accessed=10 ** 7, transcendentals=0),
        name="row_grads",
    )(at, *args)


def swap(array, axis, size, bit):
    return lax.ppermute(array, axis, [(i, i ^ bit) for i in range(size)])


def beside(array):
    return swap(array, "tensor", 4, 1)


def across(array):
    return swap(array, "tensor", 4, 2)


def after(array, *others):
    return lax.optimization_barrier((array,) + others)[0]


def plus(left, right):
    return (left.astype(F32) + right.astype(F32)).astype(BF)


def total_tensor(array):
    array = array + beside(array)
    return array + across(array)


class Share:
    def __init__(self, send, keep, size, order):
        low = size.bit_length() - 1 - 3
        self.size, self.low = size, low
        self.bits = [1 << (low + b) for b in order]
        self.send, self.terms = send, [keep]

    def start(self, *deps):
        send = after(self.send, *deps) if deps else self.send
        self.terms.append(swap(send, "dp", self.size, self.bits[len(self.terms) - 1]))

    def middle(self, *deps):
        half = 2 if len(self.terms) == 2 else 1
        got = after(self.terms[-1], *deps) if deps else self.terms[-1]
        self.terms[-1] = got
        total = sum(t[half : 2 * half].astype(F32) for t in self.terms)
        self.send = total.astype(BF)

    def finish(self, axis, *deps):
        got = after(self.terms[-1], *deps) if deps else self.terms[-1]
        total = sum(t[0].astype(F32) for t in self.terms[:-1]) + got[0].astype(F32)
        me = lax.axis_index("dp")
        for bit in range(self.low - 1, -1, -1):
            half = total.shape[axis] // 2
            mine = (me >> bit) & 1
            send = lax.dynamic_slice_in_dim(total, (1 - mine) * half, half, axis).astype(BF)
            keep = lax.dynamic_slice_in_dim(total, mine * half, half, axis)
            total = keep + swap(send, "dp", self.size, 1 << bit).astype(F32)
        return total


NSEG = 2


def per_device(
    source_rows, cotangent, lengths, dealing, norm_gain, query_weight, key_weight, value_weight,
    query_conv, key_conv, value_conv, beta_weight, decay_weight, decay_log, decay_bias, gate_weight,
    head_gain, out_weight, ffn_gain, ffn_gate, ffn_up, ffn_down,
):
    dp = lax.axis_size("dp")
    me = lax.axis_index("tensor").astype(jnp.int32)
    block = lax.axis_index("dp").astype(jnp.int32) // (dp // 8)
    length, quarter = cotangent.shape[1:]
    width = norm_gain.shape[0]
    heads, dv = decay_log.shape[0], head_gain.shape[0]
    dk = query_weight.shape[1] // heads
    qd, vd = heads * dk, heads * dv
    cw = 2 * qd + vd
    units = ffn_gate.shape[1]
    rows = length // NSEG
    pieces = [slice(s * rows, s * rows + rows) for s in range(NSEG)]
    own = lax.dynamic_slice_in_dim

    cot = cotangent[0]
    cot1 = across(cot)
    cot2 = beside(cot)
    ordered = jnp.take(source_rows, dealing, axis=0)
    arrived = lax.all_to_all(ordered, "dp", split_axis=0, concat_axis=1, tiled=True)[0]
    own_length = jnp.take(lengths, dealing)[lax.axis_index("dp")]
    idx = jnp.stack([me, me ^ 2, me ^ 1, me ^ 3, own_length, block, block, block])

    wba = jnp.pad(jnp.concatenate([beta_weight, decay_weight], 1), ((0, 0), (0, CH - 2 * heads)))
    conv = jnp.concatenate([query_conv, key_conv, value_conv], 1)
    dec = jnp.stack([-jnp.exp(decay_log), decay_bias])
    dec = jnp.pad(dec, ((0, 6), (heads, CH - 2 * heads)))
    gain1 = norm_gain.reshape(4, 1, quarter)
    gain2 = ffn_gain.reshape(4, 1, quarter)
    hgain = head_gain[None]
    mixw = (query_weight, key_weight, value_weight, gate_weight, wba, conv, dec, hgain, out_weight)

    state = jnp.zeros((heads, dk, dv), F32)
    halo = jnp.zeros((8, cw), F32)
    xs = []
    for s, p in enumerate(pieces):
        first = (cot1, wba, conv, dec, idx, state, halo)
        x = after(arrived[p], *(first if s == 0 else (xs[s - 1][1],)))
        x1 = across(x)
        xs.append((arrived[p], x1, beside(x), beside(x1)))
    cot3 = beside(cot1)
    cots = (cot, cot1, cot2, cot3)

    halos, front, t, u = [], [], [], []
    for s in range(NSEG):
        if s > 0:
            state = after(state, t[s - 1])
        halos.append(halo)
        out = mixer_forward(idx, xs[s], gain1, *mixw, state, halo)
        state, halo = out[10], out[11]
        front.append(out)
        send = after(out[8], xs[s + 1][1]) if s + 1 < NSEG else out[8]
        t.append(plus(out[9], beside(send)))
        u.append(across(t[s]))
    resid, low, ffn, t2, u2 = [], [], [], [], []
    for s in range(NSEG):
        last = front[NSEG - 1][10] if s < NSEG - 1 else ffn[s - 1][10]
        r, lo = resid_step(s * rows, idx, t[s], after(u[s], last), arrived, xs[s][1], gain2)
        resid.append(r)
        low.append(lo)
        core = beside(lo)
        if s < NSEG - 1:
            lo = after(lo, t[s + 1])
        else:
            lo = after(lo, t2[s - 1])
        fold = None if s == 0 else ffn[s - 1][7:9]
        f = ffn_both(s * rows, idx, lo, core, cots, gain2, ffn_gate.T, ffn_up.T, ffn_down.T, fold)
        ffn.append(f)
        got = beside(f[5] if s == 0 else after(f[5], u2[s - 1]))
        t2.append(plus(f[6], got))
        u2.append(across(t2[s]))
    hold = t2[NSEG - 1]
    grads = ffn_grads(after(idx, hold), ffn)
    shares = [Share(grads[0], grads[1], dp, FIRST), Share(grads[2], grads[3], dp, THIRD)]
    dr, da = [], []
    for s in range(NSEG):
        wait = (hold,) if s == 0 else (grads[0], da[s - 1][0])
        d, a = dresid_step(
            s * rows, width, idx, t2[s], after(u2[s], *wait), resid[s], cot, cot1, gain2, ffn[s][10]
        )
        dr.append(d)
        da.append((a, beside(a)))
        if s == 0:
            for sh in shares:
                sh.start()

    back = [None] * NSEG
    ds = jnp.zeros((heads, dk, dv), F32)
    dhalo = jnp.zeros((8, cw), F32)
    got1, away1, bk1 = [None] * NSEG, [None] * NSEG, [None] * NSEG
    fsend, fkeep = ffn[NSEG - 1][7:9]
    fgot = beside(after(fsend, da[NSEG - 1][1]))
    for s in reversed(range(NSEG)):
        o = front[s]
        mine = da[s][0]
        if s < NSEG - 1:
            mine = after(mine, away1[s + 1], outg[0], faway, *[sh.send for sh in shares])
        b = mixer_backward(
            idx, (mine, da[s][1]), o[0], o[1], o[2], o[3], o[4], o[5], o[6], o[13], o[14], *mixw, halos[s], ds, dhalo
        )
        ds, dhalo = b[5], b[6]
        back[s] = b
        if s == NSEG - 1:
            got1[s] = beside(b[2])
            away1[s] = plus(b[3][0], got1[s][0])
        else:
            flown = (bk1[s + 1], fback, *[sh.terms[-1] for sh in shares + outs])
            got1[s] = beside(after(b[2], *flown))
            dx = dinput_step(
                (s + 1) * rows, width, idx, back[s + 1][3], got1[s + 1], after(bk1[s + 1], ds), dr[s + 1],
                arrived, gain1, front[s + 1][12],
            )
            away1[s] = plus(b[3][0], after(got1[s], dx)[0])
        bk1[s] = across(away1[s])
        if s == NSEG - 1:
            for sh in shares:
                sh.middle(ds)
                sh.start()
            outg = out_grads(
                after(idx, away1[s]), NSEG, heads, out_weight, hgain,
                [v for q in range(NSEG) for v in (*da[q], front[q][7], front[q][0], front[q][1], front[q][4])],
            )
            outs = [Share(outg[0], outg[1], dp, FIRST)]
            for sh in outs:
                sh.start()
            faway = plus(fkeep[0], fgot[0])
            fback = across(after(faway, away1[s]))
    small = after(sum(b[4] for b in back), *flown)
    gsum = sum(f[9] for f in ffn)
    small = jnp.concatenate([small, gsum, jnp.zeros((7, width), F32)], 0)
    small = small + swap(small, "dp", dp, 1)

    lead = []
    for s in range(NSEG):
        o, b = front[s], back[s]
        lead += [o[0], b[0], b[1]]
    plan = ((FIRST, ((0, 1, 0, 2 * qd), (0, 2, 0, CH))), (SECOND, ((0, 1, 2 * qd, vd),)))
    wide = row_grads(after(idx, away1[0]), NSEG, plan, lead)
    tails = [Share(wide[0], wide[1], dp, FIRST), Share(wide[2], wide[3], dp, SECOND)]
    for sh in tails:
        sh.start()
    second = swap(after(small, wide[0]), "dp", dp, 2)
    keep = after(back[0][3], wide[0])
    dx = dinput_step(0, width, idx, keep, got1[0], bk1[0], dr[0], arrived, gain1, front[0][12], dx)
    returned = lax.all_to_all(
        dx.reshape(dp, length // dp, quarter), "dp", split_axis=0, concat_axis=0, tiled=True
    )
    for sh in shares + outs:
        sh.middle(dx)
        sh.start()
    mask = (jnp.arange(length) < own_length).astype(F32)[:, None]
    rest = fkeep[1].astype(F32) + after(fgot, dx)[1].astype(F32) + fback.astype(F32)
    mixed = (jnp.concatenate([r[0] for r in resid], 0) + mask * rest).astype(BF)
    for sh in tails:
        sh.middle(dx)
        sh.start()
    small = small + after(second, *[sh.send for sh in tails])
    third = swap(small, "dp", dp, 4)
    for sh in outs:
        sh.middle(*[t.send for t in tails])
        sh.start()
    lower, upper = [sh.finish(1, *[t.send for t in tails]) for sh in shares]
    for sh in tails:
        sh.middle()
        sh.start()
    small = small + after(third, *[sh.send for sh in tails])
    bit = 8
    while bit < dp:
        small = small + swap(small, "dp", dp, bit)
        bit *= 2
    summed = total_tensor(jnp.concatenate([small[4:5], small[7:9]], 0))
    source_grad = jnp.zeros_like(returned).at[dealing].set(after(returned, tails[0].send))
    outw = outs[0].finish(0)
    outw, gatew = outw[:, :vd], outw[:, vd:]
    wide1, wide2 = [sh.finish(0) for sh in tails]
    shared = small[0:7]
    part = width // dp
    start = lax.axis_index("dp") * part
    norm_gain_grad = own(summed[1] / norm_gain, start, part)
    ffn_gain_grad = own(summed[2] / ffn_gain, start, part)
    return (
        mixed[None],
        source_grad,
        norm_gain_grad,
        wide1[:, 0:qd],
        wide1[:, qd : 2 * qd],
        wide2,
        shared[0:4, 0:qd],
        shared[0:4, qd : 2 * qd],
        shared[0:4, 2 * qd : cw],
        wide1[:, 2 * qd : 2 * qd + heads],
        wide1[:, 2 * qd + heads : 2 * qd + 2 * heads],
        shared[5, heads : 2 * heads],
        shared[6, heads : 2 * heads],
        gatew,
        summed[0, 0:dv],
        outw,
        ffn_gain_grad,
        jnp.concatenate([lower[units:], upper[: units // 2]], 0).T,
        upper[units // 2 :].T,
        lower[:units].T,
    )


def solution(mesh):
    in_specs = (
        P(None, "dp", "tensor"),
        P("dp", None, "tensor"),
        P(),
        P(),
        P(),
        P(None, "tensor"),
        P(None, "tensor"),
        P(None, "tensor"),
        P(None, "tensor"),
        P(None, "tensor"),
        P(None, "tensor"),
        P(None, "tensor"),
        P(None, "tensor"),
        P("tensor"),
        P("tensor"),
        P(None, "tensor"),
        P(),
        P(None, "tensor"),
        P(),
        P(None, "tensor"),
        P(None, "tensor"),
        P(None, "tensor"),
    )
    out_specs = (
        P("dp", None, "tensor"),
        P(None, "dp", "tensor"),
        P("dp"),
        P("dp", "tensor"),
        P("dp", "tensor"),
        P("dp", "tensor"),
        P(None, "tensor"),
        P(None, "tensor"),
        P(None, "tensor"),
        P("dp", "tensor"),
        P("dp", "tensor"),
        P("tensor"),
        P("tensor"),
        P("dp", "tensor"),
        P(),
        P("dp", "tensor"),
        P("dp"),
        P("dp", "tensor"),
        P("dp", "tensor"),
        P("dp", "tensor"),
    )
    return jax.shard_map(
        per_device, mesh=mesh, in_specs=in_specs, out_specs=out_specs, check_vma=False
    )
```

```python
import functools
import jax
import jax.numpy as jnp
from jax import lax
from jax.sharding import PartitionSpec as P
from jax.experimental import pallas as pl
from jax.experimental.pallas import tpu as pltpu

F32 = jnp.float32
BF = jnp.bfloat16
NN = ((1,), (0,))
NT = ((1,), (1,))
TN = ((0,), (0,))
CH = 128
EPS = 1e-6
TAIL = 16
VMEM_LIMIT = 56 * 1024 * 1024


def mm(a, b, dims=NN):
    return lax.dot_general(a.astype(BF), b.astype(BF), (dims, ((), ())), preferred_element_type=F32)


def mm3(a, b, dims=NN):
    ah, bh = a.astype(BF), b.astype(BF)
    al, bl = a - ah.astype(F32), b - bh.astype(F32)
    rows = a.shape[0]
    both = mm(jnp.concatenate([ah, al.astype(BF)], 0), bh, dims)
    return both[0:rows] + (both[rows:] + mm(ah, bl, dims))


def mm_exact(a, b):
    return lax.dot_general(
        a, b, (NN, ((), ())), precision=lax.Precision.HIGHEST, preferred_element_type=F32
    )


def sigm(u):
    return 0.5 * jnp.tanh(0.5 * u) + 0.5


def grid_iotas():
    return (
        lax.broadcasted_iota(jnp.int32, (CH, CH), 0),
        lax.broadcasted_iota(jnp.int32, (CH, CH), 1),
    )


def conv_rows(buf, conv, start, cols):
    acc = None
    for i in range(4):
        term = conv[i : i + 1, cols] * buf[start - 3 + i : start - 3 + i + CH, cols]
        acc = term if acc is None else acc + term
    return acc


def soft_plus(u):
    return jnp.maximum(u, 0.0) + jnp.log1p(jnp.exp(-jnp.abs(u)))


def fwd_kernel(
    heads, dk, dv, width,
    idx, x0, x1, x2, x3, gain, wq, wk, wv, wg, wba, conv, dec, hgain, wo, s_in, halo_in,
    h_out, proj_out, ba_out, u_out, o_out, st_out, t_out, z_out, send_out, keep_out, s_fin, halo_fin, scale_out, a_out, p_out, gbuf,
    cbuf, qs, ks, vs, abuf, wbuf, vbuf, nbuf, fbuf, rowb, colb,
):
    rows = x0.shape[0]
    quarter = x0.shape[1]
    qd, vd = heads * dk, heads * dv
    chunks = rows // CH
    cbuf[0:8, :] = halo_in[...]
    xs = (x0, x1, x2, x3)
    tile = 128
    for r in range(rows // tile):
        rr = slice(r * tile, r * tile + tile)
        parts = [x[rr, :].astype(F32) for x in xs]
        total = jnp.sum(sum(p * p for p in parts), -1, keepdims=True)
        scale = lax.rsqrt(total * (1.0 / width) + EPS)
        scale_out[:, rr] = jnp.transpose(jnp.broadcast_to(scale, (tile, CH)))[0:8, :]
        for n in range(4):
            cols = pl.ds(pl.multiple_of(idx[n] * quarter, quarter), quarter)
            h_out[rr, cols] = (parts[n] * scale * gain[idx[n]]).astype(BF)
    for w, lo, n in ((wq, 0, qd), (wk, qd, qd), (wv, 2 * qd, vd)):
        part = mm(h_out[...], w[...])
        cbuf[8 : 8 + rows, lo : lo + n] = part
        proj_out[:, lo : lo + n] = part
    part = mm(h_out[...], wg[...])
    gbuf[...] = part
    ba_out[...] = mm(h_out[...], wba[...])
    halo_fin[...] = cbuf[rows : rows + 8, :]
    ii, jj = grid_iotas()
    lower = jnp.where(ii >= jj, 1.0, 0.0).astype(F32)
    lane = lax.broadcasted_iota(jnp.int32, (1, CH), 1)
    for c in range(chunks):
        rr = slice(c * CH, c * CH + CH)
        raw = ba_out[rr, :]
        beta = sigm(raw)
        rate = dec[0:1, :] * soft_plus(raw + dec[1:2, :])
        rate = jnp.where((lane >= heads) & (lane < 2 * heads), rate, 0.0)
        run = mm_exact(lower, rate)
        colb[c] = jnp.where(lane < heads, beta, run)
        rowb[c] = jnp.transpose(run)
        for h in range(heads):
            for which, dst, mul in ((0, qs, dk ** -0.5), (qd, ks, 1.0)):
                cols = slice(which + h * dk, which + h * dk + dk)
                u = conv_rows(cbuf, conv, 8 + c * CH, cols)
                u = u * sigm(u)
                norm = lax.rsqrt(jnp.sum(u * u, -1, keepdims=True) + EPS) * mul
                dst[rr, h * dk : h * dk + dk] = u * norm
            cols = slice(2 * qd + h * dv, 2 * qd + h * dv + dv)
            u = conv_rows(cbuf, conv, 8 + c * CH, cols)
            vs[rr, h * dv : h * dv + dv] = u * sigm(u)
    units = [(c, h) for c in range(chunks) for h in range(heads)]
    xr = ii ^ jj
    eye = jnp.where(ii == jj, 1.0, 0.0).astype(F32)
    for n, (c, h) in enumerate(units):
        rr = slice(c * CH, c * CH + CH)
        k = ks[rr, h * dk : h * dk + dk]
        bc = colb[c, :, heads + h : heads + h + 1]
        br = rowb[c, heads + h : heads + h + 1, :]
        bt = colb[c, :, h : h + 1]
        a = jnp.where(ii > jj, bt * mm(k, k, NT) * jnp.exp(bc - br), 0.0)
        abuf[n] = a.astype(BF)
        a_out[n] = a
        t_out[n] = (eye - jnp.where(xr == 1, a, 0.0)).astype(BF)
    step = 2
    while step < CH:
        for n in range(len(units)):
            t = t_out[n]
            part = jnp.where((xr >= step) & (xr < 2 * step), abuf[n].astype(F32), 0.0)
            t_out[n] = (t.astype(F32) - mm(mm(t, part), t)).astype(BF)
        step *= 2
    for n, (c, h) in enumerate(units):
        rr = slice(c * CH, c * CH + CH)
        k = ks[rr, h * dk : h * dk + dk]
        v = vs[rr, h * dv : h * dv + dv]
        bc = colb[c, :, heads + h : heads + h + 1]
        bt = colb[c, :, h : h + 1]
        last = colb[c, CH - 1 : CH, heads + h : heads + h + 1]
        t = jnp.where(ii > jj, t_out[n].astype(F32), 0.0).astype(BF)
        t_out[n] = t
        bk, bv = (bt * jnp.exp(bc)) * k, bt * v
        w = (bk + mm(t, bk)).astype(BF)
        vv = bv + mm(t, bv)
        wbuf[n] = w
        vbuf[n] = vv
        kt = (k * jnp.exp(last - bc)).astype(BF)
        nbuf[n] = mm(kt, w, TN).astype(BF)
        fbuf[n] = mm(kt, vv, TN)
    for h in range(heads):
        s_fin[h] = s_in[h]
    for c in range(chunks):
        rr = slice(c * CH, c * CH + CH)
        for h in range(heads):
            n = c * heads + h
            s = s_fin[h]
            sb = s.astype(BF)
            st_out[n] = sb
            last = colb[c, CH - 1 : CH, heads + h : heads + h + 1]
            s_fin[h] = jnp.exp(last) * s + fbuf[n] - mm(nbuf[n], sb)
        for h in range(heads):
            n = c * heads + h
            q = qs[rr, h * dk : h * dk + dk]
            k = ks[rr, h * dk : h * dk + dk]
            bc = colb[c, :, heads + h : heads + h + 1]
            br = rowb[c, heads + h : heads + h + 1, :]
            p = jnp.where(ii >= jj, mm3(q, k, NT) * jnp.exp(bc - br), 0.0)
            p_out[n] = p
            s = st_out[n]
            both = mm(jnp.concatenate([wbuf[n], (q * jnp.exp(bc)).astype(BF)], 0), s)
            u = vbuf[n] - both[0:CH]
            u_out[rr, h * dv : h * dv + dv] = u
            o = both[CH:] + mm3(p, u)
            o_out[rr, h * dv : h * dv + dv] = o
            scale = lax.rsqrt(jnp.mean(o * o, -1, keepdims=True) + EPS)
            g = gbuf[rr, h * dv : h * dv + dv]
            z = o * scale * hgain[...] * (g * sigm(g))
            z_out[rr, h * dv : h * dv + dv] = z.astype(BF)
    out_blocks(idx, z_out, wo, send_out, keep_out, rows, quarter)


def out_blocks(idx, src, wo, send_out, keep_out, rows, quarter):
    for dst, pos, which in ((send_out, 0, 3), (send_out, 1, 2), (keep_out, 0, 1), (keep_out, 1, 0)):
        blk = pl.ds(pl.multiple_of(idx[which] * quarter, quarter), quarter)
        dst[pos] = mm(src[...], wo[blk, :], NT).astype(BF)


def mixer_forward(idx, xs, gain, wq, wk, wv, wg, wba, conv, dec, hgain, wo, s_in, halo_in):
    rows, quarter = xs[0].shape
    width = wq.shape[0]
    heads, dk, dv = s_in.shape
    qd, vd = heads * dk, heads * dv
    units = rows // CH * heads
    chunks = rows // CH
    outs = [
        ((rows, width), BF), ((rows, 2 * qd + vd), F32), ((rows, CH), F32),
        ((rows, vd), F32), ((rows, vd), F32), ((units, dk, dv), BF), ((units, CH, CH), BF),
        ((rows, vd), BF), ((2, rows, quarter), BF), ((2, rows, quarter), BF),
        ((heads, dk, dv), F32), ((8, 2 * qd + vd), F32), ((8, rows), F32),
        ((units, CH, CH), F32), ((units, CH, CH), F32), ((rows, vd), F32),
    ]
    smem = pl.BlockSpec(memory_space=pltpu.SMEM)
    vm = pl.BlockSpec(memory_space=pltpu.VMEM)
    return pl.pallas_call(
        functools.partial(fwd_kernel, heads, dk, dv, width),
        out_shape=[jax.ShapeDtypeStruct(s, d) for s, d in outs],
        in_specs=[smem] + [vm] * 16,
        out_specs=[vm] * len(outs),
        scratch_shapes=[
            pltpu.VMEM((rows + 8, 2 * qd + vd), F32),
            pltpu.VMEM((rows, qd), F32), pltpu.VMEM((rows, qd), F32), pltpu.VMEM((rows, vd), F32),
            pltpu.VMEM((units, CH, CH), BF), pltpu.VMEM((units, CH, dk), BF),
            pltpu.VMEM((units, CH, dv), F32), pltpu.VMEM((units, dk, dk), BF),
            pltpu.VMEM((units, dk, dv), F32), pltpu.VMEM((chunks, CH, CH), F32),
            pltpu.VMEM((chunks, CH, CH), F32),
        ],
        compiler_params=pltpu.CompilerParams(vmem_limit_bytes=VMEM_LIMIT),
        cost_estimate=pl.CostEstimate(flops=rows * 32000000, bytes_accessed=12 * rows * 1024, transcendentals=rows * 4096),
        name="mix_fwd",
    )(idx, *xs, gain, wq, wk, wv, wg, wba, conv, dec, hgain, wo, s_in, halo_in)


def bwd_kernel(
    heads, dk, dv, width,
    idx, dob, dgate, h_in, proj, ba, u_in, st_in, t_in, a_in, p_in, wq, wk, wv, wg, wba, conv, dec,
    halo_in, ds_in, dhalo_in,
    dproj_out, dba_out, send_out, keep_out, small_out, ds_fin, dhalo_fin,
    pbuf, cbuf, sgbuf, dcbuf, qs, ks, vs, r0b, ktb, d0b, mb, dsb, rowb, colb,
):
    rows = dob.shape[0]
    quarter = send_out.shape[2]
    qd, vd = heads * dk, heads * dv
    cw = 2 * qd + vd
    chunks = rows // CH
    units = [(c, h) for c in range(chunks) for h in range(heads)]
    ii, jj = grid_iotas()
    lower = jnp.where(ii >= jj, 1.0, 0.0).astype(F32)
    strict = jnp.where(ii > jj, 1.0, 0.0).astype(F32)
    upper = jnp.where(ii <= jj, 1.0, 0.0).astype(F32)
    lane = lax.broadcasted_iota(jnp.int32, (1, CH), 1)
    pbuf[0:8, :] = halo_in[...]
    pbuf[8 : 8 + rows, :] = proj[...]
    dcbuf[rows : rows + 8, :] = dhalo_in[...]
    for c in range(chunks):
        rr = slice(c * CH, c * CH + CH)
        raw = ba[rr, :]
        rate = dec[0:1, :] * soft_plus(raw + dec[1:2, :])
        rate = jnp.where((lane >= heads) & (lane < 2 * heads), rate, 0.0)
        run = mm_exact(lower, rate)
        act = jnp.where(lane < heads, sigm(raw), run)
        colb[c] = act
        rowb[c] = jnp.transpose(act)
        for h in range(heads):
            for which, dst, mul in ((0, qs, dk ** -0.5), (qd, ks, 1.0)):
                cols = slice(which + h * dk, which + h * dk + dk)
                u = conv_rows(pbuf, conv, 8 + c * CH, cols)
                sg = sigm(u)
                cbuf[rr, cols] = u
                sgbuf[rr, cols] = sg
                u = u * sg
                norm = lax.rsqrt(jnp.sum(u * u, -1, keepdims=True) + EPS) * mul
                dst[rr, h * dk : h * dk + dk] = u * norm
            cols = slice(2 * qd + h * dv, 2 * qd + h * dv + dv)
            u = conv_rows(pbuf, conv, 8 + c * CH, cols)
            sg = sigm(u)
            cbuf[rr, cols] = u
            sgbuf[rr, cols] = sg
            vs[rr, h * dv : h * dv + dv] = u * sg
    small_out[...] = jnp.zeros_like(small_out)
    for n, (c, h) in enumerate(units):
        rr = slice(c * CH, c * CH + CH)
        q = qs[rr, h * dk : h * dk + dk]
        k = ks[rr, h * dk : h * dk + dk]
        do = dob[rr, h * dv : h * dv + dv]
        bc = colb[c, :, heads + h : heads + h + 1]
        br = rowb[c, heads + h : heads + h + 1, :]
        bt = colb[c, :, h : h + 1]
        last = colb[c, CH - 1 : CH, heads + h : heads + h + 1]
        grow = jnp.exp(bc)
        t = t_in[n]
        pd = mm3(jnp.transpose(p_in[n]), do)
        r0 = pd + mm(t, pd, TN)
        kt = k * jnp.exp(last - bc)
        kt = (kt + mm(t, kt, TN)).astype(BF)
        bgk = (bt * grow * k).astype(BF)
        r0b[n] = r0
        ktb[n] = kt
        d0b[n] = mm(grow * q, do, TN) - mm(bgk, r0, TN)
        mb[n] = mm(bgk, kt, TN).astype(BF)
    for h in range(heads):
        ds_fin[h] = ds_in[h]
    for c in reversed(range(chunks)):
        for h in range(heads):
            n = c * heads + h
            s = ds_fin[h]
            sb = s.astype(BF)
            dsb[n] = s
            last = colb[c, CH - 1 : CH, heads + h : heads + h + 1]
            ds_fin[h] = jnp.exp(last) * s + d0b[n] - mm(mb[n], sb)
    for c in range(chunks):
        rr = slice(c * CH, c * CH + CH)
        first = jnp.zeros((CH, CH), F32)
        second = jnp.zeros((CH, CH), F32)
        gextra = jnp.zeros((CH, CH), F32)
        for h in range(heads):
            n = c * heads + h
            q = qs[rr, h * dk : h * dk + dk]
            k = ks[rr, h * dk : h * dk + dk]
            v = vs[rr, h * dv : h * dv + dv]
            do = dob[rr, h * dv : h * dv + dv]
            u = u_in[rr, h * dv : h * dv + dv]
            s0 = st_in[n]
            ds = dsb[n]
            dsl = ds.astype(BF)
            qf, kf = q, k
            bc = colb[c, :, heads + h : heads + h + 1]
            br = rowb[c, heads + h : heads + h + 1, :]
            bt = colb[c, :, h : h + 1]
            btr = rowb[c, h : h + 1, :]
            last = colb[c, CH - 1 : CH, heads + h : heads + h + 1]
            grow = jnp.exp(bc)
            tail = jnp.exp(last - bc)
            r = r0b[n] + mm(ktb[n], dsl)
            dec_d = jnp.exp(bc - br)
            uh = u.astype(BF)
            ul = (u - uh.astype(F32)).astype(BF)
            pairh = jnp.concatenate([r, do], 0)
            pairl = pairh - pairh.astype(BF).astype(F32)
            raw4 = mm(jnp.concatenate([pairh, pairl], 0), uh, NT)
            raw = raw4[0 : 2 * CH] + (raw4[2 * CH :] + mm(pairh, ul, NT))
            da = jnp.where(ii > jj, -raw[0:CH] * dec_d, 0.0)
            dp = jnp.where(ii >= jj, raw[CH:] * dec_d, 0.0)
            inter = raw[CH:] * p_in[n] - raw[0:CH] * a_in[n]
            ih = inter.astype(BF)
            cums = mm(upper, jnp.concatenate([ih, (inter - ih.astype(F32)).astype(BF)], 1))
            cum = cums[:, 0:CH] + cums[:, CH:]
            states = mm(pairh, s0, NT)
            rs = grow * states[0:CH]
            dq1 = grow * states[CH:]
            local = mm(jnp.concatenate([dp, da], 0), k)
            dq = dq1 + local[0:CH]
            x = local[CH:] - rs
            us = tail * mm(uh, dsl, NT)
            dkw = mm(jnp.concatenate([dp, bt * da], 0), jnp.concatenate([q, k], 0), TN) + us
            dk_all = bt * x + dkw
            dbeta = jnp.sum(kf * x, -1, keepdims=True) + jnp.sum(r * v, -1, keepdims=True)
            ci = jnp.sum(qf * dq1 - bt * (kf * rs), -1, keepdims=True)
            wj = jnp.sum(kf * us, -1, keepdims=True)
            base = jnp.sum(jnp.where(jj < ii, cum, 0.0), -1, keepdims=True)
            whole = jnp.exp(last) * jnp.sum(
                jnp.sum(s0.astype(F32) * ds, -1, keepdims=True), 0, keepdims=True
            )
            first = first + jnp.where(lane == heads + h, ci, 0.0)
            second = second + jnp.where(lane == heads + h, wj, 0.0)
            gextra = gextra + jnp.where(lane == heads + h, base + whole, 0.0)
            gextra = gextra + jnp.where(lane == h, dbeta, 0.0)
            for dst, grad, mul in ((0, dq, dk ** -0.5), (qd, dk_all, 1.0)):
                cols = slice(dst + h * dk, dst + h * dk + dk)
                cv = cbuf[rr, cols]
                sg = sgbuf[rr, cols]
                y = cv * sg
                norm = lax.rsqrt(jnp.sum(y * y, -1, keepdims=True) + EPS)
                yn = y * norm
                dy = (norm * mul) * (grad - yn * jnp.sum(grad * yn, -1, keepdims=True))
                dcbuf[rr, cols] = dy * (sg * (1.0 + cv * (1.0 - sg)))
            cols = slice(2 * qd + h * dv, 2 * qd + h * dv + dv)
            cv = cbuf[rr, cols]
            sg = sgbuf[rr, cols]
            dcbuf[rr, cols] = bt * r * (sg * (1.0 + cv * (1.0 - sg)))
        dg = mm_exact(upper, first) + mm_exact(strict, second) + gextra
        raw = ba[rr, :]
        act = raw + dec[1:2, :]
        sp = soft_plus(act)
        sb = sigm(raw)
        dfac = dec[0:1, :]
        isb = lane < heads
        isd = (lane >= heads) & (lane < 2 * heads)
        draw = jnp.where(isb, dg * sb * (1.0 - sb), jnp.where(isd, dg * dfac * sigm(act), 0.0))
        dba_out[rr, :] = draw.astype(BF)
        small_out[5:6, 0:CH] += jnp.sum(jnp.where(isd, dg * dfac * sp, 0.0), 0, keepdims=True)
        small_out[6:7, 0:CH] += jnp.sum(jnp.where(isd, draw, 0.0), 0, keepdims=True)
    dhalo_fin[...] = dcbuf[0:8, :]
    for c in range(chunks):
        rr = slice(c * CH, c * CH + CH)
        for lo in range(0, cw, 256):
            cols = slice(lo, lo + 256)
            acc = None
            dc = dcbuf[rr, cols]
            for i in range(4):
                sh = slice(c * CH + 3 - i, c * CH + 3 - i + CH)
                term = conv[i : i + 1, cols] * dcbuf[sh, cols]
                acc = term if acc is None else acc + term
                src = pbuf[c * CH + 5 + i : c * CH + 5 + i + CH, cols]
                small_out[i : i + 1, cols] += jnp.sum(dc * src, 0, keepdims=True)
            dproj_out[rr, cols] = acc.astype(BF)
    rowsum = jnp.zeros((8, rows), F32)
    ones = jnp.ones((8, quarter), BF)
    for dst, pos, which in ((send_out, 0, 3), (send_out, 1, 2), (keep_out, 0, 1), (keep_out, 1, 0)):
        blk = pl.ds(pl.multiple_of(idx[which] * quarter, quarter), quarter)
        out = (
            mm(dproj_out[:, 0:qd], wq[blk, :], NT)
            + mm(dproj_out[:, qd : 2 * qd], wk[blk, :], NT)
            + mm(dproj_out[:, 2 * qd : cw], wv[blk, :], NT)
            + mm(dgate[...], wg[blk, :], NT)
            + mm(dba_out[...], wba[blk, :], NT)
        )
        dst[pos, 0:rows, :] = out.astype(BF)
        prod = out * h_in[:, blk].astype(F32)
        small_out[7:8, blk] = jnp.sum(prod, 0, keepdims=True)
        rowsum = rowsum + mm(ones, prod, NT)
    put_stats(send_out, keep_out, rowsum, rows, quarter)


def put_stats(send_out, keep_out, rowsum, rows, quarter):
    for dst in (send_out, keep_out):
        dst[:, rows : rows + TAIL, :] = jnp.zeros((2, TAIL, quarter), BF)
        for n in range(rows // quarter):
            dst[0, rows + n : rows + n + 1, :] = rowsum[0:1, n * quarter : n * quarter + quarter].astype(BF)


def mixer_backward(idx, quarter, do, dgate, h, proj, ba, u, st, t, a, p, wq, wk, wv, wg, wba, conv, dec, halo, ds, dhalo):
    rows = do.shape[0]
    width = wq.shape[0]
    heads, dk, dv = ds.shape
    qd, vd = heads * dk, heads * dv
    cw = 2 * qd + vd
    chunks = rows // CH
    units = chunks * heads
    outs = [
        ((rows, cw), BF), ((rows, CH), BF), ((2, rows + TAIL, quarter), BF), ((2, rows + TAIL, quarter), BF),
        ((8, width), F32), ((heads, dk, dv), F32), ((8, cw), F32),
    ]
    smem = pl.BlockSpec(memory_space=pltpu.SMEM)
    vm = pl.BlockSpec(memory_space=pltpu.VMEM)
    return pl.pallas_call(
        functools.partial(bwd_kernel, heads, dk, dv, width),
        out_shape=[jax.ShapeDtypeStruct(s, d) for s, d in outs],
        in_specs=[smem] + [vm] * 20,
        out_specs=[vm] * len(outs),
        scratch_shapes=[
            pltpu.VMEM((rows + 8, cw), F32), pltpu.VMEM((rows, cw), F32), pltpu.VMEM((rows, cw), F32), pltpu.VMEM((rows + 8, cw), F32),
            pltpu.VMEM((rows, qd), F32), pltpu.VMEM((rows, qd), F32), pltpu.VMEM((rows, vd), F32),
            pltpu.VMEM((units, CH, dv), F32), pltpu.VMEM((units, CH, CH), BF),
            pltpu.VMEM((units, dk, dv), F32), pltpu.VMEM((units, dk, dk), BF),
            pltpu.VMEM((units, dk, dv), F32), pltpu.VMEM((chunks, CH, CH), F32),
            pltpu.VMEM((chunks, CH, CH), F32),
        ],
        compiler_params=pltpu.CompilerParams(vmem_limit_bytes=VMEM_LIMIT),
        cost_estimate=pl.CostEstimate(flops=rows * 58000000, bytes_accessed=24 * rows * 1024, transcendentals=rows * 8192),
        name="mix_bwd",
    )(idx, do, dgate, h, proj, ba, u, st, t, a, p, wq, wk, wv, wg, wba, conv, dec, halo, ds, dhalo)


def out_bwd_kernel(heads, idx, mine, core, wo, hgain, g_in, o_in, da_out, do_out, dgate_out, head_out, dzb):
    rows, vd = o_in.shape
    quarter = mine.shape[2]
    dv = vd // heads
    for n, a in enumerate((mine.at[0], mine.at[1], core.at[0], core.at[1])):
        da_out[:, pl.ds(pl.multiple_of(idx[n] * quarter, quarter), quarter)] = a[...]
    dzb[...] = mm(da_out[...], wo[...])
    hg = hgain[...]
    ghead = jnp.zeros((1, dv), F32)
    for c in range(rows // CH):
        for h in range(heads):
            rr, hv = slice(c * CH, c * CH + CH), slice(h * dv, h * dv + dv)
            o = o_in[rr, hv]
            scale = lax.rsqrt(jnp.mean(o * o, -1, keepdims=True) + EPS)
            on = o * scale
            g = g_in[rr, hv]
            sg = sigm(g)
            dz = dzb[rr, hv]
            dgate_out[rr, hv] = (dz * on * hg * (sg * (1.0 + g * (1.0 - sg)))).astype(BF)
            dn = dz * (g * sg)
            ghead = ghead + jnp.sum(dn * on, 0, keepdims=True)
            e = dn * hg
            do_out[rr, hv] = scale * (e - on * jnp.mean(e * on, -1, keepdims=True))
    head_out[...] = jnp.broadcast_to(ghead, head_out.shape)


def out_backward(idx, heads, pair, wo, hgain, gate, o):
    rows, vd = o.shape
    smem = pl.BlockSpec(memory_space=pltpu.SMEM)
    vm = pl.BlockSpec(memory_space=pltpu.VMEM)
    outs = [((rows, wo.shape[0]), BF), ((rows, vd), F32), ((rows, vd), BF), ((8, vd // heads), F32)]
    return pl.pallas_call(
        functools.partial(out_bwd_kernel, heads),
        out_shape=[jax.ShapeDtypeStruct(s, d) for s, d in outs],
        in_specs=[smem] + [vm] * 6,
        out_specs=[vm] * 4,
        scratch_shapes=[pltpu.VMEM((rows, vd), F32)],
        compiler_params=pltpu.CompilerParams(vmem_limit_bytes=VMEM_LIMIT),
        cost_estimate=pl.CostEstimate(flops=rows * 8000000, bytes_accessed=14 * rows * 1024, transcendentals=rows * vd),
        name="out_bwd",
    )(idx, *pair, wo, hgain, gate, o)


def ffn_kernel(
    width, base, folded,
    idx, mine, core, c0, c1, c2, c3, gain, wg, wu, wd, *refs,
):
    (
        h_out, df_out, hid_out, dfg_out, dfu_out, send_out, keep_out, fsend_out, fkeep_out, gsum_out, scale_out,
        fgb, fub, dhb,
    ) = refs[2 * folded :]
    rows, quarter = mine.shape[1:]
    tile = CH
    rs, cs = (mine.at[0], mine.at[1], core.at[0], core.at[1]), (c0, c1, c2, c3)
    for r in range(rows // tile):
        rr = slice(r * tile, r * tile + tile)
        total = None
        for n in range(4):
            part = jnp.square(rs[n][rr, :].astype(F32) / gain[idx[n]])
            part = jnp.sum(part, -1, keepdims=True)
            total = part if total is None else total + part
        scale = lax.rsqrt(total * (1.0 / width) + EPS)
        scale_out[:, rr] = jnp.transpose(jnp.broadcast_to(scale, (tile, CH)))[0:8, :]
        place = base + r * tile + lax.broadcasted_iota(jnp.int32, (tile, 1), 0)
        valid = jnp.where(place < idx[4], 1.0, 0.0).astype(F32)
        for n in range(4):
            cols = pl.ds(pl.multiple_of(idx[n] * quarter, quarter), quarter)
            h_out[rr, cols] = rs[n][rr, :]
            df_out[rr, cols] = (cs[n][base + r * tile : base + r * tile + tile, :].astype(F32) * valid).astype(BF)
    fgb[...] = mm(h_out[...], wg[...], NT)
    fub[...] = mm(h_out[...], wu[...], NT)
    dhb[...] = mm(df_out[...], wd[...], NT)
    for r in range(rows // tile):
        rr = slice(r * tile, r * tile + tile)
        scale = jnp.transpose(jnp.broadcast_to(scale_out[0:1, rr], (CH, tile)))[:, 0:1]
        fg = scale * fgb[rr, :]
        fu = scale * fub[rr, :]
        ds = scale * dhb[rr, :]
        sg = sigm(fg)
        act = fg * sg
        hid_out[rr, :] = (act * fu).astype(BF)
        dfg_out[rr, :] = (ds * fu * sg * (1.0 + fg * (1.0 - sg))).astype(BF)
        dfu_out[rr, :] = (ds * act).astype(BF)
    rowsum = jnp.zeros((8, rows), F32)
    ones = jnp.ones((8, quarter), BF)
    order = ((0, 0, 3), (0, 1, 2), (1, 0, 1), (1, 1, 0))
    for kept, pos, which in order:
        blk = pl.ds(pl.multiple_of(idx[which] * quarter, quarter), quarter)
        out = mm(dfg_out[...], wg[:, blk]) + mm(dfu_out[...], wu[:, blk])
        (keep_out if kept else send_out)[pos, 0:rows, :] = out.astype(BF)
        prod = out * h_out[:, blk].astype(F32)
        gsum_out[0:1, blk] = jnp.sum(prod, 0, keepdims=True)
        rowsum = rowsum + mm(ones, prod, NT)
    put_stats(send_out, keep_out, rowsum, rows, quarter)
    for kept, pos, which in order:
        blk = pl.ds(pl.multiple_of(idx[which] * quarter, quarter), quarter)
        (fkeep_out if kept else fsend_out)[pos] = mm(hid_out[...], wd[:, blk]).astype(BF)


def ffn_both(base, idx, mine, core, cs, gain, wg, wu, wd, fold=None):
    rows, quarter = mine.shape[1:]
    units, width = wg.shape
    length = cs[0].shape[0]
    tall = ((2, rows + TAIL, quarter), BF)
    whole = ((2, length, quarter), BF)
    outs = [
        ((rows, width), BF), ((rows, width), BF), ((rows, units), BF), ((rows, units), BF), ((rows, units), BF),
        tall, tall, whole, whole, ((1, width), F32), ((8, rows), F32),
    ]
    smem = pl.BlockSpec(memory_space=pltpu.SMEM)
    vm = pl.BlockSpec(memory_space=pltpu.VMEM)
    part = base // rows
    slab = pl.BlockSpec((2, rows, quarter), lambda i: (0, part, 0), pipeline_mode=pl.Buffered(1))
    args = (idx, mine, core, *cs, gain, wg, wu, wd)
    specs = [smem] + [vm] * 10
    alias = {}
    if fold is not None:
        args += tuple(fold)
        specs += [pl.BlockSpec(memory_space=pl.ANY)] * 2
        alias = {len(args) - 2: 7, len(args) - 1: 8}
    return pl.pallas_call(
        functools.partial(ffn_kernel, width, base, fold is not None),
        grid=(1,),
        out_shape=[jax.ShapeDtypeStruct(s, d) for s, d in outs],
        in_specs=specs,
        out_specs=[vm] * 7 + [slab, slab, vm, vm],
        scratch_shapes=[pltpu.VMEM((rows, units), F32)] * 3,
        input_output_aliases=alias,
        compiler_params=pltpu.CompilerParams(vmem_limit_bytes=24 * 1024 * 1024),
        cost_estimate=pl.CostEstimate(flops=rows * 27000000, bytes_accessed=10 * rows * width, transcendentals=rows * units),
        name="ffn_both",
    )(*args)


def valid_rows(idx, start, count):
    place = start + lax.broadcasted_iota(jnp.int32, (count, 1), 0)
    return jnp.where(place < idx[4], 1.0, 0.0).astype(F32)


def columns(row):
    block = jnp.transpose(jnp.broadcast_to(row, (CH, CH)))
    return jnp.concatenate([block, block], 1)


def resid_kernel(base, idx, t, u, x0, x1, gain, r_out, low_out):
    m = valid_rows(idx, base, t.shape[1])
    for n, x in ((0, x0), (1, x1)):
        r = x[...].astype(F32) + m * (t[1 - n].astype(F32) + u[n].astype(F32))
        r_out[n] = r
        low_out[n] = (r * gain[idx[n]]).astype(BF)


def part_specs(base, rows, quarter):
    once = pl.Buffered(1)
    return (
        pl.BlockSpec((2, rows, quarter), lambda i: (0, 0, 0), pipeline_mode=once),
        pl.BlockSpec((rows, quarter), lambda i: (0, 0), pipeline_mode=once),
        pl.BlockSpec((rows, quarter), lambda i: (base // rows, 0), pipeline_mode=once),
        pl.BlockSpec(memory_space=pltpu.SMEM),
        pl.BlockSpec(memory_space=pltpu.VMEM),
    )


def resid_step(base, idx, t, u, x0, x1, gain):
    rows, quarter = t.shape[1:]
    pair, tile, whole, smem, vm = part_specs(base, rows, quarter)
    return pl.pallas_call(
        functools.partial(resid_kernel, base),
        grid=(1,),
        out_shape=[jax.ShapeDtypeStruct(t.shape, F32), jax.ShapeDtypeStruct(t.shape, BF)],
        in_specs=[smem, pair, pair, whole, tile, vm],
        out_specs=[pair, pair],
        compiler_params=pltpu.CompilerParams(vmem_limit_bytes=10 * 1024 * 1024),
        name="resid",
    )(idx, t, u, x0, x1, gain)


def stat_row(tail, c, quarter):
    line, at = c * CH // quarter, c * CH % quarter
    return tail[0, line : line + 1, at : at + CH].astype(F32)


def dresid_kernel(base, width, idx, t, tt, u, ut, r, c0, c1, gain, scale, dr_out, da_out):
    rows, quarter = r.shape[1:]
    for c in range(rows // CH):
        rr = slice(c * CH, c * CH + CH)
        m = valid_rows(idx, base + c * CH, CH)
        dot = stat_row(tt, c, quarter) + stat_row(ut, c, quarter)
        s = scale[0:1, rr]
        fac = columns(s * s * dot * (1.0 / width))
        for n, cot in ((0, c0), (1, c1)):
            d = t[1 - n, rr, :].astype(F32) + u[n, rr, :].astype(F32)
            dr = cot[rr, :].astype(F32) + d * gain[idx[n]] - r[n, rr, :] * fac
            if n == 0:
                dr_out[rr, :] = dr
            da_out[n, rr, :] = (m * dr).astype(BF)


def dresid_step(base, width, idx, t, u, r, c0, c1, gain, scale):
    rows, quarter = r.shape[1:]
    pair, tile, whole, smem, vm = part_specs(base, rows, quarter)
    foot = pl.BlockSpec((1, TAIL, quarter), lambda i: (0, rows // TAIL, 0))
    line = vm
    return pl.pallas_call(
        functools.partial(dresid_kernel, base, width),
        grid=(1,),
        out_shape=[jax.ShapeDtypeStruct(r.shape[1:], F32), jax.ShapeDtypeStruct(r.shape, BF)],
        in_specs=[smem, pair, foot, pair, foot, pair, whole, whole, vm, line],
        out_specs=[tile, pair],
        compiler_params=pltpu.CompilerParams(vmem_limit_bytes=10 * 1024 * 1024),
        name="dresid",
    )(idx, t, t, u, u, r, c0, c1, gain, scale)


def dinput_kernel(width, idx, keep, kt, got, gt, back, bt, dr, x0, gain, scale, *refs):
    rows, quarter = dr.shape
    g = gain[idx[0]]
    for c in range(rows // CH):
        rr = slice(c * CH, c * CH + CH)
        dot = stat_row(kt, c, quarter) + stat_row(gt, c, quarter) + stat_row(bt, c, quarter)
        s = scale[0:1, rr]
        d = keep[0, rr, :].astype(F32) + got[0, rr, :].astype(F32) + back[0, rr, :].astype(F32)
        fac = columns(s * s * dot * (1.0 / width))
        dx = dr[rr, :] + columns(s) * (d * g) - x0[rr, :].astype(F32) * fac
        refs[-1][rr, :] = dx.astype(BF)


def dinput_step(base, width, idx, keep, got, back, dr, x0, gain, scale, fold=None):
    rows, quarter = dr.shape
    pair, tile, whole, smem, vm = part_specs(base, rows, quarter)
    one = pl.BlockSpec((1, rows, quarter), lambda i: (1, 0, 0))
    zero = pl.BlockSpec((1, rows, quarter), lambda i: (0, 0, 0))
    foot = pl.BlockSpec((1, TAIL, quarter), lambda i: (0, rows // TAIL, 0))
    line = vm
    back = back[None]
    args = (idx, keep, keep, got, got, back, back, dr, x0, gain, scale)
    specs = [smem, one, foot, one, foot, zero, foot, tile, whole, vm, line]
    alias = {}
    if fold is not None:
        alias = {len(args): 0}
        args += (fold,)
        specs.append(pl.BlockSpec(memory_space=pl.ANY))
    return pl.pallas_call(
        functools.partial(dinput_kernel, width),
        grid=(1,),
        out_shape=jax.ShapeDtypeStruct(x0.shape, BF),
        in_specs=specs,
        out_specs=whole,
        input_output_aliases=alias,
        compiler_params=pltpu.CompilerParams(vmem_limit_bytes=8 * 1024 * 1024),
        name="dinput",
    )(*args)


def share_order(first):
    b0, b1, b2 = first
    kept = [((k >> 1) & 1) << b1 | (k & 1) << b2 for k in range(4)]
    return kept, [k | 1 << b0 for k in kept]


def ffn_grad_kernel(parts, units, at, *refs):
    ins, outs, buf = refs[: 5 * parts], refs[5 * parts : 5 * parts + 4], refs[-1]
    half = units // 2
    whole, low, high = (0, units), (0, half), (half, units)
    for left, right, places in (
        (2, 0, ((0, 0, whole),)), (3, 1, ((0, units, low), (1, 0, high))), (4, 1, ((1, half, whole),))
    ):
        total = None
        for s in range(parts):
            part = mm(ins[5 * s + left][...], ins[5 * s + right][...], TN)
            total = part if total is None else total + part
        buf[...] = total
        for group, first, (lo, hi) in places:
            kept, sent = share_order(FIRST if group == 0 else THIRD)
            for n in range(4):
                for dst, pos in ((outs[2 * group], sent), (outs[2 * group + 1], kept)):
                    blk = pl.ds(pl.multiple_of((at[5] ^ pos[n]) * 128, 128), 128)
                    dst[n, first : first + hi - lo, :] = buf[lo:hi, blk].astype(BF)


FIRST, SECOND, THIRD = (0, 1, 2), (1, 0, 2), (1, 2, 0)


def ffn_grads(at, ffn):
    rows, width = ffn[0][0].shape
    units = ffn[0][2].shape[1]
    args = [a for f in ffn for a in (f[1], f[0], f[2], f[3], f[4])]
    smem = pl.BlockSpec(memory_space=pltpu.SMEM)
    vm = pl.BlockSpec(memory_space=pltpu.VMEM)
    shapes = [(4, units + units // 2, 128)] * 4
    return pl.pallas_call(
        functools.partial(ffn_grad_kernel, len(ffn), units),
        out_shape=[jax.ShapeDtypeStruct(s, BF) for s in shapes],
        in_specs=[smem] + [vm] * len(args),
        out_specs=[vm] * 4,
        scratch_shapes=[pltpu.VMEM((units, width), F32)],
        compiler_params=pltpu.CompilerParams(vmem_limit_bytes=22 * 1024 * 1024),
        cost_estimate=pl.CostEstimate(flops=9 * 10 ** 9, bytes_accessed=10 ** 7, transcendentals=0),
        name="ffn_grads",
    )(at, *args)


def row_grad_kernel(parts, plan, at, *refs):
    count = len(refs) - 2 * len(plan) - len(plan)
    ins = refs[:count]
    outs = refs[count : count + 2 * len(plan)]
    bufs = refs[count + 2 * len(plan) :]
    each = count // parts
    for group, (order, pieces) in enumerate(plan):
        buf = bufs[group]
        col = 0
        for left, right, lo, n in pieces:
            total = None
            for s in range(parts):
                part = mm(ins[each * s + left][...], ins[each * s + right][:, lo : lo + n], TN)
                total = part if total is None else total + part
            buf[:, col : col + n] = total
            col += n
        kept, sent = share_order(order)
        for n in range(4):
            for dst, pos in ((outs[2 * group], sent), (outs[2 * group + 1], kept)):
                blk = pl.ds(pl.multiple_of((at[5] ^ pos[n]) * 128, 128), 128)
                dst[n] = buf[blk, :].astype(BF)


def out_grad_kernel(parts, at, *refs):
    ins, outs, (obuf, gbuf) = refs[: 4 * parts], refs[4 * parts : 4 * parts + 2], refs[4 * parts + 2 :]
    vd = obuf.shape[1]
    for buf, left, right in ((obuf, 0, 1), (gbuf, 2, 3)):
        total = None
        for s in range(parts):
            part = mm(ins[4 * s + left][...], ins[4 * s + right][...], TN)
            total = part if total is None else total + part
        buf[...] = total
    kept, sent = share_order(FIRST)
    for n in range(4):
        for dst, pos in ((outs[0], sent), (outs[1], kept)):
            blk = pl.ds(pl.multiple_of((at[5] ^ pos[n]) * 128, 128), 128)
            dst[n, :, 0:vd] = obuf[blk, :].astype(BF)
            dst[n, :, vd:] = gbuf[blk, :].astype(BF)


def out_grads(at, parts, args):
    width, n = args[0].shape[1], args[1].shape[1]
    smem = pl.BlockSpec(memory_space=pltpu.SMEM)
    vm = pl.BlockSpec(memory_space=pltpu.VMEM)
    return pl.pallas_call(
        functools.partial(out_grad_kernel, parts),
        out_shape=[jax.ShapeDtypeStruct((4, 128, 2 * n), BF)] * 2,
        in_specs=[smem] + [vm] * len(args),
        out_specs=[vm] * 2,
        scratch_shapes=[pltpu.VMEM((width, n), F32), pltpu.VMEM((width, n), F32)],
        compiler_params=pltpu.CompilerParams(vmem_limit_bytes=56 * 1024 * 1024),
        cost_estimate=pl.CostEstimate(flops=8 * 10 ** 9, bytes_accessed=10 ** 7, transcendentals=0),
        name="out_grads",
    )(at, *args)


def row_grads(at, parts, plan, args):
    width = args[0].shape[1]
    smem = pl.BlockSpec(memory_space=pltpu.SMEM)
    vm = pl.BlockSpec(memory_space=pltpu.VMEM)
    wides = [sum(p[3] for p in pieces) for _, pieces in plan]
    return pl.pallas_call(
        functools.partial(row_grad_kernel, parts, plan),
        out_shape=[jax.ShapeDtypeStruct((4, 128, w), BF) for w in wides for _ in range(2)],
        in_specs=[smem] + [vm] * len(args),
        out_specs=[vm] * (2 * len(plan)),
        scratch_shapes=[pltpu.VMEM((width, w), F32) for w in wides],
        compiler_params=pltpu.CompilerParams(vmem_limit_bytes=22 * 1024 * 1024),
        cost_estimate=pl.CostEstimate(flops=6 * 10 ** 9, bytes_accessed=10 ** 7, transcendentals=0),
        name="row_grads",
    )(at, *args)


def swap(array, axis, size, bit):
    return lax.ppermute(array, axis, [(i, i ^ bit) for i in range(size)])


def beside(array):
    return swap(array, "tensor", 4, 1)


def across(array):
    return swap(array, "tensor", 4, 2)


def after(array, *others):
    return lax.optimization_barrier((array,) + others)[0]


def plus(left, right):
    return (left.astype(F32) + right.astype(F32)).astype(BF)


def total_tensor(array):
    array = array + beside(array)
    return array + across(array)


class Share:
    def __init__(self, send, keep, size, order):
        low = size.bit_length() - 1 - 3
        self.size, self.low = size, low
        self.bits = [1 << (low + b) for b in order]
        self.send, self.terms = send, [keep]

    def start(self, *deps):
        send = after(self.send, *deps) if deps else self.send
        self.terms.append(swap(send, "dp", self.size, self.bits[len(self.terms) - 1]))

    def middle(self, *deps):
        half = 2 if len(self.terms) == 2 else 1
        got = after(self.terms[-1], *deps) if deps else self.terms[-1]
        self.terms[-1] = got
        total = sum(t[half : 2 * half].astype(F32) for t in self.terms)
        self.send = total.astype(BF)

    def finish(self, axis, *deps):
        got = after(self.terms[-1], *deps) if deps else self.terms[-1]
        total = sum(t[0].astype(F32) for t in self.terms[:-1]) + got[0].astype(F32)
        me = lax.axis_index("dp")
        for bit in range(self.low - 1, -1, -1):
            half = total.shape[axis] // 2
            mine = (me >> bit) & 1
            send = lax.dynamic_slice_in_dim(total, (1 - mine) * half, half, axis).astype(BF)
            keep = lax.dynamic_slice_in_dim(total, mine * half, half, axis)
            total = keep + swap(send, "dp", self.size, 1 << bit).astype(F32)
        return total


NSEG = 2


def per_device(
    source_rows, cotangent, lengths, dealing, norm_gain, query_weight, key_weight, value_weight,
    query_conv, key_conv, value_conv, beta_weight, decay_weight, decay_log, decay_bias, gate_weight,
    head_gain, out_weight, ffn_gain, ffn_gate, ffn_up, ffn_down,
):
    dp = lax.axis_size("dp")
    me = lax.axis_index("tensor").astype(jnp.int32)
    block = lax.axis_index("dp").astype(jnp.int32) // (dp // 8)
    length, quarter = cotangent.shape[1:]
    width = norm_gain.shape[0]
    heads, dv = decay_log.shape[0], head_gain.shape[0]
    dk = query_weight.shape[1] // heads
    qd, vd = heads * dk, heads * dv
    cw = 2 * qd + vd
    units = ffn_gate.shape[1]
    rows = length // NSEG
    pieces = [slice(s * rows, s * rows + rows) for s in range(NSEG)]
    own = lax.dynamic_slice_in_dim

    cot = cotangent[0]
    cot1 = across(cot)
    cot2 = beside(cot)
    ordered = source_rows.at[dealing].get(mode="promise_in_bounds", unique_indices=True)
    arrived = lax.all_to_all(ordered, "dp", split_axis=0, concat_axis=1, tiled=True)[0]
    own_length = lengths[dealing[lax.axis_index("dp")]]
    idx = jnp.stack([me, me ^ 2, me ^ 1, me ^ 3, own_length, block, block, block])

    wba = jnp.pad(jnp.concatenate([beta_weight, decay_weight], 1), ((0, 0), (0, CH - 2 * heads)))
    conv = jnp.concatenate([query_conv, key_conv, value_conv], 1)
    dec = jnp.stack([-jnp.exp(decay_log), decay_bias])
    dec = jnp.pad(dec, ((0, 6), (heads, CH - 2 * heads)))
    gain1 = norm_gain.reshape(4, 1, quarter)
    gain2 = ffn_gain.reshape(4, 1, quarter)
    hgain = head_gain[None]
    mixw = (query_weight, key_weight, value_weight, gate_weight, wba, conv, dec)

    state = jnp.zeros((heads, dk, dv), F32)
    halo = jnp.zeros((8, cw), F32)
    xs = []
    for s, p in enumerate(pieces):
        first = (cot1, wba, conv, dec, idx, state, halo)
        x = after(arrived[p], *(first if s == 0 else (xs[s - 1][1],)))
        x1 = across(x)
        xs.append((arrived[p], x1, beside(x), beside(x1)))
    cot3 = beside(cot1)
    cots = (cot, cot1, cot2, cot3)

    halos, front, t, u = [], [], [], []
    for s in range(NSEG):
        if s > 0:
            state = after(state, t[s - 1])
        halos.append(halo)
        out = mixer_forward(idx, xs[s], gain1, *mixw, hgain, out_weight, state, halo)
        state, halo = out[10], out[11]
        front.append(out)
        send = after(out[8], xs[s + 1][1]) if s + 1 < NSEG else out[8]
        t.append(plus(out[9], beside(send)))
        u.append(across(t[s]))
    resid, low, ffn, t2, u2 = [], [], [], [], []
    for s in range(NSEG):
        last = front[NSEG - 1][10] if s < NSEG - 1 else ffn[s - 1][10]
        r, lo = resid_step(s * rows, idx, t[s], after(u[s], last), arrived, xs[s][1], gain2)
        resid.append(r)
        low.append(lo)
        core = beside(lo)
        if s < NSEG - 1:
            lo = after(lo, t[s + 1])
        else:
            lo = after(lo, t2[s - 1])
        fold = None if s == 0 else ffn[s - 1][7:9]
        f = ffn_both(s * rows, idx, lo, core, cots, gain2, ffn_gate.T, ffn_up.T, ffn_down.T, fold)
        ffn.append(f)
        got = beside(f[5] if s == 0 else after(f[5], u2[s - 1]))
        t2.append(plus(f[6], got))
        u2.append(across(t2[s]))
    hold = t2[NSEG - 1]
    grads = ffn_grads(after(idx, hold), ffn)
    shares = [Share(grads[0], grads[1], dp, FIRST), Share(grads[2], grads[3], dp, THIRD)]
    dr, da, pre = [], [], []
    for s in range(NSEG):
        wait = (hold,) if s == 0 else (grads[0], pre[s - 1][3])
        d, a = dresid_step(
            s * rows, width, idx, t2[s], after(u2[s], *wait), resid[s], cot, cot1, gain2, ffn[s][10]
        )
        dr.append(d)
        da.append((a, beside(a)))
        pre.append(out_backward(idx, heads, da[s], out_weight, hgain, front[s][15], front[s][4]))
        if s == 0:
            for sh in shares:
                sh.start()

    back = [None] * NSEG
    ds = jnp.zeros((heads, dk, dv), F32)
    dhalo = jnp.zeros((8, cw), F32)
    got1, away1, bk1 = [None] * NSEG, [None] * NSEG, [None] * NSEG
    fsend, fkeep = ffn[NSEG - 1][7:9]
    fgot = beside(after(fsend, da[NSEG - 1][1]))
    for s in reversed(range(NSEG)):
        o = front[s]
        order = idx
        if s < NSEG - 1:
            order = after(idx, away1[s + 1], outg[0], faway, *[sh.send for sh in shares])
        b = mixer_backward(
            order, quarter, pre[s][1], pre[s][2], o[0], o[1], o[2], o[3], o[5], o[6], o[13], o[14],
            *mixw, halos[s], ds, dhalo,
        )
        ds, dhalo = b[5], b[6]
        back[s] = b
        if s == NSEG - 1:
            got1[s] = beside(b[2])
            away1[s] = plus(b[3][0], got1[s][0])
        else:
            flown = (bk1[s + 1], fback, *[sh.terms[-1] for sh in shares + outs])
            got1[s] = beside(after(b[2], *flown))
            dx = dinput_step(
                (s + 1) * rows, width, idx, back[s + 1][3], got1[s + 1], after(bk1[s + 1], ds), dr[s + 1],
                arrived, gain1, front[s + 1][12],
            )
            away1[s] = plus(b[3][0], after(got1[s], dx)[0])
        bk1[s] = across(away1[s])
        if s == NSEG - 1:
            for sh in shares:
                sh.middle(ds)
                sh.start()
            outg = out_grads(
                after(idx, away1[s]), NSEG,
                [v for q in range(NSEG) for v in (pre[q][0], front[q][7], front[q][0], pre[q][2])],
            )
            outs = [Share(outg[0], outg[1], dp, FIRST)]
            for sh in outs:
                sh.start()
            faway = plus(fkeep[0], fgot[0])
            fback = across(after(faway, away1[s]))
    small = after(sum(b[4] for b in back), *flown)
    gsum = sum(f[9] for f in ffn)
    ghead = jnp.pad(sum(p[3][0:1] for p in pre), ((0, 0), (0, width - dv)))
    small = jnp.concatenate([small[0:4], ghead, small[5:8], gsum, jnp.zeros((7, width), F32)], 0)
    small = small + swap(small, "dp", dp, 1)

    lead = []
    for s in range(NSEG):
        o, b = front[s], back[s]
        lead += [o[0], b[0], b[1]]
    plan = ((FIRST, ((0, 1, 0, cw), (0, 2, 0, CH))),)
    wide = row_grads(after(idx, away1[0]), NSEG, plan, lead)
    tail = Share(wide[0], wide[1], dp, FIRST)
    tail.start()
    second = swap(after(small, wide[0]), "dp", dp, 2)
    out_share = outs[0]
    out_share.middle(wide[0])
    out_share.start()
    shares[0].middle(wide[0])
    shares[0].start()
    keep = after(back[0][3], wide[0])
    dx = dinput_step(0, width, idx, keep, got1[0], bk1[0], dr[0], arrived, gain1, front[0][12], dx)
    returned = lax.all_to_all(
        dx.reshape(dp, length // dp, quarter), "dp", split_axis=0, concat_axis=0, tiled=True
    )
    mask = (jnp.arange(length) < own_length).astype(F32)[:, None]
    rest = fkeep[1].astype(F32) + after(fgot, dx)[1].astype(F32) + fback.astype(F32)
    mixed = (jnp.concatenate([r[0] for r in resid], 0) + mask * rest).astype(BF)
    out_share.middle(mixed)
    out_share.start()
    tail.middle(out_share.send)
    tail.start()
    small = small + after(second, tail.send)
    third = swap(small, "dp", dp, 4)
    shares[1].middle(tail.send)
    shares[1].start()
    lower = shares[0].finish(1, shares[1].send)
    tail.middle(lower)
    tail.start()
    small = small + after(third, tail.send)
    bit = 8
    while bit < dp:
        small = small + swap(small, "dp", dp, bit)
        bit *= 2
    upper = shares[1].finish(1, tail.send)
    summed = total_tensor(jnp.concatenate([small[4:5], small[7:9]], 0))
    source_grad = jnp.zeros_like(returned).at[dealing].set(
        after(returned, tail.send), mode="promise_in_bounds", unique_indices=True
    )
    outw = out_share.finish(0, tail.send)
    outw, gatew = outw[:, :vd], outw[:, vd:]
    wide = tail.finish(0, summed)
    shared = small[0:7]
    part = width // dp
    start = lax.axis_index("dp") * part
    norm_gain_grad = own(summed[1] / norm_gain, start, part)
    ffn_gain_grad = own(summed[2] / ffn_gain, start, part)
    return (
        mixed[None],
        source_grad,
        norm_gain_grad,
        wide[:, 0:qd],
        wide[:, qd : 2 * qd],
        wide[:, 2 * qd : cw],
        shared[0:4, 0:qd],
        shared[0:4, qd : 2 * qd],
        shared[0:4, 2 * qd : cw],
        wide[:, cw : cw + heads],
        wide[:, cw + heads : cw + 2 * heads],
        shared[5, heads : 2 * heads],
        shared[6, heads : 2 * heads],
        gatew,
        summed[0, 0:dv],
        outw,
        ffn_gain_grad,
        jnp.concatenate([lower[units:], upper[: units // 2]], 0).T,
        upper[units // 2 :].T,
        lower[:units].T,
    )


def solution(mesh):
    in_specs = (
        P(None, "dp", "tensor"),
        P("dp", None, "tensor"),
        P(),
        P(),
        P(),
        P(None, "tensor"),
        P(None, "tensor"),
        P(None, "tensor"),
        P(None, "tensor"),
        P(None, "tensor"),
        P(None, "tensor"),
        P(None, "tensor"),
        P(None, "tensor"),
        P("tensor"),
        P("tensor"),
        P(None, "tensor"),
        P(),
        P(None, "tensor"),
        P(),
        P(None, "tensor"),
        P(None, "tensor"),
        P(None, "tensor"),
    )
    out_specs = (
        P("dp", None, "tensor"),
        P(None, "dp", "tensor"),
        P("dp"),
        P("dp", "tensor"),
        P("dp", "tensor"),
        P("dp", "tensor"),
        P(None, "tensor"),
        P(None, "tensor"),
        P(None, "tensor"),
        P("dp", "tensor"),
        P("dp", "tensor"),
        P("tensor"),
        P("tensor"),
        P("dp", "tensor"),
        P(),
        P("dp", "tensor"),
        P("dp"),
        P("dp", "tensor"),
        P("dp", "tensor"),
        P("dp", "tensor"),
    )
    return jax.shard_map(
        per_device, mesh=mesh, in_specs=in_specs, out_specs=out_specs, check_vma=False
    )
```

```python
import functools
import jax
import jax.numpy as jnp
from jax import lax
from jax.sharding import PartitionSpec as P
from jax.experimental import pallas as pl
from jax.experimental.pallas import tpu as pltpu

F32 = jnp.float32
BF = jnp.bfloat16
NN = ((1,), (0,))
NT = ((1,), (1,))
TN = ((0,), (0,))
CH = 128
EPS = 1e-6
TAIL = 16
VMEM_LIMIT = 56 * 1024 * 1024


def mm(a, b, dims=NN):
    return lax.dot_general(a.astype(BF), b.astype(BF), (dims, ((), ())), preferred_element_type=F32)


def mm3(a, b, dims=NN):
    ah, bh = a.astype(BF), b.astype(BF)
    al, bl = a - ah.astype(F32), b - bh.astype(F32)
    rows = a.shape[0]
    both = mm(jnp.concatenate([ah, al.astype(BF)], 0), bh, dims)
    return both[0:rows] + (both[rows:] + mm(ah, bl, dims))


def mm_exact(a, b):
    return lax.dot_general(
        a, b, (NN, ((), ())), precision=lax.Precision.HIGHEST, preferred_element_type=F32
    )


def sigm(u):
    return 0.5 * jnp.tanh(0.5 * u) + 0.5


def grid_iotas():
    return (
        lax.broadcasted_iota(jnp.int32, (CH, CH), 0),
        lax.broadcasted_iota(jnp.int32, (CH, CH), 1),
    )


def conv_rows(buf, conv, start, cols):
    acc = None
    for i in range(4):
        term = conv[i : i + 1, cols] * buf[start - 3 + i : start - 3 + i + CH, cols]
        acc = term if acc is None else acc + term
    return acc


def soft_plus(u):
    return jnp.maximum(u, 0.0) + jnp.log1p(jnp.exp(-jnp.abs(u)))


def fwd_kernel(
    heads, dk, dv, width,
    idx, x0, x1, x2, x3, gain, wq, wk, wv, wg, wba, conv, dec, hgain, wo, s_in, halo_in,
    h_out, proj_out, ba_out, u_out, o_out, st_out, t_out, z_out, send_out, keep_out, s_fin, halo_fin, scale_out, a_out, p_out, gbuf,
    cbuf, qs, ks, vs, abuf, wbuf, vbuf, nbuf, fbuf, rowb, colb,
):
    rows = x0.shape[0]
    quarter = x0.shape[1]
    qd, vd = heads * dk, heads * dv
    chunks = rows // CH
    cbuf[0:8, :] = halo_in[...]
    xs = (x0, x1, x2, x3)
    tile = 128
    for r in range(rows // tile):
        rr = slice(r * tile, r * tile + tile)
        parts = [x[rr, :].astype(F32) for x in xs]
        total = jnp.sum(sum(p * p for p in parts), -1, keepdims=True)
        scale = lax.rsqrt(total * (1.0 / width) + EPS)
        scale_out[:, rr] = jnp.transpose(jnp.broadcast_to(scale, (tile, CH)))[0:8, :]
        for n in range(4):
            cols = pl.ds(pl.multiple_of(idx[n] * quarter, quarter), quarter)
            h_out[rr, cols] = (parts[n] * scale * gain[idx[n]]).astype(BF)
    for w, lo, n in ((wq, 0, qd), (wk, qd, qd), (wv, 2 * qd, vd)):
        part = mm(h_out[...], w[...])
        cbuf[8 : 8 + rows, lo : lo + n] = part
        proj_out[:, lo : lo + n] = part
    part = mm(h_out[...], wg[...])
    gbuf[...] = part
    ba_out[...] = mm(h_out[...], wba[...])
    halo_fin[...] = cbuf[rows : rows + 8, :]
    ii, jj = grid_iotas()
    lower = jnp.where(ii >= jj, 1.0, 0.0).astype(F32)
    lane = lax.broadcasted_iota(jnp.int32, (1, CH), 1)
    for c in range(chunks):
        rr = slice(c * CH, c * CH + CH)
        raw = ba_out[rr, :]
        beta = sigm(raw)
        rate = dec[0:1, :] * soft_plus(raw + dec[1:2, :])
        rate = jnp.where((lane >= heads) & (lane < 2 * heads), rate, 0.0)
        run = mm_exact(lower, rate)
        colb[c] = jnp.where(lane < heads, beta, run)
        rowb[c] = jnp.transpose(run)
        for h in range(heads):
            for which, dst, mul in ((0, qs, dk ** -0.5), (qd, ks, 1.0)):
                cols = slice(which + h * dk, which + h * dk + dk)
                u = conv_rows(cbuf, conv, 8 + c * CH, cols)
                u = u * sigm(u)
                norm = lax.rsqrt(jnp.sum(u * u, -1, keepdims=True) + EPS) * mul
                dst[rr, h * dk : h * dk + dk] = u * norm
            cols = slice(2 * qd + h * dv, 2 * qd + h * dv + dv)
            u = conv_rows(cbuf, conv, 8 + c * CH, cols)
            vs[rr, h * dv : h * dv + dv] = u * sigm(u)
    units = [(c, h) for c in range(chunks) for h in range(heads)]
    xr = ii ^ jj
    eye = jnp.where(ii == jj, 1.0, 0.0).astype(F32)
    for n, (c, h) in enumerate(units):
        rr = slice(c * CH, c * CH + CH)
        k = ks[rr, h * dk : h * dk + dk]
        bc = colb[c, :, heads + h : heads + h + 1]
        br = rowb[c, heads + h : heads + h + 1, :]
        bt = colb[c, :, h : h + 1]
        a = jnp.where(ii > jj, bt * mm(k, k, NT) * jnp.exp(bc - br), 0.0)
        abuf[n] = a.astype(BF)
        a_out[n] = a
        t_out[n] = (eye - jnp.where(xr == 1, a, 0.0)).astype(BF)
    step = 2
    while step < CH:
        for n in range(len(units)):
            t = t_out[n]
            part = jnp.where((xr >= step) & (xr < 2 * step), abuf[n].astype(F32), 0.0)
            t_out[n] = (t.astype(F32) - mm(mm(t, part), t)).astype(BF)
        step *= 2
    for n, (c, h) in enumerate(units):
        rr = slice(c * CH, c * CH + CH)
        k = ks[rr, h * dk : h * dk + dk]
        v = vs[rr, h * dv : h * dv + dv]
        bc = colb[c, :, heads + h : heads + h + 1]
        bt = colb[c, :, h : h + 1]
        last = colb[c, CH - 1 : CH, heads + h : heads + h + 1]
        t = jnp.where(ii > jj, t_out[n].astype(F32), 0.0).astype(BF)
        t_out[n] = t
        bk, bv = (bt * jnp.exp(bc)) * k, bt * v
        w = (bk + mm(t, bk)).astype(BF)
        vv = bv + mm(t, bv)
        wbuf[n] = w
        vbuf[n] = vv
        kt = (k * jnp.exp(last - bc)).astype(BF)
        nbuf[n] = mm(kt, w, TN).astype(BF)
        fbuf[n] = mm(kt, vv, TN)
    for h in range(heads):
        s_fin[h] = s_in[h]
    for c in range(chunks):
        rr = slice(c * CH, c * CH + CH)
        for h in range(heads):
            n = c * heads + h
            s = s_fin[h]
            sb = s.astype(BF)
            st_out[n] = sb
            last = colb[c, CH - 1 : CH, heads + h : heads + h + 1]
            s_fin[h] = jnp.exp(last) * s + fbuf[n] - mm(nbuf[n], sb)
        for h in range(heads):
            n = c * heads + h
            q = qs[rr, h * dk : h * dk + dk]
            k = ks[rr, h * dk : h * dk + dk]
            bc = colb[c, :, heads + h : heads + h + 1]
            br = rowb[c, heads + h : heads + h + 1, :]
            p = jnp.where(ii >= jj, mm3(q, k, NT) * jnp.exp(bc - br), 0.0)
            p_out[n] = p
            s = st_out[n]
            both = mm(jnp.concatenate([wbuf[n], (q * jnp.exp(bc)).astype(BF)], 0), s)
            u = vbuf[n] - both[0:CH]
            u_out[rr, h * dv : h * dv + dv] = u
            o = both[CH:] + mm3(p, u)
            o_out[rr, h * dv : h * dv + dv] = o
            scale = lax.rsqrt(jnp.mean(o * o, -1, keepdims=True) + EPS)
            g = gbuf[rr, h * dv : h * dv + dv]
            z = o * scale * hgain[...] * (g * sigm(g))
            z_out[rr, h * dv : h * dv + dv] = z.astype(BF)
    out_blocks(idx, z_out, wo, send_out, keep_out, rows, quarter)


def out_blocks(idx, src, wo, send_out, keep_out, rows, quarter):
    for dst, pos, which in ((send_out, 0, 3), (send_out, 1, 2), (keep_out, 0, 1), (keep_out, 1, 0)):
        blk = pl.ds(pl.multiple_of(idx[which] * quarter, quarter), quarter)
        dst[pos] = mm(src[...], wo[blk, :], NT).astype(BF)


def mixer_forward(idx, xs, gain, wq, wk, wv, wg, wba, conv, dec, hgain, wo, s_in, halo_in):
    rows, quarter = xs[0].shape
    width = wq.shape[0]
    heads, dk, dv = s_in.shape
    qd, vd = heads * dk, heads * dv
    units = rows // CH * heads
    chunks = rows // CH
    outs = [
        ((rows, width), BF), ((rows, 2 * qd + vd), F32), ((rows, CH), F32),
        ((rows, vd), F32), ((rows, vd), F32), ((units, dk, dv), BF), ((units, CH, CH), BF),
        ((rows, vd), BF), ((2, rows, quarter), BF), ((2, rows, quarter), BF),
        ((heads, dk, dv), F32), ((8, 2 * qd + vd), F32), ((8, rows), F32),
        ((units, CH, CH), F32), ((units, CH, CH), F32), ((rows, vd), F32),
    ]
    smem = pl.BlockSpec(memory_space=pltpu.SMEM)
    vm = pl.BlockSpec(memory_space=pltpu.VMEM)
    return pl.pallas_call(
        functools.partial(fwd_kernel, heads, dk, dv, width),
        out_shape=[jax.ShapeDtypeStruct(s, d) for s, d in outs],
        in_specs=[smem] + [vm] * 16,
        out_specs=[vm] * len(outs),
        scratch_shapes=[
            pltpu.VMEM((rows + 8, 2 * qd + vd), F32),
            pltpu.VMEM((rows, qd), F32), pltpu.VMEM((rows, qd), F32), pltpu.VMEM((rows, vd), F32),
            pltpu.VMEM((units, CH, CH), BF), pltpu.VMEM((units, CH, dk), BF),
            pltpu.VMEM((units, CH, dv), F32), pltpu.VMEM((units, dk, dk), BF),
            pltpu.VMEM((units, dk, dv), F32), pltpu.VMEM((chunks, CH, CH), F32),
            pltpu.VMEM((chunks, CH, CH), F32),
        ],
        compiler_params=pltpu.CompilerParams(vmem_limit_bytes=VMEM_LIMIT),
        cost_estimate=pl.CostEstimate(flops=rows * 32000000, bytes_accessed=12 * rows * 1024, transcendentals=rows * 4096),
        name="mix_fwd",
    )(idx, *xs, gain, wq, wk, wv, wg, wba, conv, dec, hgain, wo, s_in, halo_in)


def bwd_kernel(
    heads, dk, dv, width,
    idx, dob, dgate, h_in, proj, ba, u_in, st_in, t_in, a_in, p_in, wq, wk, wv, wg, wba, conv, dec,
    halo_in, ds_in, dhalo_in,
    dproj_out, dba_out, send_out, keep_out, small_out, ds_fin, dhalo_fin,
    pbuf, cbuf, sgbuf, dcbuf, qs, ks, vs, r0b, ktb, d0b, mb, dsb, rowb, colb,
):
    rows = dob.shape[0]
    quarter = send_out.shape[2]
    qd, vd = heads * dk, heads * dv
    cw = 2 * qd + vd
    chunks = rows // CH
    units = [(c, h) for c in range(chunks) for h in range(heads)]
    ii, jj = grid_iotas()
    lower = jnp.where(ii >= jj, 1.0, 0.0).astype(F32)
    strict = jnp.where(ii > jj, 1.0, 0.0).astype(F32)
    upper = jnp.where(ii <= jj, 1.0, 0.0).astype(F32)
    lane = lax.broadcasted_iota(jnp.int32, (1, CH), 1)
    pbuf[0:8, :] = halo_in[...]
    pbuf[8 : 8 + rows, :] = proj[...]
    dcbuf[rows : rows + 8, :] = dhalo_in[...]
    for c in range(chunks):
        rr = slice(c * CH, c * CH + CH)
        raw = ba[rr, :]
        rate = dec[0:1, :] * soft_plus(raw + dec[1:2, :])
        rate = jnp.where((lane >= heads) & (lane < 2 * heads), rate, 0.0)
        run = mm_exact(lower, rate)
        act = jnp.where(lane < heads, sigm(raw), run)
        colb[c] = act
        rowb[c] = jnp.transpose(act)
        for h in range(heads):
            for which, dst, mul in ((0, qs, dk ** -0.5), (qd, ks, 1.0)):
                cols = slice(which + h * dk, which + h * dk + dk)
                u = conv_rows(pbuf, conv, 8 + c * CH, cols)
                sg = sigm(u)
                cbuf[rr, cols] = u
                sgbuf[rr, cols] = sg
                u = u * sg
                norm = lax.rsqrt(jnp.sum(u * u, -1, keepdims=True) + EPS) * mul
                dst[rr, h * dk : h * dk + dk] = u * norm
            cols = slice(2 * qd + h * dv, 2 * qd + h * dv + dv)
            u = conv_rows(pbuf, conv, 8 + c * CH, cols)
            sg = sigm(u)
            cbuf[rr, cols] = u
            sgbuf[rr, cols] = sg
            vs[rr, h * dv : h * dv + dv] = u * sg
    small_out[...] = jnp.zeros_like(small_out)
    for n, (c, h) in enumerate(units):
        rr = slice(c * CH, c * CH + CH)
        q = qs[rr, h * dk : h * dk + dk]
        k = ks[rr, h * dk : h * dk + dk]
        do = dob[rr, h * dv : h * dv + dv]
        bc = colb[c, :, heads + h : heads + h + 1]
        br = rowb[c, heads + h : heads + h + 1, :]
        bt = colb[c, :, h : h + 1]
        last = colb[c, CH - 1 : CH, heads + h : heads + h + 1]
        grow = jnp.exp(bc)
        t = t_in[n]
        pd = mm3(jnp.transpose(p_in[n]), do)
        r0 = pd + mm(t, pd, TN)
        kt = k * jnp.exp(last - bc)
        kt = (kt + mm(t, kt, TN)).astype(BF)
        bgk = (bt * grow * k).astype(BF)
        r0b[n] = r0
        ktb[n] = kt
        d0b[n] = mm(grow * q, do, TN) - mm(bgk, r0, TN)
        mb[n] = mm(bgk, kt, TN).astype(BF)
    for h in range(heads):
        ds_fin[h] = ds_in[h]
    for c in reversed(range(chunks)):
        for h in range(heads):
            n = c * heads + h
            s = ds_fin[h]
            sb = s.astype(BF)
            dsb[n] = s
            last = colb[c, CH - 1 : CH, heads + h : heads + h + 1]
            ds_fin[h] = jnp.exp(last) * s + d0b[n] - mm(mb[n], sb)
    for c in range(chunks):
        rr = slice(c * CH, c * CH + CH)
        first = jnp.zeros((CH, CH), F32)
        second = jnp.zeros((CH, CH), F32)
        gextra = jnp.zeros((CH, CH), F32)
        for h in range(heads):
            n = c * heads + h
            q = qs[rr, h * dk : h * dk + dk]
            k = ks[rr, h * dk : h * dk + dk]
            v = vs[rr, h * dv : h * dv + dv]
            do = dob[rr, h * dv : h * dv + dv]
            u = u_in[rr, h * dv : h * dv + dv]
            s0 = st_in[n]
            ds = dsb[n]
            dsl = ds.astype(BF)
            qf, kf = q, k
            bc = colb[c, :, heads + h : heads + h + 1]
            br = rowb[c, heads + h : heads + h + 1, :]
            bt = colb[c, :, h : h + 1]
            btr = rowb[c, h : h + 1, :]
            last = colb[c, CH - 1 : CH, heads + h : heads + h + 1]
            grow = jnp.exp(bc)
            tail = jnp.exp(last - bc)
            r = r0b[n] + mm(ktb[n], dsl)
            dec_d = jnp.exp(bc - br)
            uh = u.astype(BF)
            ul = (u - uh.astype(F32)).astype(BF)
            pairh = jnp.concatenate([r, do], 0)
            pairl = pairh - pairh.astype(BF).astype(F32)
            raw4 = mm(jnp.concatenate([pairh, pairl], 0), uh, NT)
            raw = raw4[0 : 2 * CH] + (raw4[2 * CH :] + mm(pairh, ul, NT))
            da = jnp.where(ii > jj, -raw[0:CH] * dec_d, 0.0)
            dp = jnp.where(ii >= jj, raw[CH:] * dec_d, 0.0)
            inter = raw[CH:] * p_in[n] - raw[0:CH] * a_in[n]
            ih = inter.astype(BF)
            cums = mm(upper, jnp.concatenate([ih, (inter - ih.astype(F32)).astype(BF)], 1))
            cum = cums[:, 0:CH] + cums[:, CH:]
            states = mm(pairh, s0, NT)
            rs = grow * states[0:CH]
            dq1 = grow * states[CH:]
            local = mm(jnp.concatenate([dp, da], 0), k)
            dq = dq1 + local[0:CH]
            x = local[CH:] - rs
            us = tail * mm(uh, dsl, NT)
            dkw = mm(jnp.concatenate([dp, bt * da], 0), jnp.concatenate([q, k], 0), TN) + us
            dk_all = bt * x + dkw
            dbeta = jnp.sum(kf * x, -1, keepdims=True) + jnp.sum(r * v, -1, keepdims=True)
            ci = jnp.sum(qf * dq1 - bt * (kf * rs), -1, keepdims=True)
            wj = jnp.sum(kf * us, -1, keepdims=True)
            base = jnp.sum(jnp.where(jj < ii, cum, 0.0), -1, keepdims=True)
            whole = jnp.exp(last) * jnp.sum(
                jnp.sum(s0.astype(F32) * ds, -1, keepdims=True), 0, keepdims=True
            )
            first = first + jnp.where(lane == heads + h, ci, 0.0)
            second = second + jnp.where(lane == heads + h, wj, 0.0)
            gextra = gextra + jnp.where(lane == heads + h, base + whole, 0.0)
            gextra = gextra + jnp.where(lane == h, dbeta, 0.0)
            for dst, grad, mul in ((0, dq, dk ** -0.5), (qd, dk_all, 1.0)):
                cols = slice(dst + h * dk, dst + h * dk + dk)
                cv = cbuf[rr, cols]
                sg = sgbuf[rr, cols]
                y = cv * sg
                norm = lax.rsqrt(jnp.sum(y * y, -1, keepdims=True) + EPS)
                yn = y * norm
                dy = (norm * mul) * (grad - yn * jnp.sum(grad * yn, -1, keepdims=True))
                dcbuf[rr, cols] = dy * (sg * (1.0 + cv * (1.0 - sg)))
            cols = slice(2 * qd + h * dv, 2 * qd + h * dv + dv)
            cv = cbuf[rr, cols]
            sg = sgbuf[rr, cols]
            dcbuf[rr, cols] = bt * r * (sg * (1.0 + cv * (1.0 - sg)))
        dg = mm_exact(upper, first) + mm_exact(strict, second) + gextra
        raw = ba[rr, :]
        act = raw + dec[1:2, :]
        sp = soft_plus(act)
        sb = sigm(raw)
        dfac = dec[0:1, :]
        isb = lane < heads
        isd = (lane >= heads) & (lane < 2 * heads)
        draw = jnp.where(isb, dg * sb * (1.0 - sb), jnp.where(isd, dg * dfac * sigm(act), 0.0))
        dba_out[rr, :] = draw.astype(BF)
        small_out[5:6, 0:CH] += jnp.sum(jnp.where(isd, dg * dfac * sp, 0.0), 0, keepdims=True)
        small_out[6:7, 0:CH] += jnp.sum(jnp.where(isd, draw, 0.0), 0, keepdims=True)
    dhalo_fin[...] = dcbuf[0:8, :]
    for c in range(chunks):
        rr = slice(c * CH, c * CH + CH)
        for lo in range(0, cw, 256):
            cols = slice(lo, lo + 256)
            acc = None
            dc = dcbuf[rr, cols]
            for i in range(4):
                sh = slice(c * CH + 3 - i, c * CH + 3 - i + CH)
                term = conv[i : i + 1, cols] * dcbuf[sh, cols]
                acc = term if acc is None else acc + term
                src = pbuf[c * CH + 5 + i : c * CH + 5 + i + CH, cols]
                small_out[i : i + 1, cols] += jnp.sum(dc * src, 0, keepdims=True)
            dproj_out[rr, cols] = acc.astype(BF)
    rowsum = jnp.zeros((8, rows), F32)
    ones = jnp.ones((8, quarter), BF)
    for dst, pos, which in ((send_out, 0, 3), (send_out, 1, 2), (keep_out, 0, 1), (keep_out, 1, 0)):
        blk = pl.ds(pl.multiple_of(idx[which] * quarter, quarter), quarter)
        out = (
            mm(dproj_out[:, 0:qd], wq[blk, :], NT)
            + mm(dproj_out[:, qd : 2 * qd], wk[blk, :], NT)
            + mm(dproj_out[:, 2 * qd : cw], wv[blk, :], NT)
            + mm(dgate[...], wg[blk, :], NT)
            + mm(dba_out[...], wba[blk, :], NT)
        )
        dst[pos, 0:rows, :] = out.astype(BF)
        prod = out * h_in[:, blk].astype(F32)
        small_out[7:8, blk] = jnp.sum(prod, 0, keepdims=True)
        rowsum = rowsum + mm(ones, prod, NT)
    small_out[8:16, :] = mm(dba_out[...], h_in[...], TN)[0:8, :]
    put_stats(send_out, keep_out, rowsum, rows, quarter)


def put_stats(send_out, keep_out, rowsum, rows, quarter):
    for dst in (send_out, keep_out):
        dst[:, rows : rows + TAIL, :] = jnp.zeros((2, TAIL, quarter), BF)
        for n in range(rows // quarter):
            dst[0, rows + n : rows + n + 1, :] = rowsum[0:1, n * quarter : n * quarter + quarter].astype(BF)


def mixer_backward(idx, quarter, do, dgate, h, proj, ba, u, st, t, a, p, wq, wk, wv, wg, wba, conv, dec, halo, ds, dhalo):
    rows = do.shape[0]
    width = wq.shape[0]
    heads, dk, dv = ds.shape
    qd, vd = heads * dk, heads * dv
    cw = 2 * qd + vd
    chunks = rows // CH
    units = chunks * heads
    outs = [
        ((rows, cw), BF), ((rows, CH), BF), ((2, rows + TAIL, quarter), BF), ((2, rows + TAIL, quarter), BF),
        ((16, width), F32), ((heads, dk, dv), F32), ((8, cw), F32),
    ]
    smem = pl.BlockSpec(memory_space=pltpu.SMEM)
    vm = pl.BlockSpec(memory_space=pltpu.VMEM)
    return pl.pallas_call(
        functools.partial(bwd_kernel, heads, dk, dv, width),
        out_shape=[jax.ShapeDtypeStruct(s, d) for s, d in outs],
        in_specs=[smem] + [vm] * 20,
        out_specs=[vm] * len(outs),
        scratch_shapes=[
            pltpu.VMEM((rows + 8, cw), F32), pltpu.VMEM((rows, cw), F32), pltpu.VMEM((rows, cw), F32), pltpu.VMEM((rows + 8, cw), F32),
            pltpu.VMEM((rows, qd), F32), pltpu.VMEM((rows, qd), F32), pltpu.VMEM((rows, vd), F32),
            pltpu.VMEM((units, CH, dv), F32), pltpu.VMEM((units, CH, CH), BF),
            pltpu.VMEM((units, dk, dv), F32), pltpu.VMEM((units, dk, dk), BF),
            pltpu.VMEM((units, dk, dv), F32), pltpu.VMEM((chunks, CH, CH), F32),
            pltpu.VMEM((chunks, CH, CH), F32),
        ],
        compiler_params=pltpu.CompilerParams(vmem_limit_bytes=VMEM_LIMIT),
        cost_estimate=pl.CostEstimate(flops=rows * 58000000, bytes_accessed=24 * rows * 1024, transcendentals=rows * 8192),
        name="mix_bwd",
    )(idx, do, dgate, h, proj, ba, u, st, t, a, p, wq, wk, wv, wg, wba, conv, dec, halo, ds, dhalo)


def out_bwd_kernel(heads, idx, mine, core, wo, hgain, g_in, o_in, da_out, do_out, dgate_out, head_out, dzb):
    rows, vd = o_in.shape
    quarter = mine.shape[2]
    dv = vd // heads
    for n, a in enumerate((mine.at[0], mine.at[1], core.at[0], core.at[1])):
        da_out[:, pl.ds(pl.multiple_of(idx[n] * quarter, quarter), quarter)] = a[...]
    dzb[...] = mm(da_out[...], wo[...])
    hg = hgain[...]
    ghead = jnp.zeros((1, dv), F32)
    for c in range(rows // CH):
        for h in range(heads):
            rr, hv = slice(c * CH, c * CH + CH), slice(h * dv, h * dv + dv)
            o = o_in[rr, hv]
            scale = lax.rsqrt(jnp.mean(o * o, -1, keepdims=True) + EPS)
            on = o * scale
            g = g_in[rr, hv]
            sg = sigm(g)
            dz = dzb[rr, hv]
            dgate_out[rr, hv] = (dz * on * hg * (sg * (1.0 + g * (1.0 - sg)))).astype(BF)
            dn = dz * (g * sg)
            ghead = ghead + jnp.sum(dn * on, 0, keepdims=True)
            e = dn * hg
            do_out[rr, hv] = scale * (e - on * jnp.mean(e * on, -1, keepdims=True))
    head_out[...] = jnp.broadcast_to(ghead, head_out.shape)


def out_backward(idx, heads, pair, wo, hgain, gate, o):
    rows, vd = o.shape
    smem = pl.BlockSpec(memory_space=pltpu.SMEM)
    vm = pl.BlockSpec(memory_space=pltpu.VMEM)
    outs = [((rows, wo.shape[0]), BF), ((rows, vd), F32), ((rows, vd), BF), ((8, vd // heads), F32)]
    return pl.pallas_call(
        functools.partial(out_bwd_kernel, heads),
        out_shape=[jax.ShapeDtypeStruct(s, d) for s, d in outs],
        in_specs=[smem] + [vm] * 6,
        out_specs=[vm] * 4,
        scratch_shapes=[pltpu.VMEM((rows, vd), F32)],
        compiler_params=pltpu.CompilerParams(vmem_limit_bytes=VMEM_LIMIT),
        cost_estimate=pl.CostEstimate(flops=rows * 8000000, bytes_accessed=14 * rows * 1024, transcendentals=rows * vd),
        name="out_bwd",
    )(idx, *pair, wo, hgain, gate, o)


def ffn_kernel(
    width, base, folded,
    idx, mine, core, c0, c1, c2, c3, gain, wg, wu, wd, *refs,
):
    (
        h_out, df_out, hid_out, dfg_out, dfu_out, send_out, keep_out, fsend_out, fkeep_out, gsum_out, scale_out,
        fgb, fub, dhb,
    ) = refs[2 * folded :]
    rows, quarter = mine.shape[1:]
    tile = CH
    rs, cs = (mine.at[0], mine.at[1], core.at[0], core.at[1]), (c0, c1, c2, c3)
    for r in range(rows // tile):
        rr = slice(r * tile, r * tile + tile)
        total = None
        for n in range(4):
            part = jnp.square(rs[n][rr, :].astype(F32) / gain[idx[n]])
            part = jnp.sum(part, -1, keepdims=True)
            total = part if total is None else total + part
        scale = lax.rsqrt(total * (1.0 / width) + EPS)
        scale_out[:, rr] = jnp.transpose(jnp.broadcast_to(scale, (tile, CH)))[0:8, :]
        place = base + r * tile + lax.broadcasted_iota(jnp.int32, (tile, 1), 0)
        valid = jnp.where(place < idx[4], 1.0, 0.0).astype(F32)
        for n in range(4):
            cols = pl.ds(pl.multiple_of(idx[n] * quarter, quarter), quarter)
            h_out[rr, cols] = rs[n][rr, :]
            df_out[rr, cols] = (cs[n][base + r * tile : base + r * tile + tile, :].astype(F32) * valid).astype(BF)
    fgb[...] = mm(h_out[...], wg[...], NT)
    fub[...] = mm(h_out[...], wu[...], NT)
    dhb[...] = mm(df_out[...], wd[...], NT)
    for r in range(rows // tile):
        rr = slice(r * tile, r * tile + tile)
        scale = jnp.transpose(jnp.broadcast_to(scale_out[0:1, rr], (CH, tile)))[:, 0:1]
        fg = scale * fgb[rr, :]
        fu = scale * fub[rr, :]
        ds = scale * dhb[rr, :]
        sg = sigm(fg)
        act = fg * sg
        hid_out[rr, :] = (act * fu).astype(BF)
        dfg_out[rr, :] = (ds * fu * sg * (1.0 + fg * (1.0 - sg))).astype(BF)
        dfu_out[rr, :] = (ds * act).astype(BF)
    rowsum = jnp.zeros((8, rows), F32)
    ones = jnp.ones((8, quarter), BF)
    order = ((0, 0, 3), (0, 1, 2), (1, 0, 1), (1, 1, 0))
    for kept, pos, which in order:
        blk = pl.ds(pl.multiple_of(idx[which] * quarter, quarter), quarter)
        out = mm(dfg_out[...], wg[:, blk]) + mm(dfu_out[...], wu[:, blk])
        (keep_out if kept else send_out)[pos, 0:rows, :] = out.astype(BF)
        prod = out * h_out[:, blk].astype(F32)
        gsum_out[0:1, blk] = jnp.sum(prod, 0, keepdims=True)
        rowsum = rowsum + mm(ones, prod, NT)
    put_stats(send_out, keep_out, rowsum, rows, quarter)
    for kept, pos, which in order:
        blk = pl.ds(pl.multiple_of(idx[which] * quarter, quarter), quarter)
        (fkeep_out if kept else fsend_out)[pos] = mm(hid_out[...], wd[:, blk]).astype(BF)


def ffn_both(base, idx, mine, core, cs, gain, wg, wu, wd, fold=None):
    rows, quarter = mine.shape[1:]
    units, width = wg.shape
    length = cs[0].shape[0]
    tall = ((2, rows + TAIL, quarter), BF)
    whole = ((2, length, quarter), BF)
    outs = [
        ((rows, width), BF), ((rows, width), BF), ((rows, units), BF), ((rows, units), BF), ((rows, units), BF),
        tall, tall, whole, whole, ((1, width), F32), ((8, rows), F32),
    ]
    smem = pl.BlockSpec(memory_space=pltpu.SMEM)
    vm = pl.BlockSpec(memory_space=pltpu.VMEM)
    part = base // rows
    slab = pl.BlockSpec((2, rows, quarter), lambda i: (0, part, 0), pipeline_mode=pl.Buffered(1))
    args = (idx, mine, core, *cs, gain, wg, wu, wd)
    specs = [smem] + [vm] * 10
    alias = {}
    if fold is not None:
        args += tuple(fold)
        specs += [pl.BlockSpec(memory_space=pl.ANY)] * 2
        alias = {len(args) - 2: 7, len(args) - 1: 8}
    return pl.pallas_call(
        functools.partial(ffn_kernel, width, base, fold is not None),
        grid=(1,),
        out_shape=[jax.ShapeDtypeStruct(s, d) for s, d in outs],
        in_specs=specs,
        out_specs=[vm] * 7 + [slab, slab, vm, vm],
        scratch_shapes=[pltpu.VMEM((rows, units), F32)] * 3,
        input_output_aliases=alias,
        compiler_params=pltpu.CompilerParams(vmem_limit_bytes=24 * 1024 * 1024),
        cost_estimate=pl.CostEstimate(flops=rows * 27000000, bytes_accessed=10 * rows * width, transcendentals=rows * units),
        name="ffn_both",
    )(*args)


def valid_rows(idx, start, count):
    place = start + lax.broadcasted_iota(jnp.int32, (count, 1), 0)
    return jnp.where(place < idx[4], 1.0, 0.0).astype(F32)


def columns(row):
    block = jnp.transpose(jnp.broadcast_to(row, (CH, CH)))
    return jnp.concatenate([block, block], 1)


def resid_kernel(base, idx, t, u, x0, x1, gain, r_out, low_out):
    m = valid_rows(idx, base, t.shape[1])
    for n, x in ((0, x0), (1, x1)):
        r = x[...].astype(F32) + m * (t[1 - n].astype(F32) + u[n].astype(F32))
        r_out[n] = r
        low_out[n] = (r * gain[idx[n]]).astype(BF)


def part_specs(base, rows, quarter):
    once = pl.Buffered(1)
    return (
        pl.BlockSpec((2, rows, quarter), lambda i: (0, 0, 0), pipeline_mode=once),
        pl.BlockSpec((rows, quarter), lambda i: (0, 0), pipeline_mode=once),
        pl.BlockSpec((rows, quarter), lambda i: (base // rows, 0), pipeline_mode=once),
        pl.BlockSpec(memory_space=pltpu.SMEM),
        pl.BlockSpec(memory_space=pltpu.VMEM),
    )


def resid_step(base, idx, t, u, x0, x1, gain):
    rows, quarter = t.shape[1:]
    pair, tile, whole, smem, vm = part_specs(base, rows, quarter)
    return pl.pallas_call(
        functools.partial(resid_kernel, base),
        grid=(1,),
        out_shape=[jax.ShapeDtypeStruct(t.shape, F32), jax.ShapeDtypeStruct(t.shape, BF)],
        in_specs=[smem, pair, pair, whole, tile, vm],
        out_specs=[pair, pair],
        compiler_params=pltpu.CompilerParams(vmem_limit_bytes=10 * 1024 * 1024),
        name="resid",
    )(idx, t, u, x0, x1, gain)


def stat_row(tail, c, quarter):
    line, at = c * CH // quarter, c * CH % quarter
    return tail[0, line : line + 1, at : at + CH].astype(F32)


def dresid_kernel(base, width, idx, t, tt, u, ut, r, c0, c1, gain, scale, dr_out, da_out):
    rows, quarter = r.shape[1:]
    for c in range(rows // CH):
        rr = slice(c * CH, c * CH + CH)
        m = valid_rows(idx, base + c * CH, CH)
        dot = stat_row(tt, c, quarter) + stat_row(ut, c, quarter)
        s = scale[0:1, rr]
        fac = columns(s * s * dot * (1.0 / width))
        for n, cot in ((0, c0), (1, c1)):
            d = t[1 - n, rr, :].astype(F32) + u[n, rr, :].astype(F32)
            dr = cot[rr, :].astype(F32) + d * gain[idx[n]] - r[n, rr, :] * fac
            if n == 0:
                dr_out[rr, :] = dr
            da_out[n, rr, :] = (m * dr).astype(BF)


def dresid_step(base, width, idx, t, u, r, c0, c1, gain, scale):
    rows, quarter = r.shape[1:]
    pair, tile, whole, smem, vm = part_specs(base, rows, quarter)
    foot = pl.BlockSpec((1, TAIL, quarter), lambda i: (0, rows // TAIL, 0))
    line = vm
    return pl.pallas_call(
        functools.partial(dresid_kernel, base, width),
        grid=(1,),
        out_shape=[jax.ShapeDtypeStruct(r.shape[1:], F32), jax.ShapeDtypeStruct(r.shape, BF)],
        in_specs=[smem, pair, foot, pair, foot, pair, whole, whole, vm, line],
        out_specs=[tile, pair],
        compiler_params=pltpu.CompilerParams(vmem_limit_bytes=10 * 1024 * 1024),
        name="dresid",
    )(idx, t, t, u, u, r, c0, c1, gain, scale)


def dinput_kernel(width, idx, keep, kt, got, gt, back, bt, dr, x0, gain, scale, *refs):
    rows, quarter = dr.shape
    g = gain[idx[0]]
    for c in range(rows // CH):
        rr = slice(c * CH, c * CH + CH)
        dot = stat_row(kt, c, quarter) + stat_row(gt, c, quarter) + stat_row(bt, c, quarter)
        s = scale[0:1, rr]
        d = keep[0, rr, :].astype(F32) + got[0, rr, :].astype(F32) + back[0, rr, :].astype(F32)
        fac = columns(s * s * dot * (1.0 / width))
        dx = dr[rr, :] + columns(s) * (d * g) - x0[rr, :].astype(F32) * fac
        refs[-1][rr, :] = dx.astype(BF)


def dinput_step(base, width, idx, keep, got, back, dr, x0, gain, scale, fold=None):
    rows, quarter = dr.shape
    pair, tile, whole, smem, vm = part_specs(base, rows, quarter)
    one = pl.BlockSpec((1, rows, quarter), lambda i: (1, 0, 0))
    zero = pl.BlockSpec((1, rows, quarter), lambda i: (0, 0, 0))
    foot = pl.BlockSpec((1, TAIL, quarter), lambda i: (0, rows // TAIL, 0))
    line = vm
    back = back[None]
    args = (idx, keep, keep, got, got, back, back, dr, x0, gain, scale)
    specs = [smem, one, foot, one, foot, zero, foot, tile, whole, vm, line]
    alias = {}
    if fold is not None:
        alias = {len(args): 0}
        args += (fold,)
        specs.append(pl.BlockSpec(memory_space=pl.ANY))
    return pl.pallas_call(
        functools.partial(dinput_kernel, width),
        grid=(1,),
        out_shape=jax.ShapeDtypeStruct(x0.shape, BF),
        in_specs=specs,
        out_specs=whole,
        input_output_aliases=alias,
        compiler_params=pltpu.CompilerParams(vmem_limit_bytes=8 * 1024 * 1024),
        name="dinput",
    )(*args)


def share_order(first):
    b0, b1, b2 = first
    kept = [((k >> 1) & 1) << b1 | (k & 1) << b2 for k in range(4)]
    return kept, [k | 1 << b0 for k in kept]


def ffn_grad_kernel(parts, units, at, *refs):
    ins, outs, buf = refs[: 5 * parts], refs[5 * parts : 5 * parts + 4], refs[-1]
    half = units // 2
    whole, low, high = (0, units), (0, half), (half, units)
    for left, right, places in (
        (2, 0, ((0, 0, whole),)), (3, 1, ((0, units, low), (1, 0, high))), (4, 1, ((1, half, whole),))
    ):
        total = None
        for s in range(parts):
            part = mm(ins[5 * s + left][...], ins[5 * s + right][...], TN)
            total = part if total is None else total + part
        buf[...] = total
        for group, first, (lo, hi) in places:
            kept, sent = share_order(FIRST if group == 0 else THIRD)
            for n in range(4):
                for dst, pos in ((outs[2 * group], sent), (outs[2 * group + 1], kept)):
                    blk = pl.ds(pl.multiple_of((at[5] ^ pos[n]) * 128, 128), 128)
                    dst[n, first : first + hi - lo, :] = buf[lo:hi, blk].astype(BF)


FIRST, SECOND, THIRD = (0, 1, 2), (1, 0, 2), (1, 2, 0)


def ffn_grads(at, ffn):
    rows, width = ffn[0][0].shape
    units = ffn[0][2].shape[1]
    args = [a for f in ffn for a in (f[1], f[0], f[2], f[3], f[4])]
    smem = pl.BlockSpec(memory_space=pltpu.SMEM)
    vm = pl.BlockSpec(memory_space=pltpu.VMEM)
    shapes = [(4, units + units // 2, 128)] * 4
    return pl.pallas_call(
        functools.partial(ffn_grad_kernel, len(ffn), units),
        out_shape=[jax.ShapeDtypeStruct(s, BF) for s in shapes],
        in_specs=[smem] + [vm] * len(args),
        out_specs=[vm] * 4,
        scratch_shapes=[pltpu.VMEM((units, width), F32)],
        compiler_params=pltpu.CompilerParams(vmem_limit_bytes=22 * 1024 * 1024),
        cost_estimate=pl.CostEstimate(flops=9 * 10 ** 9, bytes_accessed=10 ** 7, transcendentals=0),
        name="ffn_grads",
    )(at, *args)


def row_grad_kernel(parts, plan, at, *refs):
    count = len(refs) - 2 * len(plan) - len(plan)
    ins = refs[:count]
    outs = refs[count : count + 2 * len(plan)]
    bufs = refs[count + 2 * len(plan) :]
    each = count // parts
    for group, (order, pieces) in enumerate(plan):
        buf = bufs[group]
        col = 0
        for left, right, lo, n in pieces:
            total = None
            for s in range(parts):
                part = mm(ins[each * s + left][...], ins[each * s + right][:, lo : lo + n], TN)
                total = part if total is None else total + part
            buf[:, col : col + n] = total
            col += n
        kept, sent = share_order(order)
        for n in range(4):
            for dst, pos in ((outs[2 * group], sent), (outs[2 * group + 1], kept)):
                blk = pl.ds(pl.multiple_of((at[5] ^ pos[n]) * 128, 128), 128)
                dst[n] = buf[blk, :].astype(BF)


def out_grad_kernel(parts, at, *refs):
    ins, outs, (obuf, gbuf) = refs[: 4 * parts], refs[4 * parts : 4 * parts + 2], refs[4 * parts + 2 :]
    vd = obuf.shape[1]
    for buf, left, right in ((obuf, 0, 1), (gbuf, 2, 3)):
        total = None
        for s in range(parts):
            part = mm(ins[4 * s + left][...], ins[4 * s + right][...], TN)
            total = part if total is None else total + part
        buf[...] = total
    kept, sent = share_order(FIRST)
    for n in range(4):
        for dst, pos in ((outs[0], sent), (outs[1], kept)):
            blk = pl.ds(pl.multiple_of((at[5] ^ pos[n]) * 128, 128), 128)
            dst[n, :, 0:vd] = obuf[blk, :].astype(BF)
            dst[n, :, vd:] = gbuf[blk, :].astype(BF)


def out_grads(at, parts, args):
    width, n = args[0].shape[1], args[1].shape[1]
    smem = pl.BlockSpec(memory_space=pltpu.SMEM)
    vm = pl.BlockSpec(memory_space=pltpu.VMEM)
    return pl.pallas_call(
        functools.partial(out_grad_kernel, parts),
        out_shape=[jax.ShapeDtypeStruct((4, 128, 2 * n), BF)] * 2,
        in_specs=[smem] + [vm] * len(args),
        out_specs=[vm] * 2,
        scratch_shapes=[pltpu.VMEM((width, n), F32), pltpu.VMEM((width, n), F32)],
        compiler_params=pltpu.CompilerParams(vmem_limit_bytes=56 * 1024 * 1024),
        cost_estimate=pl.CostEstimate(flops=8 * 10 ** 9, bytes_accessed=10 ** 7, transcendentals=0),
        name="out_grads",
    )(at, *args)


def row_grads(at, parts, plan, args):
    width = args[0].shape[1]
    smem = pl.BlockSpec(memory_space=pltpu.SMEM)
    vm = pl.BlockSpec(memory_space=pltpu.VMEM)
    wides = [sum(p[3] for p in pieces) for _, pieces in plan]
    return pl.pallas_call(
        functools.partial(row_grad_kernel, parts, plan),
        out_shape=[jax.ShapeDtypeStruct((4, 128, w), BF) for w in wides for _ in range(2)],
        in_specs=[smem] + [vm] * len(args),
        out_specs=[vm] * (2 * len(plan)),
        scratch_shapes=[pltpu.VMEM((width, w), F32) for w in wides],
        compiler_params=pltpu.CompilerParams(vmem_limit_bytes=22 * 1024 * 1024),
        cost_estimate=pl.CostEstimate(flops=6 * 10 ** 9, bytes_accessed=10 ** 7, transcendentals=0),
        name="row_grads",
    )(at, *args)


def swap(array, axis, size, bit):
    return lax.ppermute(array, axis, [(i, i ^ bit) for i in range(size)])


def beside(array):
    return swap(array, "tensor", 4, 1)


def across(array):
    return swap(array, "tensor", 4, 2)


def after(array, *others):
    return lax.optimization_barrier((array,) + others)[0]


def plus(left, right):
    return (left.astype(F32) + right.astype(F32)).astype(BF)


def total_tensor(array):
    array = array + beside(array)
    return array + across(array)


class Share:
    def __init__(self, send, keep, size, order):
        low = size.bit_length() - 1 - 3
        self.size, self.low = size, low
        self.bits = [1 << (low + b) for b in order]
        self.send, self.terms = send, [keep]

    def start(self, *deps):
        send = after(self.send, *deps) if deps else self.send
        self.terms.append(swap(send, "dp", self.size, self.bits[len(self.terms) - 1]))

    def middle(self, *deps):
        half = 2 if len(self.terms) == 2 else 1
        got = after(self.terms[-1], *deps) if deps else self.terms[-1]
        self.terms[-1] = got
        total = sum(t[half : 2 * half].astype(F32) for t in self.terms)
        self.send = total.astype(BF)

    def finish(self, axis, *deps):
        got = after(self.terms[-1], *deps) if deps else self.terms[-1]
        total = sum(t[0].astype(F32) for t in self.terms[:-1]) + got[0].astype(F32)
        me = lax.axis_index("dp")
        for bit in range(self.low - 1, -1, -1):
            half = total.shape[axis] // 2
            mine = (me >> bit) & 1
            send = lax.dynamic_slice_in_dim(total, (1 - mine) * half, half, axis).astype(BF)
            keep = lax.dynamic_slice_in_dim(total, mine * half, half, axis)
            total = keep + swap(send, "dp", self.size, 1 << bit).astype(F32)
        return total


NSEG = 2


def per_device(
    source_rows, cotangent, lengths, dealing, norm_gain, query_weight, key_weight, value_weight,
    query_conv, key_conv, value_conv, beta_weight, decay_weight, decay_log, decay_bias, gate_weight,
    head_gain, out_weight, ffn_gain, ffn_gate, ffn_up, ffn_down,
):
    dp = lax.axis_size("dp")
    me = lax.axis_index("tensor").astype(jnp.int32)
    block = lax.axis_index("dp").astype(jnp.int32) // (dp // 8)
    length, quarter = cotangent.shape[1:]
    width = norm_gain.shape[0]
    heads, dv = decay_log.shape[0], head_gain.shape[0]
    dk = query_weight.shape[1] // heads
    qd, vd = heads * dk, heads * dv
    cw = 2 * qd + vd
    units = ffn_gate.shape[1]
    rows = length // NSEG
    pieces = [slice(s * rows, s * rows + rows) for s in range(NSEG)]
    own = lax.dynamic_slice_in_dim

    cot = cotangent[0]
    cot1 = across(cot)
    cot2 = beside(cot)
    ordered = source_rows.at[dealing].get(mode="promise_in_bounds", unique_indices=True)
    arrived = lax.all_to_all(ordered, "dp", split_axis=0, concat_axis=1, tiled=True)[0]
    own_length = lengths[dealing[lax.axis_index("dp")]]
    idx = jnp.stack([me, me ^ 2, me ^ 1, me ^ 3, own_length, block, block, block])

    wba = jnp.pad(jnp.concatenate([beta_weight, decay_weight], 1), ((0, 0), (0, CH - 2 * heads)))
    conv = jnp.concatenate([query_conv, key_conv, value_conv], 1)
    dec = jnp.stack([-jnp.exp(decay_log), decay_bias])
    dec = jnp.pad(dec, ((0, 6), (heads, CH - 2 * heads)))
    gain1 = norm_gain.reshape(4, 1, quarter)
    gain2 = ffn_gain.reshape(4, 1, quarter)
    hgain = head_gain[None]
    mixw = (query_weight, key_weight, value_weight, gate_weight, wba, conv, dec)

    state = jnp.zeros((heads, dk, dv), F32)
    halo = jnp.zeros((8, cw), F32)
    xs = []
    for s, p in enumerate(pieces):
        first = (cot1, wba, conv, dec, idx, state, halo)
        x = after(arrived[p], *(first if s == 0 else (xs[s - 1][1],)))
        x1 = across(x)
        xs.append((arrived[p], x1, beside(x), beside(x1)))
    cot3 = beside(cot1)
    cots = (cot, cot1, cot2, cot3)

    halos, front, t, u = [], [], [], []
    for s in range(NSEG):
        if s > 0:
            state = after(state, t[s - 1])
        halos.append(halo)
        out = mixer_forward(idx, xs[s], gain1, *mixw, hgain, out_weight, state, halo)
        state, halo = out[10], out[11]
        front.append(out)
        send = after(out[8], xs[s + 1][1]) if s + 1 < NSEG else out[8]
        t.append(plus(out[9], beside(send)))
        u.append(across(t[s]))
    resid, low, ffn, t2, u2 = [], [], [], [], []
    for s in range(NSEG):
        last = front[NSEG - 1][10] if s < NSEG - 1 else ffn[s - 1][10]
        r, lo = resid_step(s * rows, idx, t[s], after(u[s], last), arrived, xs[s][1], gain2)
        resid.append(r)
        low.append(lo)
        core = beside(lo)
        if s < NSEG - 1:
            lo = after(lo, t[s + 1])
        else:
            lo = after(lo, t2[s - 1])
        fold = None if s == 0 else ffn[s - 1][7:9]
        f = ffn_both(s * rows, idx, lo, core, cots, gain2, ffn_gate.T, ffn_up.T, ffn_down.T, fold)
        ffn.append(f)
        got = beside(f[5] if s == 0 else after(f[5], u2[s - 1]))
        t2.append(plus(f[6], got))
        u2.append(across(t2[s]))
    hold = t2[NSEG - 1]
    grads = ffn_grads(after(idx, hold), ffn)
    shares = [Share(grads[0], grads[1], dp, FIRST), Share(grads[2], grads[3], dp, THIRD)]
    dr, da, pre = [], [], []
    for s in range(NSEG):
        wait = (hold,) if s == 0 else (grads[0], pre[s - 1][3])
        d, a = dresid_step(
            s * rows, width, idx, t2[s], after(u2[s], *wait), resid[s], cot, cot1, gain2, ffn[s][10]
        )
        dr.append(d)
        da.append((a, beside(a)))
        pre.append(out_backward(idx, heads, da[s], out_weight, hgain, front[s][15], front[s][4]))
        if s == 0:
            for sh in shares:
                sh.start()

    back = [None] * NSEG
    ds = jnp.zeros((heads, dk, dv), F32)
    dhalo = jnp.zeros((8, cw), F32)
    got1, away1, bk1 = [None] * NSEG, [None] * NSEG, [None] * NSEG
    fsend, fkeep = ffn[NSEG - 1][7:9]
    fgot = beside(after(fsend, da[NSEG - 1][1]))
    for s in reversed(range(NSEG)):
        o = front[s]
        order = idx
        if s < NSEG - 1:
            order = after(idx, away1[s + 1], outg[0], faway, *[sh.send for sh in shares])
        b = mixer_backward(
            order, quarter, pre[s][1], pre[s][2], o[0], o[1], o[2], o[3], o[5], o[6], o[13], o[14],
            *mixw, halos[s], ds, dhalo,
        )
        ds, dhalo = b[5], b[6]
        back[s] = b
        if s == NSEG - 1:
            got1[s] = beside(b[2])
            away1[s] = plus(b[3][0], got1[s][0])
        else:
            flown = (bk1[s + 1], fback, *[sh.terms[-1] for sh in shares + outs])
            got1[s] = beside(after(b[2], *flown))
            dx = dinput_step(
                (s + 1) * rows, width, idx, back[s + 1][3], got1[s + 1], after(bk1[s + 1], ds), dr[s + 1],
                arrived, gain1, front[s + 1][12],
            )
            away1[s] = plus(b[3][0], after(got1[s], dx)[0])
        bk1[s] = across(away1[s])
        if s == NSEG - 1:
            for sh in shares:
                sh.middle(ds)
                sh.start()
            outg = out_grads(
                after(idx, away1[s]), NSEG,
                [v for q in range(NSEG) for v in (pre[q][0], front[q][7], front[q][0], pre[q][2])],
            )
            outs = [Share(outg[0], outg[1], dp, FIRST)]
            for sh in outs:
                sh.start()
            faway = plus(fkeep[0], fgot[0])
            fback = across(after(faway, away1[s]))
    small = after(sum(b[4] for b in back), *flown)
    gsum = sum(f[9] for f in ffn)
    ghead = jnp.pad(sum(p[3][0:1] for p in pre), ((0, 0), (0, width - dv)))
    small = jnp.concatenate([small[0:4], ghead, small[5:8], gsum, small[8 : 8 + 2 * heads], jnp.zeros((7 - 2 * heads, width), F32)], 0)
    small = small + swap(small, "dp", dp, 1)

    lead = []
    for s in range(NSEG):
        o, b = front[s], back[s]
        lead += [o[0], b[0]]
    plan = ((FIRST, ((0, 1, 0, cw),)),)
    wide = row_grads(after(idx, away1[0]), NSEG, plan, lead)
    tail = Share(wide[0], wide[1], dp, FIRST)
    tail.start()
    second = swap(after(small, wide[0]), "dp", dp, 2)
    out_share = outs[0]
    out_share.middle(wide[0])
    out_share.start()
    shares[0].middle(wide[0])
    shares[0].start()
    keep = after(back[0][3], wide[0])
    dx = dinput_step(0, width, idx, keep, got1[0], bk1[0], dr[0], arrived, gain1, front[0][12], dx)
    returned = lax.all_to_all(
        dx.reshape(dp, length // dp, quarter), "dp", split_axis=0, concat_axis=0, tiled=True
    )
    mask = (jnp.arange(length) < own_length).astype(F32)[:, None]
    rest = fkeep[1].astype(F32) + after(fgot, dx)[1].astype(F32) + fback.astype(F32)
    mixed = (jnp.concatenate([r[0] for r in resid], 0) + mask * rest).astype(BF)
    out_share.middle(mixed)
    out_share.start()
    tail.middle(out_share.send)
    tail.start()
    small = small + after(second, tail.send)
    third = swap(small, "dp", dp, 4)
    shares[1].middle(tail.send)
    shares[1].start()
    lower = shares[0].finish(1, shares[1].send)
    tail.middle(lower)
    tail.start()
    small = small + after(third, tail.send)
    bit = 8
    while bit < dp:
        small = small + swap(small, "dp", dp, bit)
        bit *= 2
    upper = shares[1].finish(1, tail.send)
    summed = total_tensor(jnp.concatenate([small[4:5], small[7:9]], 0))
    source_grad = jnp.zeros_like(returned).at[dealing].set(
        after(returned, tail.send), mode="promise_in_bounds", unique_indices=True
    )
    outw = out_share.finish(0, tail.send)
    outw, gatew = outw[:, :vd], outw[:, vd:]
    wide = tail.finish(0, summed)
    shared = small[0:7]
    part = width // dp
    start = lax.axis_index("dp") * part
    norm_gain_grad = own(summed[1] / norm_gain, start, part)
    narrow = own(small[9 : 9 + 2 * heads], start, part, 1)
    ffn_gain_grad = own(summed[2] / ffn_gain, start, part)
    return (
        mixed[None],
        source_grad,
        norm_gain_grad,
        wide[:, 0:qd],
        wide[:, qd : 2 * qd],
        wide[:, 2 * qd : cw],
        shared[0:4, 0:qd],
        shared[0:4, qd : 2 * qd],
        shared[0:4, 2 * qd : cw],
        narrow[:heads].T,
        narrow[heads:].T,
        shared[5, heads : 2 * heads],
        shared[6, heads : 2 * heads],
        gatew,
        summed[0, 0:dv],
        outw,
        ffn_gain_grad,
        jnp.concatenate([lower[units:], upper[: units // 2]], 0).T,
        upper[units // 2 :].T,
        lower[:units].T,
    )


def solution(mesh):
    in_specs = (
        P(None, "dp", "tensor"),
        P("dp", None, "tensor"),
        P(),
        P(),
        P(),
        P(None, "tensor"),
        P(None, "tensor"),
        P(None, "tensor"),
        P(None, "tensor"),
        P(None, "tensor"),
        P(None, "tensor"),
        P(None, "tensor"),
        P(None, "tensor"),
        P("tensor"),
        P("tensor"),
        P(None, "tensor"),
        P(),
        P(None, "tensor"),
        P(),
        P(None, "tensor"),
        P(None, "tensor"),
        P(None, "tensor"),
    )
    out_specs = (
        P("dp", None, "tensor"),
        P(None, "dp", "tensor"),
        P("dp"),
        P("dp", "tensor"),
        P("dp", "tensor"),
        P("dp", "tensor"),
        P(None, "tensor"),
        P(None, "tensor"),
        P(None, "tensor"),
        P("dp", "tensor"),
        P("dp", "tensor"),
        P("tensor"),
        P("tensor"),
        P("dp", "tensor"),
        P(),
        P("dp", "tensor"),
        P("dp"),
        P("dp", "tensor"),
        P("dp", "tensor"),
        P("dp", "tensor"),
    )
    return jax.shard_map(
        per_device, mesh=mesh, in_specs=in_specs, out_specs=out_specs, check_vma=False
    )
```
